32 devices in a mesh: section: 4 (over y, x), batch: 8 (over z, core).
Axes of the slice: x: 2, y: 2, z: 4, core: 2. Of those that a mesh axis runs over, the one named last changes fastest.
Arguments:
- embedded_tiles: bfloat16 [4, 48, 512, 256], P('section', 'batch'), may hold values from -6 to 6
- hidden_sample: bfloat16 [4, 48, 512, 32], P('section', 'batch'), may hold values from -6 to 6
- cotangent: bfloat16 [4, 48, 512, 256], P('section', 'batch'), may hold values from -6 to 6
- lengths: int32 [48], P('batch'), may hold values from 2 to 4, as said below
- gain_attn: bfloat16 [2, 256], replicated, may hold values from 0.5 to 1.5
- shift_attn: bfloat16 [2, 256], replicated, may hold values from -1.5 to 1.5
- w_qkv: bfloat16 [2, 256, 768], replicated, may hold values from -0.375 to 0.375
- rel_table: bfloat16 [2, 225, 8], replicated, may hold values from -5 to 5
- w_out: bfloat16 [2, 256, 256], replicated, may hold values from -1.5 to 1.5
- gain_mlp: bfloat16 [2, 256], replicated, may hold values from 0.5 to 1.5
- shift_mlp: bfloat16 [2, 256], replicated, may hold values from -1.5 to 1.5
- w_up: bfloat16 [2, 256, 1024], replicated, may hold values from -0.375 to 0.375
- w_down: bfloat16 [2, 1024, 256], replicated, may hold values from -0.1875 to 0.1875
- w_latent: bfloat16 [32, 256], replicated, may hold values from -1 to 1
Outputs:
- masked_outlook: bfloat16 [4, 48, 512, 256], P('section', 'batch')
- frames_grad: bfloat16 [4, 48, 512, 256], P('section', 'batch')
- latent_grad: bfloat16 [4, 48, 512, 32], P('section', 'batch')
- gain_attn_grad: float32 [2, 256], replicated
- shift_attn_grad: float32 [2, 256], replicated
- w_qkv_grad: float32 [2, 256, 768], replicated
- rel_table_grad: float32 [2, 225, 8], replicated
- w_out_grad: float32 [2, 256, 256], replicated
- gain_mlp_grad: float32 [2, 256], replicated
- shift_mlp_grad: float32 [2, 256], replicated
- w_up_grad: float32 [2, 256, 1024], replicated
- w_down_grad: float32 [2, 1024, 256], replicated
- w_latent_grad: float32 [32, 256], replicated
The draws below stay inside these ranges and needn't reach their ends.
Inputs may be any that keep to these rules, and one draw needn't show every extreme that they name: `lengths`: among the 6 items of each index of batch at least one has all 4 steps.
All inputs are finite; a program needn't handle non-finite values.
Results may differ from the reference program's by a relative error of at most 0.02.
Values may be sent and summed in bfloat16 or wider, within the bound.
A program may use at most 128 MiB of HBM per device.

```python
import jax
import jax.numpy as jnp
import numpy as np
from jax import lax

WIDTH = 256
HEADS = 8
WIN = 8
MLP = 1024
LAT = 32
GH = 16
GW = 32
MICRO = 6
ITEMS = 1
SPAN = 225
PATCHES = 512
BATCH = 48
N_SECTION = 4


def draw_lengths(key, part):
    key = jax.random.fold_in(key, 11)
    first_key, second_key = jax.random.split(key)
    drawn = jax.random.randint(first_key, (BATCH,), 2, N_SECTION + 1)
    group_size = MICRO * ITEMS
    chosen = jax.random.randint(second_key, (BATCH // group_size, 1), 0, group_size)
    full_rows = (jnp.arange(group_size)[None, :] == chosen).reshape(BATCH)
    return jnp.where(full_rows, N_SECTION, drawn).astype(jnp.int32)


def level_of(rng, shape, cuts, low, top_value):
    level = 1.0
    for position, parts in cuts:
        steps = jax.random.uniform(jax.random.fold_in(jax.random.fold_in(rng, 6), position), (parts,), jnp.float32, low / len(cuts), top_value / len(cuts))
        level = level * jnp.repeat(jnp.exp(steps), shape[position] // parts).reshape((-1,) + (1,) * (len(shape) - 1 - position))
    return level


def gaussian(stream_key, dims, deviation, most, shards=(), kind=jnp.bfloat16):
    level = level_of(stream_key, dims, shards, -0.22, 0.18) if shards else 1.0
    entries = jax.random.normal(stream_key, dims, jnp.float32) * deviation * level
    return jnp.minimum(jnp.maximum(entries, -most), most).astype(kind)


def setup_inputs(seed: int = 0) -> dict:
    key_of = jax.random.split(jax.random.key(seed), 15)
    embedded_tiles = gaussian(key_of[0], (N_SECTION, BATCH, PATCHES, WIDTH), 1.0, 6.0, ((0, 4), (1, 8)))
    hidden_sample = gaussian(key_of[1], (N_SECTION, BATCH, PATCHES, LAT), 1.0, 6.0, ((0, 4), (1, 8)))
    cotangent = gaussian(key_of[2], (N_SECTION, BATCH, PATCHES, WIDTH), 1.0, 6.0, ((0, 4), (1, 8)))
    lengths = draw_lengths(jax.random.fold_in(key_of[14], 71), 0)
    gain_attn = jnp.clip(1.0 + 0.1 * jax.random.normal(key_of[4], (2, WIDTH), jnp.float32), 0.5, 1.5).astype(jnp.bfloat16)
    shift_attn = gaussian(key_of[5], (2, WIDTH), 0.3, 1.5)
    w_qkv = gaussian(key_of[6], (2, WIDTH, 3 * WIDTH), WIDTH ** -0.5, 0.375)
    rel_table = gaussian(key_of[7], (2, SPAN, HEADS), 1.0, 5.0)
    w_out = gaussian(key_of[8], (2, WIDTH, WIDTH), (WIDTH // 16) ** -0.5, 1.5)
    gain_mlp = jnp.clip(1.0 + 0.1 * jax.random.normal(key_of[9], (2, WIDTH), jnp.float32), 0.5, 1.5).astype(jnp.bfloat16)
    shift_mlp = gaussian(key_of[10], (2, WIDTH), 0.3, 1.5)
    w_up = gaussian(key_of[11], (2, WIDTH, MLP), WIDTH ** -0.5, 0.375)
    w_down = gaussian(key_of[12], (2, MLP, WIDTH), MLP ** -0.5, 0.1875)
    w_latent = gaussian(key_of[13], (LAT, WIDTH), LAT ** -0.5, 1.0)
    return dict(embedded_tiles=embedded_tiles, hidden_sample=hidden_sample, cotangent=cotangent, lengths=lengths, gain_attn=gain_attn, shift_attn=shift_attn, w_qkv=w_qkv, rel_table=rel_table, w_out=w_out, gain_mlp=gain_mlp, shift_mlp=shift_mlp, w_up=w_up, w_down=w_down, w_latent=w_latent)


@jax.custom_vjp
def low(v):
    return lax.optimization_barrier(v.astype(jnp.bfloat16)).astype(jnp.float32)

@jax.custom_vjp
def low_back(v):
    return v

def low_keep(v):
    return (low(v), None)

def low_pass(kept, grad):
    return (grad,)

def back_keep(v):
    return (v, None)

def back_low(kept, grad):
    return (low(grad),)
low.defvjp(low_keep, low_pass)
low_back.defvjp(back_keep, back_low)

def product(left_op, right_op):
    return jnp.dot(left_op, right_op, preferred_element_type=jnp.float32, precision=lax.Precision.HIGHEST)

def offset_index(window):
    row_ids = np.repeat(np.arange(window), window)
    col_ids = np.tile(np.arange(window), window)
    return (row_ids[:, None] - row_ids[None, :] + window - 1) * (2 * window - 1) + col_ids[:, None] - col_ids[None, :] + window - 1

def region_of(length, window):
    labels = np.zeros(length, np.int32)
    labels[length - window:length - window // 2] = 1
    labels[length - window // 2:] = 2
    return labels

def shift_penalty(height, across, window):
    labels = region_of(height, window)[:, None] * 3 + region_of(across, window)[None, :]
    tile_ids = labels.reshape(height // window, window, across // window, window).transpose(0, 2, 1, 3).reshape(-1, window * window)
    return np.where(tile_ids[:, :, None] == tile_ids[:, None, :], 0.0, -100.0).astype(np.float32)

def to_tiles(token_rows):
    channels = token_rows.shape[-1]
    shaped = token_rows.reshape(GH // WIN, WIN, GW // WIN, WIN, channels)
    return shaped.transpose(0, 2, 1, 3, 4).reshape(-1, WIN * WIN, channels)

def from_tiles(tiled_rows):
    channels = tiled_rows.shape[-1]
    shaped = tiled_rows.reshape(GH // WIN, GW // WIN, WIN, WIN, channels)
    return shaped.transpose(0, 2, 1, 3, 4).reshape(GH * GW, channels)

def roll_cells(token_rows, amount):
    shaped = token_rows.reshape(GH, GW, token_rows.shape[-1])
    return jnp.roll(shaped, (amount, amount), (0, 1)).reshape(GH * GW, token_rows.shape[-1])

def layer_norm(inputs, gain_vec, offset_vec):
    centered = inputs - lax.optimization_barrier(jnp.mean(inputs, axis=-1, keepdims=True))
    spread = lax.optimization_barrier(jnp.mean(centered * centered, axis=-1, keepdims=True))
    return centered * lax.rsqrt(spread + 1e-05) * gain_vec + offset_vec

def position_bias(bias_table):
    return jnp.transpose(bias_table[offset_index(WIN)], (2, 0, 1))

def window_mix(normed, w_qkv, bias_table, w_out, penalty):
    projected = low(low_back(product(normed, w_qkv)))
    tiled_rows = to_tiles(projected)
    tile_count = tiled_rows.shape[0]
    head_view = tiled_rows.reshape(tile_count, WIN * WIN, 3, HEADS, -1)
    query_heads = head_view[:, :, 0]
    key_heads = head_view[:, :, 1]
    value_heads = head_view[:, :, 2]
    head_depth = query_heads.shape[-1]
    raw_scores = low_back(jnp.einsum('wihd,wjhd->whij', query_heads, key_heads, precision=lax.Precision.HIGHEST))
    scores = raw_scores * head_depth ** (-0.5) + position_bias(bias_table)[None] + penalty[:, None]
    row_peak = lax.optimization_barrier(jnp.max(scores, axis=-1, keepdims=True))
    exponent = jnp.exp(scores - row_peak)
    attention = low(exponent / lax.optimization_barrier(jnp.sum(exponent, axis=-1, keepdims=True)))
    blended = jnp.einsum('whij,wjhd->wihd', attention, value_heads, precision=lax.Precision.HIGHEST)
    blended = low(low_back(from_tiles(blended.reshape(tile_count, WIN * WIN, -1))))
    return low_back(product(blended, w_out))

def swin_block(stream, layer_no, learnable_tensors, shifted):
    gain_attn, shift_attn, w_qkv, rel_table, w_out, gain_mlp, shift_mlp, w_up, w_down, w_latent = learnable_tensors
    tile_count = GH // WIN * (GW // WIN)
    if shifted:
        penalty = jnp.asarray(shift_penalty(GH, GW, WIN))
    else:
        penalty = jnp.zeros((tile_count, WIN * WIN, WIN * WIN), jnp.float32)
    normed = low(layer_norm(stream, gain_attn[layer_no], shift_attn[layer_no]))
    if shifted:
        normed = roll_cells(normed, -(WIN // 2))
    branch = window_mix(normed, w_qkv[layer_no], rel_table[layer_no], w_out[layer_no], penalty)
    if shifted:
        branch = roll_cells(branch, WIN // 2)
    halfway = stream + branch
    second = low(layer_norm(halfway, gain_mlp[layer_no], shift_mlp[layer_no]))
    pre_act = low_back(product(second, w_up[layer_no]))
    activated = low(jax.nn.gelu(pre_act, approximate=False))
    return halfway + low_back(product(activated, w_down[layer_no]))

def section_step(frame_rows, noise_rows, carried, learnable_tensors):
    lifted = low_back(product(noise_rows, learnable_tensors[9]))
    stream = frame_rows + carried + lifted
    stream = swin_block(stream, 0, learnable_tensors, False)
    return swin_block(stream, 1, learnable_tensors, True)

def reference(embedded_tiles, hidden_sample, cotangent, lengths, gain_attn, shift_attn, w_qkv, rel_table, w_out, gain_mlp, shift_mlp, w_up, w_down, w_latent):
    learnable_tensors = tuple((weight.astype(jnp.float32) for weight in (gain_attn, shift_attn, w_qkv, rel_table, w_out, gain_mlp, shift_mlp, w_up, w_down, w_latent)))
    active = (jnp.arange(N_SECTION, dtype=jnp.int32)[:, None] < lengths[None, :]).astype(jnp.float32)

    def expanded_outlook(embedded_inputs_full, sampled_latents_full, coefficient_tensors):

        def one_item(item_pair):
            frame_item, noise_item = item_pair
            carried = jnp.zeros((PATCHES, WIDTH), jnp.float32)
            results = []
            for section_no in range(N_SECTION):
                output = section_step(frame_item[section_no], noise_item[section_no], carried, coefficient_tensors)
                results.append(output)
                carried = low(low_back(output))
            return jnp.stack(results)
        stacked = lax.map(jax.checkpoint(one_item), (jnp.swapaxes(embedded_inputs_full, 0, 1), jnp.swapaxes(sampled_latents_full, 0, 1)))
        return jnp.swapaxes(stacked, 0, 1) * active[:, :, None, None]
    masked_outlook, adjoint_rule = jax.vjp(expanded_outlook, embedded_tiles.astype(jnp.float32), hidden_sample.astype(jnp.float32), learnable_tensors)
    embedded_inputs_sensitivity, sampled_latents_sensitivity, learnable_sensitivities = adjoint_rule(cotangent.astype(jnp.float32))
    return (masked_outlook.astype(jnp.bfloat16), embedded_inputs_sensitivity.astype(jnp.bfloat16), sampled_latents_sensitivity.astype(jnp.bfloat16), learnable_sensitivities[0], learnable_sensitivities[1], learnable_sensitivities[2], learnable_sensitivities[3], learnable_sensitivities[4], learnable_sensitivities[5], learnable_sensitivities[6], learnable_sensitivities[7], learnable_sensitivities[8], learnable_sensitivities[9])
```

```python
import jax, jax.numpy as jnp, numpy as np
from jax import lax
from jax.experimental import pallas as pl
from jax.experimental.pallas import tpu as pltpu
from jax.sharding import PartitionSpec as P
BF=jnp.bfloat16; F32=jnp.float32
LOG2E=1.4426950408889634
SCALE=32**-0.5
def dot(a,b): return lax.dot_general(a,b,(((1,),(0,)),((),())),preferred_element_type=F32)
def dot_nt(a,b): return lax.dot_general(a,b,(((1,),(1,)),((),())),preferred_element_type=F32)
def dot_tn(a,b): return lax.dot_general(a,b,(((0,),(0,)),((),())),preferred_element_type=F32)

GC=[0.7978695563668204, 0.0363928095591428, -8.82196615782389e-05, -3.6600001215273455e-05, 1.418529678284452e-06]
def gelu_pair(z):
    w=z*z
    wc=jnp.minimum(w,22.0)
    p=GC[4]
    for c in GC[3::-1]: p=p*wc+c
    t=jnp.tanh(z*p)
    ph=0.5+0.5*t
    e=jnp.exp2(w*(-0.5*LOG2E))
    a=z*ph
    gp=ph+z*(e*0.3989422804014327)
    return a,gp

def norm(x):
    mu=jnp.mean(x,axis=-1,keepdims=True)
    xc=x-mu
    var=jnp.mean(xc*xc,axis=-1,keepdims=True)
    r=lax.rsqrt(var+1e-5)
    return xc*r, r

def norm_back(dn,n,r):
    m1=jnp.mean(dn,axis=-1,keepdims=True)
    m2=jnp.mean(dn*n,axis=-1,keepdims=True)
    return r*(dn-m1-n*m2)

def head_masks():
    lane=lax.broadcasted_iota(jnp.int32,(1,128),1)
    return [jnp.where(lane//32==h,1.0,0.0).astype(BF) for h in range(4)]
def half_masks():
    lane=lax.broadcasted_iota(jnp.int32,(1,128),1)
    return [jnp.where(lane//64==h,1.0,0.0).astype(BF) for h in range(2)]

def unpair(o):
    lane=lax.broadcasted_iota(jnp.int32,(32,128),1)
    lo=lane<64
    ev=jnp.where(lo,o[0:32],pltpu.roll(o[64:96],64,1))
    od=jnp.where(lo,pltpu.roll(o[32:64],64,1),o[96:128])
    return ev,od

def f_chunk(x,wq,wo,wu,wd,gn,bias,act,rst):
    hm=head_masks(); sm=half_masks()
    n1,r1=norm(x)
    rst[0]=jnp.broadcast_to(r1,(256,128))
    act[0]=n1.astype(BF)
    normed=(n1*gn[0:1]+gn[1:2]).astype(BF)
    act[1]=normed
    qkv=dot(normed,wq[...]).astype(BF)
    q=qkv[:,0:256]; k=qkv[:,256:512]; v=qkv[:,512:768]
    act[2]=q; act[3]=k; act[4]=v
    vt=v.T
    for wp in range(2):
        for g in range(2):
            ps=[]
            for w in (2*wp,2*wp+1):
                kk=k[w*64:(w+1)*64,g*128:(g+1)*128]
                qq=q[w*64:(w+1)*64,g*128:(g+1)*128]
                qb=jnp.concatenate([qq*hm[h] for h in range(4)],axis=0)
                st=dot_nt(kk,qb)
                s=st*(SCALE*LOG2E)+bias(w,g)
                m=jnp.max(s,axis=0,keepdims=True)
                e=jnp.exp2(s-m)
                r=1.0/jnp.sum(e,axis=0,keepdims=True)
                p=(e*r).astype(BF)
                act[5+g,w*64:(w+1)*64,:]=p
                ps.append(p)
            pp=jnp.concatenate(ps,axis=0)
            for hp in range(2):
                b0=g*128+hp*64
                vv=vt[b0:b0+64,wp*128:(wp+1)*128]
                lhs=jnp.concatenate([vv*sm[0],vv*sm[1]],axis=0)
                o=dot(lhs,pp[:,hp*128:(hp+1)*128])
                ev,od=unpair(o)
                act[7,b0:b0+32,wp*128:(wp+1)*128]=ev.astype(BF)
                act[7,b0+32:b0+64,wp*128:(wp+1)*128]=od.astype(BF)
    branch=dot_tn(act[7],wo[...])
    h=x+branch
    n2,r2=norm(h)
    rst[1]=jnp.broadcast_to(r2,(256,128))
    act[8]=n2.astype(BF)
    second=(n2*gn[2:3]+gn[3:4]).astype(BF)
    act[9]=second
    y=h
    for j in range(4):
        pre=dot(second,wu[:,j*256:(j+1)*256])
        a,gp=gelu_pair(pre)
        a=a.astype(BF)
        act[10+j]=a
        act[14+j]=gp.astype(BF)
        y=y+dot(a,wd[j*256:(j+1)*256,:])
    return y

def colsum(a):
    return jnp.sum(a.reshape(32,8,256),axis=0)

def b_chunk(dout,wq,wo,wu,wd,gn,act,rst,gv,gb,lt,rt,pos):
    hm=head_masks(); sm=half_masks()
    db=dout.astype(BF)
    lt[2,pos]=db.T
    lt[3,pos]=act[9].T
    ds=jnp.zeros((256,256),F32)
    for j in range(4):
        c=slice(j*256,(j+1)*256)
        da=dot_nt(db,wd[c,:])
        dpre=(da*act[14+j].astype(F32)).astype(BF)
        rt[4+j,pos]=dpre
        ds=ds+dot_nt(dpre,wu[:,c])
    n2=act[8].astype(F32)
    gv[2]+=colsum(ds*n2)
    gv[3]+=colsum(ds)
    r2=rst[1][:,0:1]
    dh=dout+norm_back(ds*gn[2:3],n2,r2)
    db2=dh.astype(BF)
    rt[3,pos]=db2
    lt[1,pos]=act[7]
    dA=dot_nt(db2,wo[...]).astype(BF)
    q=act[2]; k=act[3]; v=act[4]
    kt=k.T
    dqt=[[None]*2 for _ in range(8)]
    acc=[[],[]]
    for wp in range(2):
        for g in range(2):
            dss=[]
            cs=slice(g*128,(g+1)*128)
            for w in (2*wp,2*wp+1):
                rs=slice(w*64,(w+1)*64)
                ab=jnp.concatenate([dA[rs,cs]*hm[h] for h in range(4)],axis=0)
                qb=jnp.concatenate([q[rs,cs]*hm[h] for h in range(4)],axis=0)
                dp=dot_nt(v[rs,cs],ab)
                p=act[5+g,rs,:]
                pf=p.astype(F32)
                t=dp*pf
                delta=jnp.sum(t,axis=0,keepdims=True)
                dsc=t-pf*delta
                acc[g].append(dsc)
                dsr=(dsc*SCALE).astype(BF)
                dss.append(dsr)
                rt[2,pos,rs,cs]=dot(p,ab).astype(BF)
                rt[1,pos,rs,cs]=dot(dsr,qb).astype(BF)
            dd=jnp.concatenate(dss,axis=0)
            for hp in range(2):
                b0=g*128+hp*64
                kk=kt[b0:b0+64,wp*128:(wp+1)*128]
                lhs=jnp.concatenate([kk*sm[0],kk*sm[1]],axis=0)
                o=dot(lhs,dd[:,hp*128:(hp+1)*128])
                ev,od=unpair(o)
                i=b0//32
                dqt[i][wp]=ev.astype(BF); dqt[i+1][wp]=od.astype(BF)
    for g in range(2): gb[:,g*256:(g+1)*256]+=(acc[g][0]+acc[g][1])+(acc[g][2]+acc[g][3])
    dqT=jnp.concatenate([jnp.concatenate(r,axis=1) for r in dqt],axis=0)
    dq=dqT.T
    rt[0,pos]=dq
    dn=dot_nt(dq,wq[:,0:256])+dot_nt(rt[1,pos],wq[:,256:512])+dot_nt(rt[2,pos],wq[:,512:768])
    lt[0,pos]=act[1].T
    n1=act[0].astype(F32)
    gv[0]+=colsum(dn*n1)
    gv[1]+=colsum(dn)
    r1=rst[0][:,0:1]
    return dh+norm_back(dn*gn[0:1],n1,r1)

def weight_grads(G,lt,rt,act):
    def one(t,c):
        kind=jnp.where(t<3,0,jnp.where(t<4,1,3))
        G[t]+=dot(lt[kind,0],rt[t,0])+dot(lt[kind,1],rt[t,1])+dot(lt[kind,2],rt[t,2])
        return c
    lax.fori_loop(0,8,one,0)
    def two(j,c):
        G[8+j]+=dot(lt[2,0],act[0,10+j])+dot(lt[2,1],act[1,10+j])+dot(lt[2,2],act[2,10+j])
        return c
    lax.fori_loop(0,4,two,0)


MESH = pl.DeviceIdType.MESH
SECTIONS = 4


def local_copy(src, dst, sem):
    return pltpu.make_async_copy(src, dst, sem)


def to_windows(rows):
    return rows.reshape(8, 4, 8, rows.shape[-1]).transpose(1, 0, 2, 3)


def to_rows(tiles):
    return tiles.transpose(1, 0, 2, 3).reshape(256, tiles.shape[-1])


def turn(tiles):
    flat = tiles.reshape(32, 8, 256)
    return jnp.concatenate([flat[:, 4:8], flat[:, 0:4]], axis=1).reshape(4, 8, 8, 256)


def shift_out(tiles):
    turned = turn(tiles)
    nxt = jnp.concatenate([turned[1:], turned[:1]], axis=0)
    low_half = lax.broadcasted_iota(jnp.int32, (1, 1, 8, 256), 2) < 4
    return jnp.where(low_half, turned, nxt)


def shift_back(tiles):
    turned = turn(tiles)
    prev = jnp.concatenate([turned[3:], turned[:3]], axis=0)
    low_half = lax.broadcasted_iota(jnp.int32, (1, 1, 8, 256), 2) < 4
    return jnp.where(low_half, prev, turned)


def toward_shifted(buf, par, pos):
    own = buf[par, pos, :, 32:64, :].reshape(4, 4, 8, 256)
    other = buf[par, 3 - pos, :, 0:32, :].reshape(4, 4, 8, 256)
    return shift_out(jnp.concatenate([own, other], axis=1)).reshape(256, 256)


def toward_plain(buf, par, pos):
    other = buf[par, 3 - pos, :, 32:64, :].reshape(4, 4, 8, 256)
    own = buf[par, pos, :, 0:32, :].reshape(4, 4, 8, 256)
    return shift_back(jnp.concatenate([other, own], axis=1)).reshape(256, 256)


def rollout_kernel(
    emb, hid, cot, wq, wo, wu, wd, wl, gn, bt,
    y_home, fg_home, lg_home, gw, gb, gv, gl, act_far,
    emb_in, cot_in, hid_in, y_st, fg_st, lg_st, xs, dxs, xin, act, rst, lt, rt,
    emb_ss, emb_rs, hid_ss, hid_rs, cot_ss, cot_rs,
    y_ss, y_rs, fg_ss, fg_rs, lg_ss, lg_rs, xf_ss, xf_rs, xb_ss, xb_rs, act_os, act_is,
):
    sec = lax.axis_index("section")
    bat = lax.axis_index("batch")
    core = lax.rem(bat, 2)
    first = bat - core
    partner = first + 1 - core

    barrier = pltpu.get_barrier_semaphore()
    xs[1] = jnp.zeros((4, 4, 64, 256), F32)
    dxs[1] = jnp.zeros((4, 4, 64, 256), F32)
    for ds in range(SECTIONS):
        for dc in range(2):
            if ds == 0 and dc == 0:
                continue
            pl.semaphore_signal(
                barrier, inc=1,
                device_id={"section": lax.rem(sec + ds, SECTIONS), "batch": first + lax.rem(core + dc, 2)},
                device_id_type=MESH)
    pl.semaphore_wait(barrier, 2 * SECTIONS - 1)

    def spread(src, dst, ssem, rsem, begin):
        for pos in range(3):
            for t in range(4):
                if pos == 0:
                    to_sec = 2 * core + t // 2
                    to_bat = first + t % 2
                    piece = src.at[4 + t // 2, t % 2]
                    mine = (to_sec == sec) & (core == t % 2)
                else:
                    to_sec = jnp.int32(t)
                    to_bat = bat
                    piece = src.at[t, pos - 1]
                    mine = to_sec == sec

                @pl.when(mine)
                def _():
                    if begin:
                        local_copy(piece, dst.at[sec, pos], rsem.at[sec, pos]).start()

                @pl.when(jnp.logical_not(mine))
                def _():
                    rc = pltpu.make_async_remote_copy(
                        src_ref=piece, dst_ref=dst.at[sec, pos],
                        send_sem=ssem.at[pos, t], recv_sem=rsem.at[sec, pos],
                        device_id={"section": to_sec, "batch": to_bat}, device_id_type=MESH)
                    if begin:
                        rc.start()
                    else:
                        rc.wait_send()

    def arrived(src, dst, rsem, step, pos):
        local_copy(src.at[0, 0], dst.at[step, pos], rsem.at[step, pos]).wait()

    def home_copy(src, dst, ssem, rsem, step, pos, begin):
        half = pos == 0
        item = jnp.where(half, 4 + lax.rem(sec, 2), sec)
        part = jnp.where(half, core, pos - 1)
        to_bat = jnp.where(half, first + sec // 2, bat)
        slot = jnp.where(half, lax.rem(sec, 2) * 2 + core, sec)
        mine = (step == sec) & (to_bat == bat)

        @pl.when(mine)
        def _():
            if begin:
                local_copy(src.at[step, pos], dst.at[item, part], rsem.at[pos, slot]).start()

        @pl.when(jnp.logical_not(mine))
        def _():
            rc = pltpu.make_async_remote_copy(
                src_ref=src.at[step, pos], dst_ref=dst.at[item, part],
                send_sem=ssem.at[step, pos], recv_sem=rsem.at[pos, slot],
                device_id={"section": step, "batch": to_bat}, device_id_type=MESH)
            if begin:
                rc.start()
            else:
                rc.wait_send()

    def home_arrivals(src, dst, rsem):
        for pos in range(3):
            for t in range(4):
                piece = dst.at[4 + t // 2, t % 2] if pos == 0 else dst.at[t, pos - 1]
                local_copy(src.at[0, 0], piece, rsem.at[pos, t]).wait()

    def exchange(buf, par, off, ssem, rsem, n):
        return pltpu.make_async_remote_copy(
            src_ref=buf.at[par, 0, :, pl.ds(off, 32), :],
            dst_ref=buf.at[par, 3, :, pl.ds(off, 32), :],
            send_sem=ssem.at[n], recv_sem=rsem.at[n],
            device_id={"section": sec, "batch": partner}, device_id_type=MESH)

    @pl.when(sec == 0)
    def _():
        spread(emb, emb_in, emb_ss, emb_rs, True)
        spread(hid, hid_in, hid_ss, hid_rs, True)

    for ref in (gw, gb, gl):
        ref[...] = jnp.zeros(ref.shape, F32)
    gv[...] = jnp.zeros(gv.shape, F32)

    def act_out(ph, pos):
        return local_copy(act.at[lax.rem(ph, 3), pos], act_far.at[ph, pos], act_os.at[ph, pos])

    def act_in(ph, pos):
        return local_copy(act_far.at[ph, pos], act.at[lax.rem(ph, 3), pos], act_is.at[ph, pos])

    def forward_phase(ph, c):
        step = ph // 2
        blk = lax.rem(ph, 2)
        par = lax.rem(ph, 2)
        old = 1 - par

        def chunk(pos, c):
            @pl.when((ph >= 1) & (pos == 0))
            def _():
                prev = exchange(xs, old, pl.multiple_of(32 * old, 32), xf_ss, xf_rs, ph - 1)
                prev.wait_recv()

            @pl.when(blk == 0)
            def _():
                arrived(emb, emb_in, emb_rs, step, pos)
                arrived(hid, hid_in, hid_rs, step, pos)
                lifted = emb_in[step, pos].astype(F32) + dot(hid_in[step, pos], wl[...])
                carried = toward_plain(xs, old, pos).astype(BF).astype(F32)
                xin[...] = to_windows(lifted).reshape(256, 256) + carried

            @pl.when(blk == 1)
            def _():
                xin[...] = toward_shifted(xs, old, pos)

            @pl.when((ph >= 3) & (ph <= 7))
            def _():
                @pl.when(ph - 3 < 5)
                def _():
                    act_out(ph - 3, pos).wait()

            slot = act.at[lax.rem(ph, 3), pos]
            bottom = jnp.where(pos == 0, core, pos - 1)

            def bias(w, g):
                which = jnp.where(blk == 0, 0, 1 + 2 * bottom + (1 if w == 3 else 0))
                return bt[which, :, g * 256:(g + 1) * 256]

            y = f_chunk(xin[...], wq.at[blk], wo.at[blk], wu.at[blk], wd.at[blk], gn.at[blk], bias,
                        slot, rst.at[ph, pos])

            @pl.when((ph >= 2) & (pos == 0))
            def _():
                exchange(xs, par, pl.multiple_of(32 * par, 32), xf_ss, xf_rs, ph - 2).wait_send()

            xs[par, pos] = y.reshape(4, 64, 256)

            @pl.when((ph < 7) & (pos == 0))
            def _():
                exchange(xs, par, pl.multiple_of(32 * par, 32), xf_ss, xf_rs, ph).start()

            @pl.when(ph < 5)
            def _():
                act_out(ph, pos).start()

            @pl.when(blk == 1)
            def _():
                tiles = shift_back(xs[par, pos].reshape(4, 8, 8, 256))
                y_st[step, pos] = to_rows(tiles).astype(BF)
                home_copy(y_st, y_home, y_ss, y_rs, step, pos, True)

            @pl.when((pos == 0) & (sec >= 1) & (ph == 2 * (sec - 1)))
            def _():
                spread(emb, emb_in, emb_ss, emb_rs, True)
                spread(hid, hid_in, hid_ss, hid_rs, True)

            @pl.when((pos == 0) & (ph == 7 - sec))
            def _():
                spread(cot, cot_in, cot_ss, cot_rs, True)
            return c

        return lax.fori_loop(0, 3, chunk, c)

    lax.fori_loop(0, 8, forward_phase, 0)
    exchange(xs, 0, 0, xf_ss, xf_rs, 6).wait_send()

    def backward_phase(bph, c):
        ph = 7 - bph
        step = ph // 2
        blk = lax.rem(ph, 2)
        par = lax.rem(bph, 2)
        old = 1 - par

        def chunk(pos, c):
            @pl.when((bph >= 1) & (pos == 0))
            def _():
                exchange(dxs, old, pl.multiple_of(32 * par, 32), xb_ss, xb_rs, bph - 1).wait_recv()

            @pl.when(blk == 1)
            def _():
                arrived(cot, cot_in, cot_rs, step, pos)
                here = shift_out(to_windows(cot_in[step, pos].astype(F32))).reshape(256, 256)
                xin[...] = here + toward_shifted(dxs, old, pos)

            @pl.when(blk == 0)
            def _():
                xin[...] = toward_plain(dxs, old, pos)

            @pl.when(ph < 5)
            def _():
                act_in(ph, pos).wait()

            slot = act.at[lax.rem(ph, 3), pos]
            dx = b_chunk(xin[...], wq.at[blk], wo.at[blk], wu.at[blk], wd.at[blk], gn.at[blk], slot, rst.at[ph, pos],
                         gv.at[blk], gb.at[blk], lt, rt, pos)

            @pl.when((bph >= 2) & (pos == 0))
            def _():
                exchange(dxs, par, pl.multiple_of(32 * old, 32), xb_ss, xb_rs, bph - 2).wait_send()

            @pl.when(blk == 1)
            def _():
                dxs[par, pos] = dx.reshape(4, 64, 256)

            @pl.when(blk == 0)
            def _():
                db = dx.astype(BF)
                dxs[par, pos] = db.astype(F32).reshape(4, 64, 256)
                rows = to_rows(db.astype(F32).reshape(4, 8, 8, 256)).astype(BF)
                fg_st[step, pos] = rows
                lg_st[step, pos] = dot_nt(rows, wl[...]).astype(BF)
                gl[...] += dot_tn(hid_in[step, pos], rows)
                home_copy(fg_st, fg_home, fg_ss, fg_rs, step, pos, True)
                home_copy(lg_st, lg_home, lg_ss, lg_rs, step, pos, True)

            @pl.when((bph < 7) & (pos == 0))
            def _():
                exchange(dxs, par, pl.multiple_of(32 * old, 32), xb_ss, xb_rs, bph).start()
            return c

        lax.fori_loop(0, 3, chunk, 0)
        weight_grads(gw.at[blk], lt, rt, act.at[lax.rem(ph, 3)])

        @pl.when(ph >= 3)
        def _():
            for pos in range(3):
                act_in(ph - 3, pos).start()
        return c

    lax.fori_loop(0, 8, backward_phase, 0)
    exchange(dxs, 0, 32, xb_ss, xb_rs, 6).wait_send()

    spread(emb, emb_in, emb_ss, emb_rs, False)
    spread(hid, hid_in, hid_ss, hid_rs, False)
    spread(cot, cot_in, cot_ss, cot_rs, False)

    def leave(i, c):
        step, pos = i // 3, lax.rem(i, 3)
        home_copy(y_st, y_home, y_ss, y_rs, step, pos, False)
        home_copy(fg_st, fg_home, fg_ss, fg_rs, step, pos, False)
        home_copy(lg_st, lg_home, lg_ss, lg_rs, step, pos, False)
        return c

    lax.fori_loop(0, 12, leave, 0)
    home_arrivals(y_st, y_home, y_rs)
    home_arrivals(fg_st, fg_home, fg_rs)
    home_arrivals(lg_st, lg_home, lg_rs)


def rollout(emb, hid, cot, wq, wo, wu, wd, wl, gn, bt):
    vm = pl.BlockSpec(memory_space=pltpu.VMEM)
    far = pl.BlockSpec(memory_space=pl.ANY)
    S = jax.ShapeDtypeStruct
    dma = pltpu.SemaphoreType.DMA
    return pl.pallas_call(
        rollout_kernel,
        name="rollout",
        in_specs=[far, far, far, vm, vm, vm, vm, vm, vm, vm],
        out_specs=(far, far, far, vm, vm, vm, vm, far),
        out_shape=(
            S((6, 2, 256, 256), BF), S((6, 2, 256, 256), BF), S((6, 2, 256, 32), BF),
            S((2, 12, 256, 256), F32),
            S((2, 64, 512), F32), S((2, 4, 8, 256), F32), S((32, 256), F32),
            S((5, 3, 18, 256, 256), BF),
        ),
        scratch_shapes=[
            pltpu.VMEM((4, 3, 256, 256), BF), pltpu.VMEM((4, 3, 256, 256), BF), pltpu.VMEM((4, 3, 256, 32), BF),
            pltpu.VMEM((4, 3, 256, 256), BF), pltpu.VMEM((4, 3, 256, 256), BF), pltpu.VMEM((4, 3, 256, 32), BF),
            pltpu.VMEM((2, 4, 4, 64, 256), F32), pltpu.VMEM((2, 4, 4, 64, 256), F32), pltpu.VMEM((256, 256), F32),
            pltpu.VMEM((3, 3, 18, 256, 256), BF), pltpu.VMEM((8, 3, 2, 256, 128), F32),
            pltpu.VMEM((4, 3, 256, 256), BF), pltpu.VMEM((8, 3, 256, 256), BF),
            dma((3, 4)), dma((4, 3)), dma((3, 4)), dma((4, 3)), dma((3, 4)), dma((4, 3)),
            dma((4, 3)), dma((3, 4)), dma((4, 3)), dma((3, 4)), dma((4, 3)), dma((3, 4)),
            dma((7,)), dma((7,)), dma((7,)), dma((7,)), dma((5, 3)), dma((5, 3)),
        ],
        compiler_params=pltpu.CompilerParams(collective_id=0, has_side_effects=True, vmem_limit_bytes=60 * 2**20),
        cost_estimate=pl.CostEstimate(flops=60 * 10**9, bytes_accessed=100 * 10**6, transcendentals=0),
    )(emb, hid, cot, wq, wo, wu, wd, wl, gn, bt)


def offset_index(window):
    row_ids = np.repeat(np.arange(window), window)
    col_ids = np.tile(np.arange(window), window)
    return (
        (row_ids[:, None] - row_ids[None, :] + window - 1) * (2 * window - 1)
        + col_ids[:, None]
        - col_ids[None, :]
        + window
        - 1
    )


def picker():
    index = offset_index(8).T.reshape(-1)
    return (np.arange(225)[:, None] == index[None, :]).astype(np.float32)


def penalties():
    rows = np.repeat(np.arange(8) // 4, 8)
    cols = np.tile(np.arange(8) // 4, 8)
    out = []
    for by_row in (0, 1):
        for by_col in (0, 1):
            label = rows * by_row * 2 + cols * by_col
            out.append(np.where(label[:, None] == label[None, :], 0.0, -100.0))
    return np.stack(out).astype(np.float32)[:, :, None, :]


def on_device(
    embedded_tiles, hidden_sample, cotangent, lengths, gain_attn, shift_attn, w_qkv, rel_table, w_out,
    gain_mlp, shift_mlp, w_up, w_down, w_latent,
):
    sec = lax.axis_index("section")
    active = sec < lengths
    emb = embedded_tiles.reshape(6, 2, 256, 256)
    hid = hidden_sample.reshape(6, 2, 256, 32)
    masked = jnp.where(active[:, None, None], cotangent[0], 0)
    cot = jnp.concatenate([masked[:, 128:], masked[:, :128]], axis=1).reshape(6, 2, 256, 256)
    gn = jnp.stack([gain_attn, shift_attn, gain_mlp, shift_mlp], axis=1).astype(F32)
    pick = jnp.asarray(picker(), BF)
    table = lax.dot_general(
        rel_table.transpose(0, 2, 1).reshape(16, 225), pick, (((1,), (0,)), ((), ())), preferred_element_type=F32)
    table = table.reshape(2, 8, 64, 64).transpose(0, 2, 1, 3)
    bt = jnp.concatenate([table[:1], table[1:] + jnp.asarray(penalties())], axis=0) * LOG2E
    bt = bt.reshape(5, 64, 512)
    out = rollout(emb, hid, cot, w_qkv, w_out, w_up, w_down, w_latent, gn, bt)
    y, fg, lg, gw, gb, gv, gl, _ = out
    gw, gb, gv, gl = lax.psum((gw, gb, gv.sum(2), gl), ("section", "batch"))
    y = y.reshape(6, 512, 256)
    y = jnp.concatenate([y[:, 384:], y[:, :384]], axis=1)
    y = jnp.where(active[:, None, None], y, 0)
    by_head = gb.reshape(2, 64, 8, 64).transpose(0, 2, 1, 3).reshape(16, 4096)
    rel = lax.dot_general(
        by_head, jnp.asarray(picker()), (((1,), (1,)), ((), ())), precision=lax.Precision.HIGHEST,
        preferred_element_type=F32)
    rel = rel.reshape(2, 8, 225).transpose(0, 2, 1)
    gq = gw[:, 0:3].transpose(0, 2, 1, 3).reshape(2, 256, 768)
    gu = gw[:, 4:8].transpose(0, 2, 1, 3).reshape(2, 256, 1024)
    gd = gw[:, 8:12].transpose(0, 1, 3, 2).reshape(2, 1024, 256)
    return (
        y[None], fg.reshape(1, 6, 512, 256), lg.reshape(1, 6, 512, 32),
        gv[:, 0], gv[:, 1], gq, rel, gw[:, 3], gv[:, 2], gv[:, 3], gu, gd, gl,
    )


def solution(mesh):
    data = P("section", "batch", None, None)
    return jax.shard_map(
        on_device,
        mesh=mesh,
        in_specs=(data, data, data, P("batch")) + (P(),) * 10,
        out_specs=(data, data, data) + (P(),) * 10,
        check_vma=False,
    )
```

```python
import functools

import jax
import jax.numpy as jnp
import numpy as np
from jax import lax
from jax.experimental import pallas as pl
from jax.experimental.pallas import tpu as pltpu
from jax.sharding import PartitionSpec as P

BF = jnp.bfloat16
F32 = jnp.float32
LOG2E = 1.4426950408889634
SCALE = 32**-0.5


def dot(a, b):
    return lax.dot_general(a, b, (((1,), (0,)), ((), ())), preferred_element_type=F32)


def dot_nt(a, b):
    return lax.dot_general(a, b, (((1,), (1,)), ((), ())), preferred_element_type=F32)


def dot_tn(a, b):
    return lax.dot_general(a, b, (((0,), (0,)), ((), ())), preferred_element_type=F32)


PHI = (0.7978695563668204, 0.0363928095591428, -8.82196615782389e-05, -3.6600001215273455e-05, 1.418529678284452e-06)


def gelu_pair(z):
    square = z * z
    inside = jnp.minimum(square, 22.0)
    poly = PHI[4]
    for c in PHI[3::-1]:
        poly = poly * inside + c
    phi = 0.5 + 0.5 * jnp.tanh(z * poly)
    density = jnp.exp2(square * (-0.5 * LOG2E)) * 0.3989422804014327
    return z * phi, phi + z * density


def norm(x):
    centered = x - jnp.mean(x, axis=-1, keepdims=True)
    r = lax.rsqrt(jnp.mean(centered * centered, axis=-1, keepdims=True) + 1e-5)
    return centered * r, r


def norm_back(dn, n, r):
    m1 = jnp.mean(dn, axis=-1, keepdims=True)
    m2 = jnp.mean(dn * n, axis=-1, keepdims=True)
    return r * (dn - m1 - n * m2)


def low_lanes(rows):
    return lax.broadcasted_iota(jnp.int32, (rows, 128), 1) < 64


def head_blocks(t):
    cols = []
    for h in range(4):
        parts = []
        if h:
            parts.append(jnp.zeros((32 * h, 128), BF))
        parts.append(t[32 * h:32 * h + 32])
        if h < 3:
            parts.append(jnp.zeros((96 - 32 * h, 128), BF))
        cols.append(jnp.concatenate(parts, axis=0))
    return jnp.concatenate(cols, axis=1)


def own_window(both):
    lo = low_lanes(64)
    return jnp.concatenate(
        [jnp.where(lo, both[0:64, 128 * h:128 * h + 128], both[64:128, 128 * h:128 * h + 128]) for h in range(4)], axis=1)


def by_window(p):
    lane = lax.broadcasted_iota(jnp.int32, (1, 512), 1)
    lo = jnp.where(lane % 128 < 64, 1.0, 0.0).astype(BF)
    hi = jnp.where(lane % 128 < 64, 0.0, 1.0).astype(BF)
    return jnp.concatenate([p * lo, p * hi], axis=0)


def f_parts(x, wq, wo, wu, wd, gn, bias, act, rst, done):
    s = {}

    def start():
        xv = x()
        n1, r1 = norm(xv)
        rst[0] = jnp.broadcast_to(r1, (256, 128))
        act[0] = n1.astype(BF)
        normed = (n1 * gn[0:1] + gn[1:2]).astype(BF)
        act[1] = normed
        qkv = dot(normed, wq[...]).astype(BF)
        s['q'], s['k'], s['v'] = qkv[:, 0:256], qkv[:, 256:512], qkv[:, 512:768]
        act[3] = s['k']
        act[4] = s['v']
        s['qt'] = s['q'].T
        act[2] = s['qt']
        s['vt'] = s['v'].T

    def attention(g, wp):
        def run():
            ch = slice(g * 128, (g + 1) * 128)
            tok = slice(wp * 128, (wp + 1) * 128)
            both = dot(s['k'][tok, ch], head_blocks(s['qt'][ch, tok]))
            sc = own_window(both) * (SCALE * LOG2E) + bias(g, wp)
            e = jnp.exp2(sc - jnp.max(sc, axis=0, keepdims=True))
            p = (e * (1.0 / jnp.sum(e, axis=0, keepdims=True))).astype(BF)
            act[5 + g, wp * 128:wp * 128 + 64, :] = p[:, 0:256]
            act[5 + g, wp * 128 + 64:wp * 128 + 128, :] = p[:, 256:512]
            pb = by_window(p)
            for h in range(4):
                rows = slice(g * 128 + 32 * h, g * 128 + 32 * h + 32)
                act[7, rows, tok] = dot(s['vt'][rows, tok], pb[:, 128 * h:128 * h + 128]).astype(BF)
        return run

    def middle():
        h = x() + dot_tn(act[7], wo[...])
        n2, r2 = norm(h)
        rst[1] = jnp.broadcast_to(r2, (256, 128))
        act[8] = n2.astype(BF)
        second = (n2 * gn[2:3] + gn[3:4]).astype(BF)
        act[9] = second
        s['second'] = second
        s['y'] = h

    def mlp(j):
        def run():
            a, slope = gelu_pair(dot(s['second'], wu[:, j * 256:(j + 1) * 256]))
            a = a.astype(BF)
            act[10 + j] = a
            act[14 + j] = slope.astype(BF)
            s['y'] = s['y'] + dot(a, wd[j * 256:(j + 1) * 256, :])
            if j == 3:
                done(s['y'])
        return run

    return [start] + [attention(g, wp) for g in range(2) for wp in range(2)] + [middle] + [mlp(j) for j in range(4)]


def colsum(a):
    return jnp.sum(a.reshape(32, 8, 256), axis=0)


def b_parts(dout, wq, wo, wu, wd, gn, act, rst, gv, gb, gw, done):
    s = {}

    def start():
        s['dout'] = dout()
        s['db'] = s['dout'].astype(BF)
        s['dbt'] = s['db'].T
        s['st'] = act[9].T
        s['ds'] = None

    def mlp(j):
        def run():
            c = slice(j * 256, (j + 1) * 256)
            da = dot_nt(s['db'], wd[c, :])
            dpre = (da * act[14 + j].astype(F32)).astype(BF)
            ds = dot_nt(dpre, wu[:, c])
            s['ds'] = ds if s['ds'] is None else s['ds'] + ds
            gw[8 + j] += dot(s['dbt'], act[10 + j])
            gw[4 + j] += dot(s['st'], dpre)
        return run

    def middle():
        ds = s['ds']
        n2 = act[8].astype(F32)
        gv[2] += colsum(ds * n2)
        gv[3] += colsum(ds)
        s['dh'] = s['dout'] + norm_back(ds * gn[2:3], n2, rst[1][:, 0:1])
        db2 = s['dh'].astype(BF)
        s['dat'] = dot_nt(wo[...], db2).astype(BF)
        gw[3] += dot(act[7], db2)
        s['kt'] = act[3].T
        s['gb'] = [None, None]
        s['dq'], s['dk'], s['dv'] = {}, {}, {}

    def attention(g, wp):
        def run():
            ch = slice(g * 128, (g + 1) * 128)
            tok = slice(wp * 128, (wp + 1) * 128)
            ab = head_blocks(s['dat'][ch, tok])
            qb = head_blocks(act[2, ch, tok])
            dp = own_window(dot(act[4, tok, ch], ab))
            p = jnp.concatenate(
                [act[5 + g, wp * 128:wp * 128 + 64, :], act[5 + g, wp * 128 + 64:wp * 128 + 128, :]], axis=1)
            pf = p.astype(F32)
            t = dp * pf
            dsc = t - pf * jnp.sum(t, axis=0, keepdims=True)
            s['gb'][g] = dsc if s['gb'][g] is None else s['gb'][g] + dsc
            sb = by_window((dsc * SCALE).astype(BF))
            s['dv'][g, wp] = dot_nt(by_window(p), ab).astype(BF)
            s['dk'][g, wp] = dot_nt(sb, qb).astype(BF)
            for h in range(4):
                rows = slice(g * 128 + 32 * h, g * 128 + 32 * h + 32)
                s['dq'][g, h, wp] = dot(s['kt'][rows, tok], sb[:, 128 * h:128 * h + 128]).astype(BF)
        return run

    def finish():
        for g in range(2):
            gb[:, g * 512:(g + 1) * 512] += s['gb'][g]
        cat = jnp.concatenate
        dqt = cat([cat([s['dq'][g, h, wp] for wp in range(2)], axis=1) for g in range(2) for h in range(4)], axis=0)
        dq = dqt.T
        dk = cat([cat([s['dk'][g, wp] for g in range(2)], axis=1) for wp in range(2)], axis=0)
        dv = cat([cat([s['dv'][g, wp] for g in range(2)], axis=1) for wp in range(2)], axis=0)
        dn = dot_nt(dq, wq[:, 0:256]) + dot_nt(dk, wq[:, 256:512]) + dot_nt(dv, wq[:, 512:768])
        nt = act[1].T
        gw[0] += dot(nt, dq)
        gw[1] += dot(nt, dk)
        gw[2] += dot(nt, dv)
        n1 = act[0].astype(F32)
        gv[0] += colsum(dn * n1)
        gv[1] += colsum(dn)
        done(s['dh'] + norm_back(dn * gn[0:1], n1, rst[0][:, 0:1]))

    return ([start] + [mlp(j) for j in range(4)] + [middle]
            + [attention(g, wp) for g in range(2) for wp in range(2)] + [finish])


MESH = pl.DeviceIdType.MESH
SECTIONS = 4


def local_copy(src, dst, sem):
    return pltpu.make_async_copy(src, dst, sem)


def to_windows(rows):
    return rows.reshape(8, 4, 8, rows.shape[-1]).transpose(1, 0, 2, 3)


def to_rows(tiles):
    return tiles.transpose(1, 0, 2, 3).reshape(256, tiles.shape[-1])


def turn(tiles):
    flat = tiles.reshape(32, 8, 256)
    return jnp.concatenate([flat[:, 4:8], flat[:, 0:4]], axis=1).reshape(4, 8, 8, 256)


def shift_out(tiles):
    turned = turn(tiles)
    nxt = jnp.concatenate([turned[1:], turned[:1]], axis=0)
    low_half = lax.broadcasted_iota(jnp.int32, (1, 1, 8, 256), 2) < 4
    return jnp.where(low_half, turned, nxt)


def shift_back(tiles):
    turned = turn(tiles)
    prev = jnp.concatenate([turned[3:], turned[:3]], axis=0)
    low_half = lax.broadcasted_iota(jnp.int32, (1, 1, 8, 256), 2) < 4
    return jnp.where(low_half, prev, turned)


def toward_shifted(buf, par, pos):
    own = buf[par, pos, :, 32:64, :].reshape(4, 4, 8, 256)
    other = buf[par, 3 - pos, :, 0:32, :].reshape(4, 4, 8, 256)
    return shift_out(jnp.concatenate([own, other], axis=1)).reshape(256, 256)


def toward_plain(buf, par, pos):
    other = buf[par, 3 - pos, :, 32:64, :].reshape(4, 4, 8, 256)
    own = buf[par, pos, :, 0:32, :].reshape(4, 4, 8, 256)
    return shift_back(jnp.concatenate([other, own], axis=1)).reshape(256, 256)


F_FIRST = [((), 0), ((), 1)]
F_MAIN = [((0,), 2), ((1,), 3), ((2, 3), 4), ((4,), 5), ((5,), 6), ((6, 7), 7), ((8, 9), 8)]
F_LAST = [((), 9)]
B_FIRST = [((), 0), ((), 1)]
B_MAIN = [((0,), 2), ((1, 2), 3), ((3,), 4), ((4,), 5), ((5,), 6), ((6, 7), 7), ((8, 9), 8), ((10,), 9)]
B_LAST = [((), 10)]


def ordered(plan, p0, p1, p2):
    for mine, both in plan:
        p1[both]()
        p2[both]()
        for i in mine:
            p0[i]()


def rollout_kernel(
    emb, hid, cot, wq, wo, wu, wd, wl, gn, bt,
    y_home, fg_home, lg_home, grads, act_far,
    emb_in, cot_in, hid_in, y_st, fg_st, lg_st, xs, dxs, xin, yout, act, rst, gb, gv, gl,
    emb_ss, emb_rs, hid_ss, hid_rs, cot_ss, cot_rs,
    y_ss, y_rs, fg_ss, fg_rs, lg_ss, lg_rs, xf_ss, xf_rs, xb_ss, xb_rs, act_os, act_is,
):
    sec = lax.axis_index("section")
    bat = lax.axis_index("batch")
    core = lax.rem(bat, 2)
    first = bat - core
    partner = first + 1 - core

    barrier = pltpu.get_barrier_semaphore()
    xs[1] = jnp.zeros((4, 4, 64, 256), F32)
    dxs[1] = jnp.zeros((4, 4, 64, 256), F32)
    for ds in range(SECTIONS):
        for dc in range(2):
            if ds == 0 and dc == 0:
                continue
            pl.semaphore_signal(
                barrier, inc=1,
                device_id={"section": lax.rem(sec + ds, SECTIONS), "batch": first + lax.rem(core + dc, 2)},
                device_id_type=MESH)
    pl.semaphore_wait(barrier, 2 * SECTIONS - 1)

    def spread(src, dst, ssem, rsem, begin):
        for pos in (1, 2, 0):
            for t in range(4):
                if pos == 0:
                    to_sec = 2 * core + t // 2
                    to_bat = first + t % 2
                    piece = src.at[4 + t // 2, t % 2]
                    mine = (to_sec == sec) & (core == t % 2)
                else:
                    to_sec = jnp.int32(t)
                    to_bat = bat
                    piece = src.at[t, pos - 1]
                    mine = to_sec == sec

                @pl.when(mine)
                def _():
                    if begin:
                        local_copy(piece, dst.at[sec, pos], rsem.at[sec, pos]).start()

                @pl.when(jnp.logical_not(mine))
                def _():
                    rc = pltpu.make_async_remote_copy(
                        src_ref=piece, dst_ref=dst.at[sec, pos],
                        send_sem=ssem.at[pos, t], recv_sem=rsem.at[sec, pos],
                        device_id={"section": to_sec, "batch": to_bat}, device_id_type=MESH)
                    if begin:
                        rc.start()
                    else:
                        rc.wait_send()

    def arrived(src, dst, rsem, step, pos):
        local_copy(src.at[0, 0], dst.at[step, pos], rsem.at[step, pos]).wait()

    def home_copy(src, dst, ssem, rsem, step, pos, begin):
        half = pos == 0
        item = jnp.where(half, 4 + lax.rem(sec, 2), sec)
        part = jnp.where(half, core, pos - 1)
        to_bat = jnp.where(half, first + sec // 2, bat)
        slot = jnp.where(half, lax.rem(sec, 2) * 2 + core, sec)
        mine = (step == sec) & (to_bat == bat)

        @pl.when(mine)
        def _():
            if begin:
                local_copy(src.at[step, pos], dst.at[item, part], rsem.at[pos, slot]).start()

        @pl.when(jnp.logical_not(mine))
        def _():
            rc = pltpu.make_async_remote_copy(
                src_ref=src.at[step, pos], dst_ref=dst.at[item, part],
                send_sem=ssem.at[step, pos], recv_sem=rsem.at[pos, slot],
                device_id={"section": step, "batch": to_bat}, device_id_type=MESH)
            if begin:
                rc.start()
            else:
                rc.wait_send()

    def home_arrivals(src, dst, rsem):
        for pos in range(3):
            for t in range(4):
                piece = dst.at[4 + t // 2, t % 2] if pos == 0 else dst.at[t, pos - 1]
                local_copy(src.at[0, 0], piece, rsem.at[pos, t]).wait()

    def exchange(buf, par, off, ssem, rsem, n):
        return pltpu.make_async_remote_copy(
            src_ref=buf.at[par, 0, :, pl.ds(off, 32), :],
            dst_ref=buf.at[par, 3, :, pl.ds(off, 32), :],
            send_sem=ssem.at[n], recv_sem=rsem.at[n],
            device_id={"section": sec, "batch": partner}, device_id_type=MESH)

    spread(emb, emb_in, emb_ss, emb_rs, True)
    spread(hid, hid_in, hid_ss, hid_rs, True)

    for ref in (gb, gv, gl):
        ref[...] = jnp.zeros(ref.shape, F32)

    def clear(t, c):
        grads[t] = jnp.zeros((256, 256), F32)
        return c

    lax.fori_loop(0, 26, clear, 0)

    def act_out(ph, pos):
        return local_copy(act.at[lax.rem(ph, 3), pos], act_far.at[ph, pos], act_os.at[ph, pos])

    def act_in(ph, pos):
        return local_copy(act_far.at[ph, pos], act.at[lax.rem(ph, 3), pos], act_is.at[ph, pos])

    def keep(ref, pos):
        def run(value):
            ref[pos] = value
        return run

    def forward_phase(ph, c):
        step = ph // 2
        blk = lax.rem(ph, 2)
        par = lax.rem(ph, 2)
        old = 1 - par

        def build(pos):
            @pl.when(blk == 0)
            def _():
                arrived(emb, emb_in, emb_rs, step, pos)
                arrived(hid, hid_in, hid_rs, step, pos)
                lifted = emb_in[step, pos].astype(F32) + dot(hid_in[step, pos], wl[...])
                carried = toward_plain(xs, old, pos).astype(BF).astype(F32)
                xin[pos] = to_windows(lifted).reshape(256, 256) + carried

            @pl.when(blk == 1)
            def _():
                xin[pos] = toward_shifted(xs, old, pos)

        def parts(pos):
            bottom = core if pos == 0 else pos - 1

            def bias(g, wp):
                return bt[jnp.where(blk == 0, 0, 1 + 2 * bottom + wp), :, g * 512:(g + 1) * 512]

            return f_parts(lambda: xin[pos], wq.at[blk], wo.at[blk], wu.at[blk], wd.at[blk], gn.at[blk], bias,
                           act.at[lax.rem(ph, 3), pos], rst.at[ph, pos], keep(yout, pos))

        def finish(pos):
            xs[par, pos] = yout[pos].reshape(4, 64, 256)

            @pl.when(blk == 1)
            def _():
                tiles = shift_back(xs[par, pos].reshape(4, 8, 8, 256))
                y_st[step, pos] = to_rows(tiles).astype(BF)
                home_copy(y_st, y_home, y_ss, y_rs, step, pos, True)

            @pl.when(ph < 5)
            def _():
                act_out(ph, pos).start()

        p0, p1, p2 = parts(0), parts(1), parts(2)

        @pl.when(ph >= 3)
        def _():
            for pos in range(3):
                act_out(ph - 3, pos).wait()

        build(1)
        build(2)
        ordered(F_FIRST, p0, p1, p2)

        @pl.when(ph >= 1)
        def _():
            exchange(xs, old, pl.multiple_of(32 * old, 32), xf_ss, xf_rs, ph - 1).wait_recv()

        build(0)
        ordered(F_MAIN, p0, p1, p2)

        @pl.when(ph >= 2)
        def _():
            exchange(xs, par, pl.multiple_of(32 * par, 32), xf_ss, xf_rs, ph - 2).wait_send()

        finish(0)

        @pl.when(ph < 7)
        def _():
            exchange(xs, par, pl.multiple_of(32 * par, 32), xf_ss, xf_rs, ph).start()

        @pl.when(ph == 4 - sec)
        def _():
            spread(cot, cot_in, cot_ss, cot_rs, True)

        ordered(F_LAST, p0, p1, p2)
        finish(1)
        finish(2)
        return c

    lax.fori_loop(0, 8, forward_phase, 0)
    exchange(xs, 0, 0, xf_ss, xf_rs, 6).wait_send()

    def backward_phase(bph, c):
        ph = 7 - bph
        step = ph // 2
        blk = lax.rem(ph, 2)
        par = lax.rem(bph, 2)
        old = 1 - par

        def build(pos):
            @pl.when(blk == 1)
            def _():
                arrived(cot, cot_in, cot_rs, step, pos)
                here = shift_out(to_windows(cot_in[step, pos].astype(F32))).reshape(256, 256)
                xin[pos] = here + toward_shifted(dxs, old, pos)

            @pl.when(blk == 0)
            def _():
                xin[pos] = toward_plain(dxs, old, pos)

            @pl.when(ph < 5)
            def _():
                act_in(ph, pos).wait()

        def parts(pos):
            return b_parts(lambda: xin[pos], wq.at[blk], wo.at[blk], wu.at[blk], wd.at[blk], gn.at[blk],
                           act.at[lax.rem(ph, 3), pos], rst.at[ph, pos], gv.at[blk], gb.at[blk],
                           grads.at[pl.ds(12 * blk, 12)], keep(yout, pos))

        def finish(pos):
            @pl.when(ph >= 3)
            def _():
                act_in(ph - 3, pos).start()

            @pl.when(blk == 1)
            def _():
                dxs[par, pos] = yout[pos].reshape(4, 64, 256)

            @pl.when(blk == 0)
            def _():
                db = yout[pos].astype(BF).astype(F32)
                dxs[par, pos] = db.reshape(4, 64, 256)
                rows = to_rows(db.reshape(4, 8, 8, 256)).astype(BF)
                fg_st[step, pos] = rows
                lg_st[step, pos] = dot_nt(rows, wl[...]).astype(BF)
                gl[...] += dot_tn(hid_in[step, pos], rows)
                home_copy(fg_st, fg_home, fg_ss, fg_rs, step, pos, True)
                home_copy(lg_st, lg_home, lg_ss, lg_rs, step, pos, True)

        p0, p1, p2 = parts(0), parts(1), parts(2)
        build(1)
        build(2)
        ordered(B_FIRST, p0, p1, p2)

        @pl.when(bph >= 1)
        def _():
            exchange(dxs, old, pl.multiple_of(32 * par, 32), xb_ss, xb_rs, bph - 1).wait_recv()

        build(0)
        ordered(B_MAIN, p0, p1, p2)

        @pl.when(bph >= 2)
        def _():
            exchange(dxs, par, pl.multiple_of(32 * old, 32), xb_ss, xb_rs, bph - 2).wait_send()

        finish(0)

        @pl.when(bph < 7)
        def _():
            exchange(dxs, par, pl.multiple_of(32 * old, 32), xb_ss, xb_rs, bph).start()

        ordered(B_LAST, p0, p1, p2)
        finish(1)
        finish(2)
        return c

    lax.fori_loop(0, 8, backward_phase, 0)
    exchange(dxs, 0, 32, xb_ss, xb_rs, 6).wait_send()

    lo = low_lanes(64)
    for blk in range(2):
        for half in range(2):
            parts = []
            for pair in range(2):
                h = 4 * half + 2 * pair
                a = gb[blk, :, 128 * h:128 * h + 128]
                b = gb[blk, :, 128 * h + 128:128 * h + 256]
                parts.append(jnp.where(lo, a + pltpu.roll(a, 64, 1), b + pltpu.roll(b, 64, 1)))
            grads[24, 128 * blk + 64 * half:128 * blk + 64 * half + 64, :] = jnp.concatenate(parts, axis=1)
    grads[25, 0:8, :] = jnp.concatenate(
        [jnp.sum(gv[blk, i], axis=0, keepdims=True) for blk in range(2) for i in range(4)], axis=0)
    grads[25, 8:40, :] = gl[...]

    spread(emb, emb_in, emb_ss, emb_rs, False)
    spread(hid, hid_in, hid_ss, hid_rs, False)
    spread(cot, cot_in, cot_ss, cot_rs, False)

    def leave(i, c):
        step, pos = i // 3, lax.rem(i, 3)
        home_copy(y_st, y_home, y_ss, y_rs, step, pos, False)
        home_copy(fg_st, fg_home, fg_ss, fg_rs, step, pos, False)
        home_copy(lg_st, lg_home, lg_ss, lg_rs, step, pos, False)
        return c

    lax.fori_loop(0, 12, leave, 0)
    home_arrivals(y_st, y_home, y_rs)
    home_arrivals(fg_st, fg_home, fg_rs)
    home_arrivals(lg_st, lg_home, lg_rs)


def rollout(emb, hid, cot, wq, wo, wu, wd, wl, gn, bt):
    vm = pl.BlockSpec(memory_space=pltpu.VMEM)
    far = pl.BlockSpec(memory_space=pl.ANY)
    S = jax.ShapeDtypeStruct
    dma = pltpu.SemaphoreType.DMA
    return pl.pallas_call(
        rollout_kernel,
        name="rollout",
        in_specs=[far, far, far, vm, vm, vm, vm, vm, vm, vm],
        out_specs=(far, far, far, vm, far),
        out_shape=(
            S((6, 2, 256, 256), BF), S((6, 2, 256, 256), BF), S((6, 2, 256, 32), BF),
            S((26, 256, 256), F32),
            S((5, 3, 18, 256, 256), BF),
        ),
        scratch_shapes=[
            pltpu.VMEM((4, 3, 256, 256), BF), pltpu.VMEM((4, 3, 256, 256), BF), pltpu.VMEM((4, 3, 256, 32), BF),
            pltpu.VMEM((4, 3, 256, 256), BF), pltpu.VMEM((4, 3, 256, 256), BF), pltpu.VMEM((4, 3, 256, 32), BF),
            pltpu.VMEM((2, 4, 4, 64, 256), F32), pltpu.VMEM((2, 4, 4, 64, 256), F32), pltpu.VMEM((3, 256, 256), F32), pltpu.VMEM((3, 256, 256), F32),
            pltpu.VMEM((3, 3, 18, 256, 256), BF), pltpu.VMEM((8, 3, 2, 256, 128), F32),
            pltpu.VMEM((2, 64, 1024), F32), pltpu.VMEM((2, 4, 8, 256), F32), pltpu.VMEM((32, 256), F32),
            dma((3, 4)), dma((4, 3)), dma((3, 4)), dma((4, 3)), dma((3, 4)), dma((4, 3)),
            dma((4, 3)), dma((3, 4)), dma((4, 3)), dma((3, 4)), dma((4, 3)), dma((3, 4)),
            dma((7,)), dma((7,)), dma((7,)), dma((7,)), dma((5, 3)), dma((5, 3)),
        ],
        compiler_params=pltpu.CompilerParams(collective_id=0, has_side_effects=True, vmem_limit_bytes=60 * 2**20),
        cost_estimate=pl.CostEstimate(flops=60 * 10**9, bytes_accessed=100 * 10**6, transcendentals=0),
    )(emb, hid, cot, wq, wo, wu, wd, wl, gn, bt)


def all_reduce_kernel(size, grads, gq, go, gu, gd, small, out1, in1, out2, in2, total, gathered,
                      s1, r1, s2, r2, s3, r3, s4, r4):
    sec = lax.axis_index("section")
    bat = lax.axis_index("batch")
    core = lax.rem(bat, 2)
    half_batch = size // 2
    chips = SECTIONS * half_batch
    me = sec * half_batch + bat // 2
    rows = gathered.shape[0]
    half = rows // 2
    piece = half // chips
    partner = {"section": sec, "batch": bat + 1 - 2 * core}

    def twin(k):
        chip = lax.rem(me + k, chips)
        return chip, {"section": chip // half_batch, "batch": 2 * lax.rem(chip, half_batch) + core}

    barrier = pltpu.get_barrier_semaphore()

    def greet(k, c):
        pl.semaphore_signal(barrier, inc=1, device_id=twin(k)[1], device_id_type=MESH)
        return c

    lax.fori_loop(1, chips, greet, 0)
    pl.semaphore_signal(barrier, inc=1, device_id=partner, device_id_type=MESH)
    pl.semaphore_wait(barrier, chips)

    def at(base, chip):
        return pl.ds(pl.multiple_of(base + chip * piece, 16), piece)

    mine = core * half
    theirs = half - mine

    def swap(k):
        chip = lax.rem(me + k, chips)
        return pltpu.make_async_remote_copy(
            src_ref=out1.at[chip], dst_ref=in1.at[chip], send_sem=s1.at[chip], recv_sem=r1.at[chip],
            device_id=partner, device_id_type=MESH)

    def scatter(k):
        chip, where = twin(k)
        return pltpu.make_async_remote_copy(
            src_ref=out2.at[chip], dst_ref=in2.at[me], send_sem=s2.at[chip], recv_sem=r2.at[me],
            device_id=where, device_id_type=MESH)

    def gather(k):
        chip, where = twin(k)
        here = gathered.at[at(mine, me)]
        return pltpu.make_async_remote_copy(
            src_ref=here, dst_ref=here, send_sem=s3.at[chip], recv_sem=r3.at[me],
            device_id=where, device_id_type=MESH)

    def share(chip):
        here = gathered.at[at(mine, chip)]
        return pltpu.make_async_remote_copy(
            src_ref=here, dst_ref=here, send_sem=s4.at[chip], recv_sem=r4.at[chip],
            device_id=partner, device_id_type=MESH)

    def run(lo, hi, fn):
        def body(k, c):
            fn(k)
            return c
        lax.fori_loop(lo, hi, body, 0)

    def first(k):
        chip = lax.rem(me + k, chips)
        out1[chip] = grads[at(theirs, chip), :].astype(BF)
        swap(k).start()

    run(1, chips + 1, first)

    def second(k):
        chip = lax.rem(me + k, chips)
        swap(k).wait_recv()
        out2[chip] = (grads[at(mine, chip), :] + in1[chip].astype(F32)).astype(BF)
        scatter(k).start()

    run(1, chips, second)
    swap(0).wait_recv()
    total[...] = grads[at(mine, me), :] + in1[me].astype(F32)

    def third(k):
        chip = lax.rem(me + chips - k, chips)
        pltpu.make_async_copy(in2.at[chip], in2.at[chip], r2.at[chip]).wait()
        total[...] += in2[chip].astype(F32)

    run(1, chips, third)
    gathered[at(mine, me), :] = total[...].astype(BF)
    share(me).start()
    run(1, chips, lambda k: gather(k).start())

    def fourth(k):
        chip = lax.rem(me + chips - k, chips)
        here = gathered.at[at(mine, chip)]
        pltpu.make_async_copy(here, here, r3.at[chip]).wait()
        share(chip).start()

    run(1, chips, fourth)

    def fifth(k):
        chip = lax.rem(me + chips - k, chips)
        here = gathered.at[at(theirs, chip)]
        pltpu.make_async_copy(here, here, r4.at[chip]).wait()

    run(0, chips, fifth)

    def tile(t):
        return gathered[t * 256:(t + 1) * 256, :].astype(F32)

    for blk in range(2):
        for j in range(3):
            gq[blk, :, j * 256:(j + 1) * 256] = tile(12 * blk + j)
        go[blk] = tile(12 * blk + 3)
        for j in range(4):
            gu[blk, :, j * 256:(j + 1) * 256] = tile(12 * blk + 4 + j)
            gd[blk, j * 256:(j + 1) * 256, :] = tile(12 * blk + 8 + j).T
    small[0:256, :] = tile(24)
    small[256:296, :] = gathered[25 * 256:25 * 256 + 40, :].astype(F32)

    run(0, chips, lambda k: swap(k).wait_send())
    run(1, chips, lambda k: scatter(k).wait_send())
    run(1, chips, lambda k: gather(k).wait_send())
    run(0, chips, lambda k: share(k).wait_send())


def all_reduce(grads, size):
    vm = pl.BlockSpec(memory_space=pltpu.VMEM)
    S = jax.ShapeDtypeStruct
    dma = pltpu.SemaphoreType.DMA
    chips = SECTIONS * size // 2
    unit = 32 * chips
    rows = (26 * 256 + unit - 1) // unit * unit
    grads = grads.reshape(26 * 256, 256)
    if rows > 26 * 256:
        grads = jnp.pad(grads, ((0, rows - 26 * 256), (0, 0)))
    piece = rows // 2 // chips
    return pl.pallas_call(
        functools.partial(all_reduce_kernel, size),
        name="all_reduce",
        in_specs=[vm],
        out_specs=(vm,) * 5,
        out_shape=(S((2, 256, 768), F32), S((2, 256, 256), F32), S((2, 256, 1024), F32), S((2, 1024, 256), F32), S((296, 256), F32)),
        scratch_shapes=[pltpu.VMEM((chips, piece, 256), BF)] * 4
        + [pltpu.VMEM((piece, 256), F32), pltpu.VMEM((rows, 256), BF)]
        + [dma((chips,))] * 8,
        compiler_params=pltpu.CompilerParams(collective_id=1, has_side_effects=True, vmem_limit_bytes=60 * 2**20),
        cost_estimate=pl.CostEstimate(flops=0, bytes_accessed=14 * 10**6, transcendentals=0),
    )(grads)


def offset_index(window):
    row_ids = np.repeat(np.arange(window), window)
    col_ids = np.tile(np.arange(window), window)
    return (
        (row_ids[:, None] - row_ids[None, :] + window - 1) * (2 * window - 1)
        + col_ids[:, None]
        - col_ids[None, :]
        + window
        - 1
    )


def picker():
    index = offset_index(8).T.reshape(-1)
    return (np.arange(225)[:, None] == index[None, :]).astype(np.float32)


def penalties():
    rows = np.repeat(np.arange(8) // 4, 8)
    cols = np.tile(np.arange(8) // 4, 8)
    out = []
    for by_row in (0, 1):
        for wp in (0, 1):
            both = []
            for w in (2 * wp, 2 * wp + 1):
                label = rows * by_row * 2 + cols * (w == 3)
                both.append(np.where(label[:, None] == label[None, :], 0.0, -100.0))
            out.append(np.stack(both, axis=1)[:, None])
    return np.stack(out).astype(np.float32)


def on_device(
    embedded_tiles, hidden_sample, cotangent, lengths, gain_attn, shift_attn, w_qkv, rel_table, w_out,
    gain_mlp, shift_mlp, w_up, w_down, w_latent,
):
    sec = lax.axis_index("section")
    active = sec < lengths
    emb = embedded_tiles.reshape(6, 2, 256, 256)
    hid = hidden_sample.reshape(6, 2, 256, 32)
    masked = jnp.where(active[:, None, None], cotangent[0], 0)
    cot = jnp.concatenate([masked[:, 128:], masked[:, :128]], axis=1).reshape(6, 2, 256, 256)
    gn = jnp.stack([gain_attn, shift_attn, gain_mlp, shift_mlp], axis=1).astype(F32)
    pick = jnp.asarray(picker(), BF)
    table = lax.dot_general(
        rel_table.transpose(0, 2, 1).reshape(16, 225), pick, (((1,), (0,)), ((), ())), preferred_element_type=F32)
    table = table.reshape(2, 8, 64, 64).transpose(0, 2, 1, 3)[:, :, :, None, :]
    plain = jnp.broadcast_to(table[:1], (1, 64, 8, 2, 64))
    bt = jnp.concatenate([plain, table[1:] + jnp.asarray(penalties())], axis=0) * LOG2E
    bt = bt.reshape(5, 64, 1024)
    out = rollout(emb, hid, cot, w_qkv, w_out, w_up, w_down, w_latent, gn, bt)
    y, fg, lg, grads, _ = out
    gq, go, gu, gd, small = all_reduce(grads, lax.axis_size("batch"))
    gb, gv, gl = small[:256], small[256:264].reshape(2, 4, 256), small[264:296]
    y = y.reshape(6, 512, 256)
    y = jnp.concatenate([y[:, 384:], y[:, :384]], axis=1)
    y = jnp.where(active[:, None, None], y, 0)
    by_head = gb.reshape(2, 2, 64, 4, 64).transpose(0, 1, 3, 2, 4).reshape(16, 4096)
    rel = lax.dot_general(by_head.astype(BF), pick, (((1,), (1,)), ((), ())), preferred_element_type=F32)
    rel = rel.reshape(2, 8, 225).transpose(0, 2, 1)
    return (
        y[None], fg.reshape(1, 6, 512, 256), lg.reshape(1, 6, 512, 32),
        gv[:, 0], gv[:, 1], gq, rel, go, gv[:, 2], gv[:, 3], gu, gd, gl,
    )


def solution(mesh):
    data = P("section", "batch", None, None)
    return jax.shard_map(
        on_device,
        mesh=mesh,
        in_specs=(data, data, data, P("batch")) + (P(),) * 10,
        out_specs=(data, data, data) + (P(),) * 10,
        check_vma=False,
    )
```

```python
import functools

import jax
import jax.numpy as jnp
import numpy as np
from jax import lax
from jax.experimental import pallas as pl
from jax.experimental.pallas import tpu as pltpu
from jax.sharding import PartitionSpec as P

BF = jnp.bfloat16
F32 = jnp.float32
LOG2E = 1.4426950408889634
SCALE = 32**-0.5


def dot(a, b):
    return lax.dot_general(a, b, (((1,), (0,)), ((), ())), preferred_element_type=F32)


def dot_nt(a, b):
    return lax.dot_general(a, b, (((1,), (1,)), ((), ())), preferred_element_type=F32)


def dot_tn(a, b):
    return lax.dot_general(a, b, (((0,), (0,)), ((), ())), preferred_element_type=F32)


PHI = (0.7978695563668204, 0.0363928095591428, -8.82196615782389e-05, -3.6600001215273455e-05, 1.418529678284452e-06)


def gelu_pair(z):
    square = z * z
    inside = jnp.minimum(square, 22.0)
    poly = PHI[4]
    for c in PHI[3::-1]:
        poly = poly * inside + c
    phi = 0.5 + 0.5 * jnp.tanh(z * poly)
    density = jnp.exp2(square * (-0.5 * LOG2E)) * 0.3989422804014327
    return z * phi, phi + z * density


def norm(x):
    centered = x - jnp.mean(x, axis=-1, keepdims=True)
    r = lax.rsqrt(jnp.mean(centered * centered, axis=-1, keepdims=True) + 1e-5)
    return centered * r, r


def norm_back(dn, n, r):
    m1 = jnp.mean(dn, axis=-1, keepdims=True)
    m2 = jnp.mean(dn * n, axis=-1, keepdims=True)
    return r * (dn - m1 - n * m2)


def low_lanes(rows):
    return lax.broadcasted_iota(jnp.int32, (rows, 128), 1) < 64


def head_blocks(t):
    cols = []
    for h in range(4):
        parts = []
        if h:
            parts.append(jnp.zeros((32 * h, 128), BF))
        parts.append(t[32 * h:32 * h + 32])
        if h < 3:
            parts.append(jnp.zeros((96 - 32 * h, 128), BF))
        cols.append(jnp.concatenate(parts, axis=0))
    return jnp.concatenate(cols, axis=1)


def own_window(both):
    lo = low_lanes(64)
    return jnp.concatenate(
        [jnp.where(lo, both[0:64, 128 * h:128 * h + 128], both[64:128, 128 * h:128 * h + 128]) for h in range(4)], axis=1)


def by_window(p):
    lane = lax.broadcasted_iota(jnp.int32, (1, 512), 1)
    lo = jnp.where(lane % 128 < 64, 1.0, 0.0).astype(BF)
    hi = jnp.where(lane % 128 < 64, 0.0, 1.0).astype(BF)
    return jnp.concatenate([p * lo, p * hi], axis=0)


def f_parts(x, wq, wo, wu, wd, gn, bias, act, rst, done):
    s = {}

    def start():
        xv = x()
        n1, r1 = norm(xv)
        s['r1'] = r1
        act[0] = n1.astype(BF)
        normed = (n1 * gn[0:1] + gn[1:2]).astype(BF)
        act[1] = normed
        qkv = dot(normed, wq[...]).astype(BF)
        s['q'], s['k'], s['v'] = qkv[:, 0:256], qkv[:, 256:512], qkv[:, 512:768]
        act[3] = s['k']
        act[4] = s['v']
        s['qt'] = s['q'].T
        act[2] = s['qt']
        s['vt'] = s['v'].T

    def attention(g, wp):
        def run():
            ch = slice(g * 128, (g + 1) * 128)
            tok = slice(wp * 128, (wp + 1) * 128)
            both = dot(s['k'][tok, ch], head_blocks(s['qt'][ch, tok]))
            sc = own_window(both) * (SCALE * LOG2E) + bias(g, wp)
            e = jnp.exp2(sc - jnp.max(sc, axis=0, keepdims=True))
            p = (e * (1.0 / jnp.sum(e, axis=0, keepdims=True))).astype(BF)
            act[5 + g, wp * 128:wp * 128 + 64, :] = p[:, 0:256]
            act[5 + g, wp * 128 + 64:wp * 128 + 128, :] = p[:, 256:512]
            pb = by_window(p)
            for h in range(4):
                rows = slice(g * 128 + 32 * h, g * 128 + 32 * h + 32)
                act[7, rows, tok] = dot(s['vt'][rows, tok], pb[:, 128 * h:128 * h + 128]).astype(BF)
        return run

    def middle():
        h = x() + dot_tn(act[7], wo[...])
        n2, r2 = norm(h)
        rst[...] = jnp.where(low_lanes(256), s['r1'], r2)
        act[8] = n2.astype(BF)
        second = (n2 * gn[2:3] + gn[3:4]).astype(BF)
        act[9] = second
        s['second'] = second
        s['y'] = h

    def mlp(j):
        def run():
            a, slope = gelu_pair(dot(s['second'], wu[:, j * 256:(j + 1) * 256]))
            a = a.astype(BF)
            act[10 + j] = a
            act[14 + j] = slope.astype(BF)
            s['y'] = s['y'] + dot(a, wd[j * 256:(j + 1) * 256, :])
            if j == 3:
                done(s['y'])
        return run

    return [start] + [attention(g, wp) for g in range(2) for wp in range(2)] + [middle] + [mlp(j) for j in range(4)]


def colsum(a):
    return jnp.sum(a.reshape(32, 8, 256), axis=0)


def b_parts(dout, wq, wo, wu, wd, gn, act, rst, gv, gb, gw, done):
    s = {}

    def start():
        s['dout'] = dout()
        s['db'] = s['dout'].astype(BF)
        s['dbt'] = s['db'].T
        s['st'] = act[9].T
        s['ds'] = None

    def mlp(j):
        def run():
            c = slice(j * 256, (j + 1) * 256)
            da = dot_nt(s['db'], wd[c, :])
            dpre = (da * act[14 + j].astype(F32)).astype(BF)
            ds = dot_nt(dpre, wu[:, c])
            s['ds'] = ds if s['ds'] is None else s['ds'] + ds
            gw(8 + j)[...] += dot(s['dbt'], act[10 + j])
            gw(4 + j)[...] += dot(s['st'], dpre)
        return run

    def middle():
        ds = s['ds']
        n2 = act[8].astype(F32)
        gv[2] += colsum(ds * n2)
        gv[3] += colsum(ds)
        s['dh'] = s['dout'] + norm_back(ds * gn[2:3], n2, rst[...][:, 64:65])
        db2 = s['dh'].astype(BF)
        s['dat'] = dot_nt(wo[...], db2).astype(BF)
        gw(3)[...] += dot(act[7], db2)
        s['kt'] = act[3].T
        s['gb'] = [None, None]
        s['dq'], s['dk'], s['dv'] = {}, {}, {}

    def attention(g, wp):
        def run():
            ch = slice(g * 128, (g + 1) * 128)
            tok = slice(wp * 128, (wp + 1) * 128)
            ab = head_blocks(s['dat'][ch, tok])
            qb = head_blocks(act[2, ch, tok])
            dp = own_window(dot(act[4, tok, ch], ab))
            p = jnp.concatenate(
                [act[5 + g, wp * 128:wp * 128 + 64, :], act[5 + g, wp * 128 + 64:wp * 128 + 128, :]], axis=1)
            pf = p.astype(F32)
            t = dp * pf
            dsc = t - pf * jnp.sum(t, axis=0, keepdims=True)
            s['gb'][g] = dsc if s['gb'][g] is None else s['gb'][g] + dsc
            sb = by_window((dsc * SCALE).astype(BF))
            s['dv'][g, wp] = dot_nt(by_window(p), ab).astype(BF)
            s['dk'][g, wp] = dot_nt(sb, qb).astype(BF)
            for h in range(4):
                rows = slice(g * 128 + 32 * h, g * 128 + 32 * h + 32)
                s['dq'][g, h, wp] = dot(s['kt'][rows, tok], sb[:, 128 * h:128 * h + 128]).astype(BF)
        return run

    def finish():
        for g in range(2):
            gb[:, g * 512:(g + 1) * 512] += s['gb'][g]
        cat = jnp.concatenate
        dqt = cat([cat([s['dq'][g, h, wp] for wp in range(2)], axis=1) for g in range(2) for h in range(4)], axis=0)
        dq = dqt.T
        dk = cat([cat([s['dk'][g, wp] for g in range(2)], axis=1) for wp in range(2)], axis=0)
        dv = cat([cat([s['dv'][g, wp] for g in range(2)], axis=1) for wp in range(2)], axis=0)
        dn = dot_nt(dq, wq[:, 0:256]) + dot_nt(dk, wq[:, 256:512]) + dot_nt(dv, wq[:, 512:768])
        nt = act[1].T
        gw(0)[...] += dot(nt, dq)
        gw(1)[...] += dot(nt, dk)
        gw(2)[...] += dot(nt, dv)
        n1 = act[0].astype(F32)
        gv[0] += colsum(dn * n1)
        gv[1] += colsum(dn)
        done(s['dh'] + norm_back(dn * gn[0:1], n1, rst[...][:, 0:1]))

    return ([start] + [mlp(j) for j in range(4)] + [middle]
            + [attention(g, wp) for g in range(2) for wp in range(2)] + [finish])


MESH = pl.DeviceIdType.MESH
SECTIONS = 4


def local_copy(src, dst, sem):
    return pltpu.make_async_copy(src, dst, sem)


def to_windows(rows):
    return rows.reshape(8, 4, 8, rows.shape[-1]).transpose(1, 0, 2, 3)


def to_rows(tiles):
    return tiles.transpose(1, 0, 2, 3).reshape(256, tiles.shape[-1])


def turn(tiles):
    flat = tiles.reshape(32, 8, 256)
    return jnp.concatenate([flat[:, 4:8], flat[:, 0:4]], axis=1).reshape(4, 8, 8, 256)


def shift_out(tiles):
    turned = turn(tiles)
    nxt = jnp.concatenate([turned[1:], turned[:1]], axis=0)
    low_half = lax.broadcasted_iota(jnp.int32, (1, 1, 8, 256), 2) < 4
    return jnp.where(low_half, turned, nxt)


def shift_back(tiles):
    turned = turn(tiles)
    prev = jnp.concatenate([turned[3:], turned[:3]], axis=0)
    low_half = lax.broadcasted_iota(jnp.int32, (1, 1, 8, 256), 2) < 4
    return jnp.where(low_half, prev, turned)


def toward_shifted(buf, par, pos):
    own = buf[par, pos, :, 32:64, :].reshape(4, 4, 8, 256)
    other = buf[par, 3 - pos, :, 0:32, :].reshape(4, 4, 8, 256)
    return shift_out(jnp.concatenate([own, other], axis=1)).reshape(256, 256)


def toward_plain(buf, par, pos):
    other = buf[par, 3 - pos, :, 32:64, :].reshape(4, 4, 8, 256)
    own = buf[par, pos, :, 0:32, :].reshape(4, 4, 8, 256)
    return shift_back(jnp.concatenate([other, own], axis=1)).reshape(256, 256)


F_FIRST = [((), 0), ((), 1)]
F_MAIN = [((0,), 2), ((1,), 3), ((2, 3), 4), ((4,), 5), ((5,), 6), ((6, 7), 7), ((8, 9), 8)]
F_LAST = [((), 9)]
B_FIRST = [((), 0), ((), 1)]
B_MAIN = [((0,), 2), ((1, 2), 3), ((3,), 4), ((4,), 5), ((5,), 6), ((6, 7), 7), ((8, 9), 8), ((10,), 9)]
B_LAST = [((), 10)]


def ordered(plan, p0, p1, p2):
    for mine, both in plan:
        p1[both]()
        p2[both]()
        for i in mine:
            p0[i]()


def ring(n, fn, start=0):
    def body(k, c):
        fn(k)
        return c
    lax.fori_loop(start, n, body, 0)


def fill_bias(rel, pick, line, bt):
    lo = low_lanes(8)
    key = lax.broadcasted_iota(jnp.int32, (64, 128), 0)
    lane = lax.broadcasted_iota(jnp.int32, (64, 128), 1)
    apart_rows = key // 32 != (lane % 64) // 32
    apart_cols = jnp.logical_and((key % 8) // 4 != (lane % 8) // 4, lane >= 64)
    for blk in range(2):
        raw = dot(rel[blk], pick[...]) * LOG2E
        for n in range(32):
            tile = raw[:, 128 * n:128 * n + 128]
            other = pltpu.roll(tile, 64, 1)
            line[16 * n:16 * n + 8, :] = jnp.where(lo, tile, other)
            line[16 * n + 8:16 * n + 16, :] = jnp.where(lo, other, tile)
        for h in range(8):
            cols = slice(128 * h, 128 * h + 128)
            plain = line[pl.ds(h, 64, stride=8), :]
            if blk == 0:
                bt[0, :, cols] = plain
            else:
                cut = plain - 100.0 * LOG2E
                bt[1, :, cols] = plain
                bt[2, :, cols] = jnp.where(apart_cols, cut, plain)
                bt[3, :, cols] = jnp.where(apart_rows, cut, plain)
                bt[4, :, cols] = jnp.where(jnp.logical_or(apart_rows, apart_cols), cut, plain)


def table_grad(gb, pick, line):
    for h in range(8):
        a = gb[:, 128 * h:128 * h + 128]
        line[pl.ds(h, 64, stride=8), :] = a + pltpu.roll(a, 64, 1)
    lo = low_lanes(8)
    row = jnp.concatenate(
        [jnp.where(lo, line[16 * n:16 * n + 8, :], line[16 * n + 8:16 * n + 16, :]) for n in range(32)], axis=1)
    high = row.astype(BF)
    rest = (row - high.astype(F32)).astype(BF)
    return dot_nt(high, pick[...]) + dot_nt(rest, pick[...])


def sizes(batch):
    unit = 16 * SECTIONS * (batch // 2)
    ra = -(-3072 // (2 * unit)) * 2 * unit
    rb = -(-(3072 + 64) // (2 * unit)) * 2 * unit
    units = rb // 2 // unit
    c = units * 3 // 7
    return ra, rb, (ra // 2, (units - c) * unit, c * unit)


class Reduction:
    def __init__(self, base, half, g1, g2, core, partner, grads, gathered, bufs, sems):
        self.n1, self.me1, self.dev1 = g1
        self.n2, self.me2, self.dev2 = g2
        self.p1 = half // self.n1
        self.p2 = self.p1 // self.n2
        self.mine = base + core * half
        self.theirs = base + (1 - core) * half
        self.partner, self.grads, self.gathered = partner, grads, gathered
        self.o1, self.i1, self.o2, self.i2, self.o3, self.i3, self.t = bufs
        (self.s1, self.r1, self.s2, self.r2, self.s3, self.r3, self.sg2, self.rg2, self.sg1, self.rg1, self.sc, self.rc) = sems

    def rows1(self, start, i1):
        return pl.ds(pl.multiple_of(start + i1 * self.p1, 16), self.p1)

    def piece(self, start, i1, i2):
        return self.gathered.at[pl.ds(pl.multiple_of(start + i1 * self.p1 + i2 * self.p2, 16), self.p2)]

    def send(self, src, dst, ssem, rsem, device):
        return pltpu.make_async_remote_copy(
            src_ref=src, dst_ref=dst, send_sem=ssem, recv_sem=rsem, device_id=device, device_id_type=MESH)

    def landed(self, ref, sem):
        pltpu.make_async_copy(ref, ref, sem).wait()

    def others1(self, fn):
        ring(self.n1, lambda k: fn(lax.rem(self.me1 + k, self.n1)), 1)

    def others2(self, fn):
        ring(self.n2, lambda k: fn(lax.rem(self.me2 + k, self.n2)), 1)

    def to_partner(self, i):
        return self.send(self.o1.at[i], self.i1.at[i], self.s1.at[i], self.r1.at[i], self.partner)

    def scatter1(self, i):
        return self.send(self.o2.at[i], self.i2.at[self.me1], self.s2.at[i], self.r2.at[self.me1], self.dev1(i))

    def scatter2(self, i):
        return self.send(self.o3.at[i], self.i3.at[self.me2], self.s3.at[i], self.r3.at[self.me2], self.dev2(i))

    def gather2(self, i):
        here = self.piece(self.mine, self.me1, self.me2)
        return self.send(here, here, self.sg2.at[i], self.rg2.at[self.me2], self.dev2(i))

    def gather1(self, i, j2):
        here = self.piece(self.mine, self.me1, j2)
        return self.send(here, here, self.sg1.at[i, j2], self.rg1.at[self.me1, j2], self.dev1(i))

    def share(self, i1, i2):
        here = self.piece(self.mine, i1, i2)
        return self.send(here, here, self.sc.at[i1, i2], self.rc.at[i1, i2], self.partner)

    def swap(self):
        def one(k):
            i = lax.rem(self.me1 + k, self.n1)
            self.o1[i] = self.grads[self.rows1(self.theirs, i), :].astype(BF)
            self.to_partner(i).start()
        ring(self.n1 + 1, one, 1)

    def summed(self, i):
        self.landed(self.i1.at[i], self.r1.at[i])
        return self.grads[self.rows1(self.mine, i), :] + self.i1[i].astype(F32)

    def stage1(self):
        def one(i):
            self.o2[i] = self.summed(i).astype(BF)
            self.scatter1(i).start()
        self.others1(one)
        self.t[...] = self.summed(self.me1)

    def stage2(self):
        def add(j):
            self.landed(self.i2.at[j], self.r2.at[j])
            self.t[...] += self.i2[j].astype(F32)
        self.others1(add)

        def one(i):
            self.o3[i] = self.t[self.slice2(i), :].astype(BF)
            self.scatter2(i).start()
        self.others2(one)

    def slice2(self, i):
        return pl.ds(pl.multiple_of(i * self.p2, 16), self.p2)

    def pass_on(self, j2):
        self.others1(lambda i: self.gather1(i, j2).start())
        self.share(self.me1, j2).start()

    def stage3(self):
        here = self.slice2(self.me2)

        def add(j):
            self.landed(self.i3.at[j], self.r3.at[j])
            self.t[here, :] += self.i3[j].astype(F32)
        self.others2(add)
        self.piece(self.mine, self.me1, self.me2)[...] = self.t[here, :].astype(BF)
        self.others2(lambda i: self.gather2(i).start())
        self.pass_on(self.me2)

    def stage4(self):
        def one(j):
            self.landed(self.piece(self.mine, self.me1, j), self.rg2.at[j])
            self.pass_on(j)
        self.others2(one)

    def stage5(self):
        def one(j1):
            def two(j2):
                self.landed(self.piece(self.mine, j1, j2), self.rg1.at[j1, j2])
                self.share(j1, j2).start()
            ring(self.n2, two)
        self.others1(one)

    def stage6(self):
        ring(self.n1, lambda i: ring(self.n2, lambda j: self.landed(self.piece(self.theirs, i, j), self.rc.at[i, j])))

    def drain(self):
        ring(self.n1, lambda i: self.to_partner(i).wait_send())
        self.others1(lambda i: self.scatter1(i).wait_send())
        self.others2(lambda i: self.scatter2(i).wait_send())
        self.others2(lambda i: self.gather2(i).wait_send())
        self.others1(lambda i: ring(self.n2, lambda j: self.gather1(i, j).wait_send()))
        ring(self.n1, lambda i: ring(self.n2, lambda j: self.share(i, j).wait_send()))


def rollout_kernel(
    size, lengths, emb, hid, cot, wq, wo, wu, wd, wl, ga, sa, gm, sm, rel, pick,
    y_home, fg_home, lg_home, gq, go, gu, gd, g_ga, g_sa, g_gm, g_sm, g_rel, g_lat, act_far,
    emb_in, cot_in, hid_in, lg_st, cot_mk, xs, dxs, xin, act, rst, gb, gv, gl, gn, bt, line,
    grads, gathered,
    emb_ss, emb_rs, hid_ss, hid_rs, cot_ss, cot_rs,
    y_ss, y_rs, fg_ss, fg_rs, lg_ss, lg_rs, xf_ss, xf_rs, xb_ss, xb_rs, act_os, act_is, cot_ls, out_ss, *reduction,
):
    sec = lax.axis_index("section")
    bat = lax.axis_index("batch")
    core = lax.rem(bat, 2)
    first = bat - core
    partner = first + 1 - core
    rows_a, rows_b, halves = sizes(size)

    barrier = pltpu.get_barrier_semaphore()
    xs[1] = jnp.zeros((4, 4, 64, 256), F32)
    dxs[1] = jnp.zeros((4, 4, 64, 256), F32)
    for ds in range(SECTIONS):
        for dc in range(2):
            if ds == 0 and dc == 0:
                continue
            pl.semaphore_signal(
                barrier, inc=1,
                device_id={"section": lax.rem(sec + ds, SECTIONS), "batch": first + lax.rem(core + dc, 2)},
                device_id_type=MESH)

    def greet(k):
        pl.semaphore_signal(
            barrier, inc=1, device_id={"section": sec, "batch": lax.rem(bat + 2 * k, size)}, device_id_type=MESH)

    ring(size // 2, greet, 1)
    pl.semaphore_wait(barrier, 2 * SECTIONS - 1 + size // 2 - 1)

    def route(pos, t):
        if pos == 0:
            to_sec, to_bat = 2 * core + t // 2, first + t % 2
            return to_sec, to_bat, 4 + t // 2, t % 2, jnp.logical_and(to_sec == sec, core == t % 2)
        return jnp.int32(t), bat, t, pos - 1, sec == t

    def deliver(src, dst, ssem, rsem, to_sec, to_bat, mine, begin):
        @pl.when(mine)
        def _():
            if begin:
                local_copy(src, dst, rsem).start()

        @pl.when(jnp.logical_not(mine))
        def _():
            rc = pltpu.make_async_remote_copy(
                src_ref=src, dst_ref=dst, send_sem=ssem, recv_sem=rsem,
                device_id={"section": to_sec, "batch": to_bat}, device_id_type=MESH)
            if begin:
                rc.start()
            else:
                rc.wait_send()

    def spread_tiles(begin):
        for pos in (1, 2, 0):
            for t in range(4):
                to_sec, to_bat, item, part, mine = route(pos, t)
                deliver(emb.at[item, part], emb_in.at[sec, pos], emb_ss.at[pos, t], emb_rs.at[sec, pos],
                        to_sec, to_bat, mine, begin)
                deliver(hid.at[item, :, pl.ds(256 * part, 256)], hid_in.at[sec, pos], hid_ss.at[pos, t],
                        hid_rs.at[sec, pos], to_sec, to_bat, mine, begin)

    def spread_cotangents(begin):
        for pos in (1, 2, 0):
            for t in range(4):
                to_sec, to_bat, item, part, mine = route(pos, t)
                for u in range(2):
                    deliver(cot_mk.at[item, (2 * part + 1 + u) % 4], cot_in.at[sec, pos, u], cot_ss.at[pos, t, u],
                            cot_rs.at[sec, pos, u], to_sec, to_bat, mine, begin)

    def home(step, pos):
        half = pos == 0
        item = jnp.where(half, 4 + lax.rem(sec, 2), sec)
        part = jnp.where(half, core, pos - 1)
        to_bat = jnp.where(half, first + sec // 2, bat)
        slot = jnp.where(half, lax.rem(sec, 2) * 2 + core, sec)
        return item, part, to_bat, slot, jnp.logical_and(step == sec, to_bat == bat)

    def return_y(step, pos, begin):
        item, part, to_bat, slot, mine = home(step, pos)
        for u in range(2):
            deliver(emb_in.at[step, pos, u], y_home.at[item, lax.rem(2 * part + 1 + u, 4)], y_ss.at[step, pos, u],
                    y_rs.at[pos, slot, u], step, to_bat, mine, begin)

    def return_grads(step, pos, begin):
        item, part, to_bat, slot, mine = home(step, pos)
        deliver(cot_in.at[step, pos], fg_home.at[item, part], fg_ss.at[step, pos], fg_rs.at[pos, slot],
                step, to_bat, mine, begin)
        deliver(lg_st.at[step, pos], lg_home.at[item, :, pl.ds(pl.multiple_of(256 * part, 256), 256)],
                lg_ss.at[step, pos], lg_rs.at[pos, slot], step, to_bat, mine, begin)

    def exchange(buf, par, off, ssem, rsem, n):
        return pltpu.make_async_remote_copy(
            src_ref=buf.at[par, 0, :, pl.ds(off, 32), :],
            dst_ref=buf.at[par, 3, :, pl.ds(off, 32), :],
            send_sem=ssem.at[n], recv_sem=rsem.at[n],
            device_id={"section": sec, "batch": partner}, device_id_type=MESH)

    xy = (SECTIONS, sec, lambda i: {"section": i, "batch": bat})
    zs = (size // 2, bat // 2, lambda i: {"section": sec, "batch": 2 * i + core})
    bases = (0, rows_a, rows_a + 2 * halves[1])
    jobs = []
    for k, half in enumerate(halves):
        if half:
            g1, g2 = (zs, xy) if k == 2 else (xy, zs)
            jobs.append(Reduction(bases[k], half, g1, g2, core, {"section": sec, "batch": partner}, grads, gathered,
                                  reduction[19 * k:19 * k + 7], reduction[19 * k + 7:19 * k + 19]))
    early, late = jobs[0], jobs[1:][::-1]

    spread_tiles(True)
    local_copy(cot, cot_mk, cot_ls).start()
    for i, ref in enumerate((ga, sa, gm, sm)):
        for blk in range(2):
            gn[blk, i:i + 1, :] = ref[blk:blk + 1, :].astype(F32)
    fill_bias(rel, pick, line, bt)
    for ref in (gb, gv, gl):
        ref[...] = jnp.zeros(ref.shape, F32)

    def clear(t):
        grads[pl.ds(pl.multiple_of(64 * t, 64), 64), :] = jnp.zeros((64, 256), F32)

    ring((rows_a + rows_b) // 64, clear)

    def act_out(ph, pos):
        return local_copy(act.at[lax.rem(ph, 2), pos], act_far.at[ph, pos], act_os.at[ph, pos])

    def act_in(ph, pos):
        return local_copy(act_far.at[ph, pos], act.at[lax.rem(ph, 2), pos], act_is.at[ph, pos])

    def keep(ref, pos):
        def run(value):
            ref[pos] = value
        return run

    def forward_phase(ph):
        step = ph // 2
        blk = lax.rem(ph, 2)
        par = lax.rem(ph, 2)
        old = 1 - par

        def build(pos):
            @pl.when(blk == 0)
            def _():
                local_copy(emb.at[0, 0], emb_in.at[step, pos], emb_rs.at[step, pos]).wait()
                local_copy(hid.at[0, :, pl.ds(0, 256)], hid_in.at[step, pos], hid_rs.at[step, pos]).wait()
                lifted = emb_in[step, pos].reshape(256, 256).astype(F32) + dot_tn(hid_in[step, pos], wl[...])
                carried = toward_plain(xs, old, pos).astype(BF).astype(F32)
                xin[pos] = to_windows(lifted).reshape(256, 256) + carried

            @pl.when(blk == 1)
            def _():
                xin[pos] = toward_shifted(xs, old, pos)

        def parts(pos):
            bottom = core if pos == 0 else pos - 1

            def bias(g, wp):
                return bt[jnp.where(blk == 0, 0, 1 + 2 * bottom + wp), :, g * 512:(g + 1) * 512]

            return f_parts(lambda: xin[pos], wq.at[blk], wo.at[blk], wu.at[blk], wd.at[blk], gn.at[blk], bias,
                           act.at[lax.rem(ph, 2), pos], rst.at[ph, pos], keep(xin, pos))

        def finish(pos):
            xs[par, pos] = xin[pos].reshape(4, 64, 256)

            @pl.when(blk == 1)
            def _():
                rows = to_rows(shift_back(xs[par, pos].reshape(4, 8, 8, 256))).astype(BF)
                emb_in[step, pos] = rows.reshape(2, 128, 256)
                return_y(step, pos, True)

            @pl.when(ph < 6)
            def _():
                act_out(ph, pos).start()

        p0, p1, p2 = parts(0), parts(1), parts(2)

        @pl.when(ph >= 2)
        def _():
            for pos in range(3):
                act_out(ph - 2, pos).wait()

        build(1)
        build(2)
        ordered(F_FIRST, p0, p1, p2)

        @pl.when(ph >= 1)
        def _():
            exchange(xs, old, pl.multiple_of(32 * old, 32), xf_ss, xf_rs, ph - 1).wait_recv()

        build(0)
        ordered(F_MAIN, p0, p1, p2)

        @pl.when(ph >= 2)
        def _():
            exchange(xs, par, pl.multiple_of(32 * par, 32), xf_ss, xf_rs, ph - 2).wait_send()

        finish(0)

        @pl.when(ph < 7)
        def _():
            exchange(xs, par, pl.multiple_of(32 * par, 32), xf_ss, xf_rs, ph).start()

        @pl.when(ph == 4 - sec)
        def _():
            local_copy(cot, cot_mk, cot_ls).wait()
            for i in range(6):
                on = jnp.where(sec < lengths[i], 1.0, 0.0)
                for u in range(4):
                    cot_mk[i, u] = (cot_mk[i, u].astype(F32) * on).astype(BF)
            spread_cotangents(True)

        ordered(F_LAST, p0, p1, p2)
        finish(1)
        finish(2)

    ring(8, forward_phase)
    exchange(xs, 0, 0, xf_ss, xf_rs, 6).wait_send()

    def backward_phase(bph):
        ph = 7 - bph
        step = ph // 2
        blk = lax.rem(ph, 2)
        par = lax.rem(bph, 2)
        old = 1 - par

        def build(pos):
            @pl.when(blk == 1)
            def _():
                for u in range(2):
                    local_copy(cot_mk.at[0, 0], cot_in.at[step, pos, u], cot_rs.at[step, pos, u]).wait()
                rows = cot_in[step, pos].reshape(256, 256).astype(F32)
                xin[pos] = shift_out(to_windows(rows)).reshape(256, 256) + toward_shifted(dxs, old, pos)

            @pl.when(blk == 0)
            def _():
                xin[pos] = toward_plain(dxs, old, pos)

            @pl.when(ph < 6)
            def _():
                act_in(ph, pos).wait()

        def gw(t):
            return grads.at[pl.ds(pl.multiple_of(rows_a * (1 - blk) + 256 * t, 256), 256)]

        def parts(pos):
            return b_parts(lambda: xin[pos], wq.at[blk], wo.at[blk], wu.at[blk], wd.at[blk], gn.at[blk],
                           act.at[lax.rem(ph, 2), pos], rst.at[ph, pos], gv.at[blk], gb.at[blk], gw, keep(xin, pos))

        def finish(pos):
            @pl.when(ph >= 2)
            def _():
                act_in(ph - 2, pos).start()

            @pl.when(blk == 1)
            def _():
                dxs[par, pos] = xin[pos].reshape(4, 64, 256)

            @pl.when(blk == 0)
            def _():
                db = xin[pos].astype(BF).astype(F32)
                dxs[par, pos] = db.reshape(4, 64, 256)
                rows = to_rows(db.reshape(4, 8, 8, 256)).astype(BF)
                cot_in[step, pos] = rows.reshape(2, 128, 256)
                lg_st[step, pos] = dot_nt(wl[...], rows).astype(BF)
                gl[...] += dot(hid_in[step, pos], rows)
                return_grads(step, pos, True)

        p0, p1, p2 = parts(0), parts(1), parts(2)

        @pl.when(bph == 7)
        def _():
            early.swap()

        build(1)
        build(2)
        ordered(B_FIRST, p0, p1, p2)

        @pl.when(bph >= 1)
        def _():
            exchange(dxs, old, pl.multiple_of(32 * par, 32), xb_ss, xb_rs, bph - 1).wait_recv()

        build(0)

        @pl.when(bph == 7)
        def _():
            early.stage1()

        ordered(B_MAIN, p0, p1, p2)

        @pl.when(bph >= 2)
        def _():
            exchange(dxs, par, pl.multiple_of(32 * old, 32), xb_ss, xb_rs, bph - 2).wait_send()

        finish(0)

        @pl.when(bph < 7)
        def _():
            exchange(dxs, par, pl.multiple_of(32 * old, 32), xb_ss, xb_rs, bph).start()

        ordered(B_LAST, p0, p1, p2)
        finish(1)
        finish(2)

    ring(8, backward_phase)
    exchange(dxs, 0, 32, xb_ss, xb_rs, 6).wait_send()

    small = rows_a + 3072
    grads[small:small + 8, :] = jnp.concatenate(
        [jnp.sum(gv[blk, i], axis=0, keepdims=True) for blk in range(2) for i in range(4)], axis=0)
    grads[small + 8:small + 40, :] = gl[...]
    for blk in range(2):
        grads[small + 40 + 8 * blk:small + 48 + 8 * blk, 0:225] = table_grad(gb.at[blk], pick, line)

    for job in late:
        job.swap()
    early.stage2()
    for job in late:
        job.stage1()
    early.stage3()
    for job in late:
        job.stage2()
    early.stage4()
    for job in late:
        job.stage3()
    early.stage5()
    for job in late:
        job.stage4()
    early.stage6()

    def give(blk, t, dst, turn_it):
        here = pl.ds(rows_a * (1 - blk) + 256 * t, 256)
        value = gathered[here, :].astype(F32)
        grads[here, :] = value.T if turn_it else value
        copy = local_copy(grads.at[here], dst, out_ss.at[blk, t])
        copy.start()
        return copy

    def give_block(blk):
        out = [give(blk, j, gq.at[blk, :, pl.ds(256 * j, 256)], False) for j in range(3)]
        out.append(give(blk, 3, go.at[blk], False))
        out += [give(blk, 4 + j, gu.at[blk, :, pl.ds(256 * j, 256)], False) for j in range(4)]
        out += [give(blk, 8 + j, gd.at[blk, pl.ds(256 * j, 256), :], True) for j in range(4)]
        return out

    copies = give_block(1)
    for job in late:
        job.stage5()
    for job in late:
        job.stage6()
    copies += give_block(0)
    tail = gathered[small:small + 64, :].astype(F32)
    for i, ref in enumerate((g_ga, g_sa, g_gm, g_sm)):
        for blk in range(2):
            ref[blk:blk + 1, :] = tail[4 * blk + i:4 * blk + i + 1]
    g_lat[...] = tail[8:40]
    for blk in range(2):
        g_rel[blk] = tail[40 + 8 * blk:48 + 8 * blk, 0:225]

    spread_tiles(False)
    spread_cotangents(False)

    def leave(i):
        return_y(i // 3, lax.rem(i, 3), False)
        return_grads(i // 3, lax.rem(i, 3), False)

    ring(3 * SECTIONS, leave)
    for pos in range(3):
        for t in range(4):
            item, part = (4 + t // 2, t % 2) if pos == 0 else (t, pos - 1)
            for u in range(2):
                local_copy(emb_in.at[0, 0, 0], y_home.at[item, (2 * part + 1 + u) % 4], y_rs.at[pos, t, u]).wait()
            local_copy(cot_in.at[0, 0], fg_home.at[item, part], fg_rs.at[pos, t]).wait()
            local_copy(lg_st.at[0, 0], lg_home.at[item, :, pl.ds(256 * part, 256)], lg_rs.at[pos, t]).wait()
    for job in jobs:
        job.drain()
    for copy in copies:
        copy.wait()


def rollout(size, *operands):
    vm = pl.BlockSpec(memory_space=pltpu.VMEM)
    far = pl.BlockSpec(memory_space=pl.ANY)
    S = jax.ShapeDtypeStruct
    dma = pltpu.SemaphoreType.DMA
    rows_a, rows_b, halves = sizes(size)
    reduction = []
    for k, half in enumerate(halves):
        n1, n2 = (size // 2, SECTIONS) if k == 2 else (SECTIONS, size // 2)
        p1 = max(half // n1, 16)
        p2 = max(p1 // n2, 16)
        reduction += [pltpu.VMEM((n1, p1, 256), BF)] * 4 + [pltpu.VMEM((n2, p2, 256), BF)] * 2
        reduction += [pltpu.VMEM((p1, 256), F32)]
        reduction += [dma((n1,))] * 4 + [dma((n2,))] * 4 + [dma((n1, n2))] * 4
    return pl.pallas_call(
        functools.partial(rollout_kernel, size),
        name="rollout",
        in_specs=[pl.BlockSpec(memory_space=pltpu.SMEM), far, far, far] + [vm] * 11,
        out_specs=(far,) * 7 + (vm,) * 6 + (far,),
        out_shape=(
            S((6, 4, 128, 256), BF), S((6, 2, 2, 128, 256), BF), S((6, 32, 512), BF),
            S((2, 256, 768), F32), S((2, 256, 256), F32), S((2, 256, 1024), F32), S((2, 1024, 256), F32),
            S((2, 256), F32), S((2, 256), F32), S((2, 256), F32), S((2, 256), F32),
            S((2, 8, 225), F32), S((32, 256), F32),
            S((6, 3, 18, 256, 256), BF),
        ),
        scratch_shapes=[
            pltpu.VMEM((4, 3, 2, 128, 256), BF), pltpu.VMEM((4, 3, 2, 128, 256), BF), pltpu.VMEM((4, 3, 32, 256), BF),
            pltpu.VMEM((4, 3, 32, 256), BF),
            pltpu.VMEM((6, 4, 128, 256), BF),
            pltpu.VMEM((2, 4, 4, 64, 256), F32), pltpu.VMEM((2, 4, 4, 64, 256), F32),
            pltpu.VMEM((3, 256, 256), F32),
            pltpu.VMEM((2, 3, 18, 256, 256), BF), pltpu.VMEM((8, 3, 256, 128), F32),
            pltpu.VMEM((2, 64, 1024), F32), pltpu.VMEM((2, 4, 8, 256), F32), pltpu.VMEM((32, 256), F32),
            pltpu.VMEM((2, 4, 256), F32), pltpu.VMEM((5, 64, 1024), F32), pltpu.VMEM((512, 128), F32),
            pltpu.VMEM((rows_a + rows_b, 256), F32), pltpu.VMEM((rows_a + rows_b, 256), BF),
            dma((3, 4)), dma((4, 3)), dma((3, 4)), dma((4, 3)), dma((3, 4, 2)), dma((4, 3, 2)),
            dma((4, 3, 2)), dma((3, 4, 2)), dma((4, 3)), dma((3, 4)), dma((4, 3)), dma((3, 4)),
            dma((7,)), dma((7,)), dma((7,)), dma((7,)), dma((6, 3)), dma((6, 3)), dma, dma((2, 12)),
        ] + reduction,
        compiler_params=pltpu.CompilerParams(collective_id=0, has_side_effects=True, vmem_limit_bytes=61 * 2**20),
        cost_estimate=pl.CostEstimate(flops=60 * 10**9, bytes_accessed=100 * 10**6, transcendentals=0),
    )(*operands)


def picker():
    row = np.repeat(np.arange(8), 8)
    col = np.tile(np.arange(8), 8)
    index = (row[None, :] - row[:, None] + 7) * 15 + col[None, :] - col[:, None] + 7
    return (np.arange(225)[:, None] == index.reshape(1, -1)).astype(np.float32)


def on_device(
    embedded_tiles, hidden_sample, cotangent, lengths, gain_attn, shift_attn, w_qkv, rel_table, w_out,
    gain_mlp, shift_mlp, w_up, w_down, w_latent,
):
    active = lax.axis_index("section") < lengths
    out = rollout(
        lax.axis_size("batch"), lengths, embedded_tiles.reshape(6, 2, 2, 128, 256),
        hidden_sample[0].transpose(0, 2, 1), cotangent.reshape(6, 4, 128, 256),
        w_qkv, w_out, w_up, w_down, w_latent, gain_attn, shift_attn, gain_mlp, shift_mlp,
        rel_table.transpose(0, 2, 1), jnp.asarray(picker(), BF))
    y, fg, lg, gq, go, gu, gd, g_ga, g_sa, g_gm, g_sm, g_rel, g_lat, _ = out
    y = jnp.where(active[:, None, None], y.reshape(6, 512, 256), 0)
    return (
        y[None], fg.reshape(1, 6, 512, 256), lg.transpose(0, 2, 1)[None],
        g_ga, g_sa, gq, g_rel.transpose(0, 2, 1), go, g_gm, g_sm, gu, gd, g_lat,
    )


def solution(mesh):
    data = P("section", "batch", None, None)
    return jax.shard_map(
        on_device,
        mesh=mesh,
        in_specs=(data, data, data, P("batch")) + (P(),) * 10,
        out_specs=(data, data, data) + (P(),) * 10,
        check_vma=False,
    )
```

```python
import functools

import jax
import jax.numpy as jnp
import numpy as np
from jax import lax
from jax.experimental import pallas as pl
from jax.experimental.pallas import tpu as pltpu
from jax.sharding import PartitionSpec as P

BF = jnp.bfloat16
F32 = jnp.float32
LOG2E = 1.4426950408889634
SCALE = 32**-0.5


def dot(a, b):
    return lax.dot_general(a, b, (((1,), (0,)), ((), ())), preferred_element_type=F32)


def dot_nt(a, b):
    return lax.dot_general(a, b, (((1,), (1,)), ((), ())), preferred_element_type=F32)


def dot_tn(a, b):
    return lax.dot_general(a, b, (((0,), (0,)), ((), ())), preferred_element_type=F32)


PHI = (0.7978695563668204, 0.0363928095591428, -8.82196615782389e-05, -3.6600001215273455e-05, 1.418529678284452e-06)


def gelu_pair(z):
    square = z * z
    inside = jnp.minimum(square, 22.0)
    poly = PHI[4]
    for c in PHI[3::-1]:
        poly = poly * inside + c
    phi = 0.5 + 0.5 * jnp.tanh(z * poly)
    density = jnp.exp2(square * (-0.5 * LOG2E)) * 0.3989422804014327
    return z * phi, phi + z * density


def norm(x):
    centered = x - jnp.mean(x, axis=-1, keepdims=True)
    r = lax.rsqrt(jnp.mean(centered * centered, axis=-1, keepdims=True) + 1e-5)
    return centered * r, r


def norm_back(dn, n, r):
    m1 = jnp.mean(dn, axis=-1, keepdims=True)
    m2 = jnp.mean(dn * n, axis=-1, keepdims=True)
    return r * (dn - m1 - n * m2)


def low_lanes(rows):
    return lax.broadcasted_iota(jnp.int32, (rows, 128), 1) < 64


def head_rows(t):
    lane = lax.broadcasted_iota(jnp.int32, (1, 128), 1)
    return jnp.concatenate([t * jnp.where(lane // 32 == h, 1.0, 0.0).astype(BF) for h in range(4)], axis=0)


def own_rows(both):
    lo = low_lanes(64)
    return jnp.concatenate(
        [jnp.where(lo, both[128 * h:128 * h + 64], both[128 * h + 64:128 * h + 128]) for h in range(4)], axis=1)


def own_heads(rows):
    lane = lax.broadcasted_iota(jnp.int32, (128, 128), 1)
    return jnp.where(lane < 64, jnp.where(lane < 32, rows[0:128], rows[128:256]), jnp.where(lane < 96, rows[256:384], rows[384:512]))


def stacked(p):
    return jnp.concatenate([p[:, 128 * h:128 * h + 128] for h in range(4)], axis=0)


def by_window(p):
    lane = lax.broadcasted_iota(jnp.int32, (1, 512), 1)
    lo = jnp.where(lane % 128 < 64, 1.0, 0.0).astype(BF)
    hi = jnp.where(lane % 128 < 64, 0.0, 1.0).astype(BF)
    return jnp.concatenate([p * lo, p * hi], axis=0)


def f_parts(x, wq, wo, wu, wd, gn, bias, act, rst, done):
    s = {}

    def start():
        xv = x()
        n1, r1 = norm(xv)
        s['r1'] = r1
        act[0] = n1.astype(BF)
        normed = (n1 * gn[0:1] + gn[1:2]).astype(BF)
        act[1] = normed
        qkv = dot(normed, wq[...]).astype(BF)
        s['q'], s['k'], s['v'] = qkv[:, 0:256], qkv[:, 256:512], qkv[:, 512:768]
        act[3] = s['k']
        act[4] = s['v']
        s['qt'] = s['q'].T
        act[2] = s['qt']
        s['vt'] = s['v'].T

    def attention(g, wp):
        def run():
            ch = slice(g * 128, (g + 1) * 128)
            tok = slice(wp * 128, (wp + 1) * 128)
            both = dot(head_rows(s['k'][tok, ch]), s['qt'][ch, tok])
            sc = own_rows(both) * (SCALE * LOG2E) + bias(g, wp)
            e = jnp.exp2(sc - jnp.max(sc, axis=0, keepdims=True))
            p = (e * (1.0 / jnp.sum(e, axis=0, keepdims=True))).astype(BF)
            act[5 + g, wp * 128:wp * 128 + 64, :] = p[:, 0:256]
            act[5 + g, wp * 128 + 64:wp * 128 + 128, :] = p[:, 256:512]
            pb = by_window(p)
            for h in range(4):
                rows = slice(g * 128 + 32 * h, g * 128 + 32 * h + 32)
                act[7, rows, tok] = dot(s['vt'][rows, tok], pb[:, 128 * h:128 * h + 128]).astype(BF)
        return run

    def middle():
        h = x() + dot_tn(act[7], wo[...])
        n2, r2 = norm(h)
        rst[...] = jnp.where(low_lanes(256), s['r1'], r2)
        act[8] = n2.astype(BF)
        second = (n2 * gn[2:3] + gn[3:4]).astype(BF)
        act[9] = second
        s['second'] = second
        s['y'] = h

    def mlp(j):
        def run():
            a, slope = gelu_pair(dot(s['second'], wu[:, j * 256:(j + 1) * 256]))
            a = a.astype(BF)
            act[10 + j] = a
            act[14 + j] = slope.astype(BF)
            s['y'] = s['y'] + dot(a, wd[j * 256:(j + 1) * 256, :])
            if j == 3:
                done(s['y'])
        return run

    return [start] + [attention(g, wp) for g in range(2) for wp in range(2)] + [middle] + [mlp(j) for j in range(4)]


def colsum(a):
    return jnp.sum(a.reshape(32, 8, 256), axis=0)


def b_parts(dout, wq, wo, wu, wd, gn, act, rst, gv, gb, gw, done):
    s = {}

    def start():
        s['dout'] = dout()
        s['db'] = s['dout'].astype(BF)
        s['dbt'] = s['db'].T
        s['st'] = act[9].T
        s['ds'] = None

    def mlp(j):
        def run():
            c = slice(j * 256, (j + 1) * 256)
            da = dot_nt(s['db'], wd[c, :])
            dpre = (da * act[14 + j].astype(F32)).astype(BF)
            ds = dot_nt(dpre, wu[:, c])
            s['ds'] = ds if s['ds'] is None else s['ds'] + ds
            gw(4 + j)[...] += dot(s['dbt'], act[10 + j])
            gw(j)[...] += dot(s['st'], dpre)
        return run

    def middle():
        ds = s['ds']
        n2 = act[8].astype(F32)
        gv[2] += colsum(ds * n2)
        gv[3] += colsum(ds)
        s['dh'] = s['dout'] + norm_back(ds * gn[2:3], n2, rst[...][:, 64:65])
        db2 = s['dh'].astype(BF)
        s['dat'] = dot_nt(wo[...], db2).astype(BF)
        s['da'] = s['dat'].T
        s['q'] = act[2].T
        gw(11)[...] += dot(act[7], db2)
        s['kt'] = act[3].T
        s['gb'] = [None, None]
        s['dq'], s['dk'], s['dv'] = {}, {}, {}

    def attention(g, wp):
        def run():
            ch = slice(g * 128, (g + 1) * 128)
            tok = slice(wp * 128, (wp + 1) * 128)
            dp = own_rows(dot(head_rows(act[4, tok, ch]), s['dat'][ch, tok]))
            p = jnp.concatenate(
                [act[5 + g, wp * 128:wp * 128 + 64, :], act[5 + g, wp * 128 + 64:wp * 128 + 128, :]], axis=1)
            pf = p.astype(F32)
            t = dp * pf
            dsc = t - pf * jnp.sum(t, axis=0, keepdims=True)
            s['gb'][g] = dsc if s['gb'][g] is None else s['gb'][g] + dsc
            sb = by_window((dsc * SCALE).astype(BF))
            s['dv'][g, wp] = own_heads(dot(stacked(by_window(p)), s['da'][tok, ch])).astype(BF)
            s['dk'][g, wp] = own_heads(dot(stacked(sb), s['q'][tok, ch])).astype(BF)
            for h in range(4):
                rows = slice(g * 128 + 32 * h, g * 128 + 32 * h + 32)
                s['dq'][g, h, wp] = dot(s['kt'][rows, tok], sb[:, 128 * h:128 * h + 128]).astype(BF)
        return run

    def finish():
        for g in range(2):
            gb[:, g * 512:(g + 1) * 512] += s['gb'][g]
        cat = jnp.concatenate
        dqt = cat([cat([s['dq'][g, h, wp] for wp in range(2)], axis=1) for g in range(2) for h in range(4)], axis=0)
        dq = dqt.T
        dk = cat([cat([s['dk'][g, wp] for g in range(2)], axis=1) for wp in range(2)], axis=0)
        dv = cat([cat([s['dv'][g, wp] for g in range(2)], axis=1) for wp in range(2)], axis=0)
        dn = dot_nt(dq, wq[:, 0:256]) + dot_nt(dk, wq[:, 256:512]) + dot_nt(dv, wq[:, 512:768])
        nt = act[1].T
        gw(8)[...] += dot(nt, dq)
        gw(9)[...] += dot(nt, dk)
        gw(10)[...] += dot(nt, dv)
        n1 = act[0].astype(F32)
        gv[0] += colsum(dn * n1)
        gv[1] += colsum(dn)
        done(s['dh'] + norm_back(dn * gn[0:1], n1, rst[...][:, 0:1]))

    return ([start] + [mlp(j) for j in range(4)] + [middle]
            + [attention(g, wp) for g in range(2) for wp in range(2)] + [finish])


MESH = pl.DeviceIdType.MESH
SECTIONS = 4


def local_copy(src, dst, sem):
    return pltpu.make_async_copy(src, dst, sem)


def to_windows(rows):
    return rows.reshape(8, 4, 8, rows.shape[-1]).transpose(1, 0, 2, 3)


def to_rows(tiles):
    return tiles.transpose(1, 0, 2, 3).reshape(256, tiles.shape[-1])


def turn(tiles):
    flat = tiles.reshape(32, 8, 256)
    return jnp.concatenate([flat[:, 4:8], flat[:, 0:4]], axis=1).reshape(4, 8, 8, 256)


def shift_out(tiles):
    turned = turn(tiles)
    nxt = jnp.concatenate([turned[1:], turned[:1]], axis=0)
    low_half = lax.broadcasted_iota(jnp.int32, (1, 1, 8, 256), 2) < 4
    return jnp.where(low_half, turned, nxt)


def shift_back(tiles):
    turned = turn(tiles)
    prev = jnp.concatenate([turned[3:], turned[:3]], axis=0)
    low_half = lax.broadcasted_iota(jnp.int32, (1, 1, 8, 256), 2) < 4
    return jnp.where(low_half, prev, turned)


def toward_shifted(buf, par, pos):
    own = buf[par, pos, :, 32:64, :].reshape(4, 4, 8, 256)
    other = buf[par, 3 - pos, :, 0:32, :].reshape(4, 4, 8, 256)
    return shift_out(jnp.concatenate([own, other], axis=1)).reshape(256, 256)


def toward_plain(buf, par, pos):
    other = buf[par, 3 - pos, :, 32:64, :].reshape(4, 4, 8, 256)
    own = buf[par, pos, :, 0:32, :].reshape(4, 4, 8, 256)
    return shift_back(jnp.concatenate([other, own], axis=1)).reshape(256, 256)


F_FIRST = [((), 0), ((), 1)]
F_MAIN = [((0,), 2), ((1,), 3), ((2, 3), 4), ((4,), 5), ((5,), 6), ((6, 7), 7), ((8, 9), 8)]
F_LAST = [((), 9)]
B_FIRST = [((), 0), ((), 1)]
B_MLP = [((0,), 2), ((1, 2), 3), ((3,), 4), ((4,), 5)]
B_MAIN = [((5,), 6), ((6, 7), 7), ((8, 9), 8), ((10,), 9)]
B_LAST = [((), 10)]


def ordered(plan, p0, p1, p2):
    for mine, both in plan:
        p1[both]()
        p2[both]()
        for i in mine:
            p0[i]()


def ring(n, fn, start=0):
    def body(k, c):
        fn(k)
        return c
    lax.fori_loop(start, n, body, 0)


def fill_bias(rel, pick, line, bt):
    lo = low_lanes(8)
    key = lax.broadcasted_iota(jnp.int32, (64, 128), 0)
    lane = lax.broadcasted_iota(jnp.int32, (64, 128), 1)
    apart_rows = key // 32 != (lane % 64) // 32
    apart_cols = jnp.logical_and((key % 8) // 4 != (lane % 8) // 4, lane >= 64)
    for blk in range(2):
        raw = dot(rel[blk], pick[...]) * LOG2E
        for n in range(32):
            tile = raw[:, 128 * n:128 * n + 128]
            other = pltpu.roll(tile, 64, 1)
            line[16 * n:16 * n + 8, :] = jnp.where(lo, tile, other)
            line[16 * n + 8:16 * n + 16, :] = jnp.where(lo, other, tile)
        for h in range(8):
            cols = slice(128 * h, 128 * h + 128)
            plain = line[pl.ds(h, 64, stride=8), :]
            if blk == 0:
                bt[0, :, cols] = plain
            else:
                cut = plain - 100.0 * LOG2E
                bt[1, :, cols] = plain
                bt[2, :, cols] = jnp.where(apart_cols, cut, plain)
                bt[3, :, cols] = jnp.where(apart_rows, cut, plain)
                bt[4, :, cols] = jnp.where(jnp.logical_or(apart_rows, apart_cols), cut, plain)


def table_grad(gb, pick, line):
    for h in range(8):
        a = gb[:, 128 * h:128 * h + 128]
        line[pl.ds(h, 64, stride=8), :] = a + pltpu.roll(a, 64, 1)
    lo = low_lanes(8)
    row = jnp.concatenate(
        [jnp.where(lo, line[16 * n:16 * n + 8, :], line[16 * n + 8:16 * n + 16, :]) for n in range(32)], axis=1)
    high = row.astype(BF)
    rest = (row - high.astype(F32)).astype(BF)
    return dot_nt(high, pick[...]) + dot_nt(rest, pick[...])


def sizes(batch):
    unit = 16 * SECTIONS * (batch // 2)
    ra = -(-3072 // (2 * unit)) * 2 * unit
    rb = -(-(3072 + 64) // (2 * unit)) * 2 * unit
    units = rb // 2 // unit
    c = units * 3 // 7
    return ra, rb, (ra // 2, (units - c) * unit, c * unit)


class Reduction:
    def __init__(self, base, half, g1, g2, core, partner, grads, gathered, bufs, sems):
        self.n1, self.me1, self.dev1 = g1
        self.n2, self.me2, self.dev2 = g2
        self.p1 = half // self.n1
        self.p2 = self.p1 // self.n2
        self.mine = base + core * half
        self.theirs = base + (1 - core) * half
        self.partner, self.grads, self.gathered = partner, grads, gathered
        self.o1, self.i1, self.o2, self.i2, self.o3, self.i3, self.t = bufs
        (self.s1, self.r1, self.s2, self.r2, self.s3, self.r3, self.sg2, self.rg2, self.sg1, self.rg1, self.sc, self.rc) = sems

    def rows1(self, start, i1):
        return pl.ds(pl.multiple_of(start + i1 * self.p1, 16), self.p1)

    def piece(self, start, i1, i2):
        return self.gathered.at[pl.ds(pl.multiple_of(start + i1 * self.p1 + i2 * self.p2, 16), self.p2)]

    def send(self, src, dst, ssem, rsem, device):
        return pltpu.make_async_remote_copy(
            src_ref=src, dst_ref=dst, send_sem=ssem, recv_sem=rsem, device_id=device, device_id_type=MESH)

    def landed(self, ref, sem):
        pltpu.make_async_copy(ref, ref, sem).wait()

    def others1(self, fn):
        ring(self.n1, lambda k: fn(lax.rem(self.me1 + k, self.n1)), 1)

    def others2(self, fn):
        ring(self.n2, lambda k: fn(lax.rem(self.me2 + k, self.n2)), 1)

    def to_partner(self, i):
        return self.send(self.o1.at[i], self.i1.at[i], self.s1.at[i], self.r1.at[i], self.partner)

    def scatter1(self, i):
        return self.send(self.o2.at[i], self.i2.at[self.me1], self.s2.at[i], self.r2.at[self.me1], self.dev1(i))

    def scatter2(self, i):
        return self.send(self.o3.at[i], self.i3.at[self.me2], self.s3.at[i], self.r3.at[self.me2], self.dev2(i))

    def gather2(self, i):
        here = self.piece(self.mine, self.me1, self.me2)
        return self.send(here, here, self.sg2.at[i], self.rg2.at[self.me2], self.dev2(i))

    def gather1(self, i, j2):
        here = self.piece(self.mine, self.me1, j2)
        return self.send(here, here, self.sg1.at[i, j2], self.rg1.at[self.me1, j2], self.dev1(i))

    def share(self, i1, i2):
        here = self.piece(self.mine, i1, i2)
        return self.send(here, here, self.sc.at[i1, i2], self.rc.at[i1, i2], self.partner)

    def swap(self):
        def one(k):
            i = lax.rem(self.me1 + k, self.n1)
            self.o1[i] = self.grads[self.rows1(self.theirs, i), :].astype(BF)
            self.to_partner(i).start()
        ring(self.n1 + 1, one, 1)

    def summed(self, i):
        self.landed(self.i1.at[i], self.r1.at[i])
        return self.grads[self.rows1(self.mine, i), :] + self.i1[i].astype(F32)

    def stage1(self):
        def one(i):
            self.o2[i] = self.summed(i).astype(BF)
            self.scatter1(i).start()
        self.others1(one)
        self.t[...] = self.summed(self.me1)

    def stage2(self):
        def add(j):
            self.landed(self.i2.at[j], self.r2.at[j])
            self.t[...] += self.i2[j].astype(F32)
        self.others1(add)

        def one(i):
            self.o3[i] = self.t[self.slice2(i), :].astype(BF)
            self.scatter2(i).start()
        self.others2(one)

    def slice2(self, i):
        return pl.ds(pl.multiple_of(i * self.p2, 16), self.p2)

    def pass_on(self, j2):
        self.others1(lambda i: self.gather1(i, j2).start())
        self.share(self.me1, j2).start()

    def stage3(self):
        here = self.slice2(self.me2)

        def add(j):
            self.landed(self.i3.at[j], self.r3.at[j])
            self.t[here, :] += self.i3[j].astype(F32)
        self.others2(add)
        self.piece(self.mine, self.me1, self.me2)[...] = self.t[here, :].astype(BF)
        self.others2(lambda i: self.gather2(i).start())
        self.pass_on(self.me2)

    def stage4(self):
        def one(j):
            self.landed(self.piece(self.mine, self.me1, j), self.rg2.at[j])
            self.pass_on(j)
        self.others2(one)

    def stage5(self):
        def one(j1):
            def two(j2):
                self.landed(self.piece(self.mine, j1, j2), self.rg1.at[j1, j2])
                self.share(j1, j2).start()
            ring(self.n2, two)
        self.others1(one)

    def stage6(self):
        ring(self.n1, lambda i: ring(self.n2, lambda j: self.landed(self.piece(self.theirs, i, j), self.rc.at[i, j])))

    def drain(self):
        ring(self.n1, lambda i: self.to_partner(i).wait_send())
        self.others1(lambda i: self.scatter1(i).wait_send())
        self.others2(lambda i: self.scatter2(i).wait_send())
        self.others2(lambda i: self.gather2(i).wait_send())
        self.others1(lambda i: ring(self.n2, lambda j: self.gather1(i, j).wait_send()))
        ring(self.n1, lambda i: ring(self.n2, lambda j: self.share(i, j).wait_send()))


def rollout_kernel(
    size, lengths, emb, hid, cot, wq_far, wo_far, wu_far, wd_far, wl, ga, sa, gm, sm, rel, pick_far,
    y_home, fg_home, lg_home, sums, act_far,
    emb_in, cot_in, hid_in, lg_st, cot_mk, xs, dxs, xin, act, rst, gb, gv, gl, gn, bt, line,
    grads, gathered, wq, wo, wu, wd, pick,
    emb_ss, emb_rs, hid_ss, hid_rs, cot_ss, cot_rs,
    y_ss, y_rs, fg_ss, fg_rs, lg_ss, lg_rs, xf_ss, xf_rs, xb_ss, xb_rs, act_os, act_is, cot_ls, out_ss, w_ls, *reduction,
):
    sec = lax.axis_index("section")
    bat = lax.axis_index("batch")
    core = lax.rem(bat, 2)
    first = bat - core
    partner = first + 1 - core
    rows_a, rows_b, halves = sizes(size)

    barrier = pltpu.get_barrier_semaphore()
    for ds in range(SECTIONS):
        for dc in range(2):
            if ds == 0 and dc == 0:
                continue
            pl.semaphore_signal(
                barrier, inc=1,
                device_id={"section": lax.rem(sec + ds, SECTIONS), "batch": first + lax.rem(core + dc, 2)},
                device_id_type=MESH)

    def greet(k):
        pl.semaphore_signal(
            barrier, inc=1, device_id={"section": sec, "batch": lax.rem(bat + 2 * k, size)}, device_id_type=MESH)

    ring(size // 2, greet, 1)
    pl.semaphore_wait(barrier, 2 * SECTIONS - 1 + size // 2 - 1)

    def route(pos, t):
        if pos == 0:
            to_sec, to_bat = 2 * core + t // 2, first + t % 2
            return to_sec, to_bat, 4 + t // 2, t % 2, jnp.logical_and(to_sec == sec, core == t % 2)
        return jnp.int32(t), bat, t, pos - 1, sec == t

    def deliver(src, dst, ssem, rsem, to_sec, to_bat, mine, begin):
        @pl.when(mine)
        def _():
            if begin:
                local_copy(src, dst, rsem).start()

        @pl.when(jnp.logical_not(mine))
        def _():
            rc = pltpu.make_async_remote_copy(
                src_ref=src, dst_ref=dst, send_sem=ssem, recv_sem=rsem,
                device_id={"section": to_sec, "batch": to_bat}, device_id_type=MESH)
            if begin:
                rc.start()
            else:
                rc.wait_send()

    def spread_tiles(begin):
        for pos in (1, 2, 0):
            for t in range(4):
                to_sec, to_bat, item, part, mine = route(pos, t)
                deliver(emb.at[item, part], emb_in.at[sec, pos], emb_ss.at[pos, t], emb_rs.at[sec, pos],
                        to_sec, to_bat, mine, begin)
                deliver(hid.at[item, :, pl.ds(256 * part, 256)], hid_in.at[sec, pos], hid_ss.at[pos, t],
                        hid_rs.at[sec, pos], to_sec, to_bat, mine, begin)

    def spread_cotangents(begin):
        for pos in (1, 2, 0):
            for t in range(4):
                to_sec, to_bat, item, part, mine = route(pos, t)
                for u in range(2):
                    deliver(cot_mk.at[item, (2 * part + 1 + u) % 4], cot_in.at[sec, pos, u], cot_ss.at[pos, t, u],
                            cot_rs.at[sec, pos, u], to_sec, to_bat, mine, begin)

    def home(step, pos):
        half = pos == 0
        item = jnp.where(half, 4 + lax.rem(sec, 2), sec)
        part = jnp.where(half, core, pos - 1)
        to_bat = jnp.where(half, first + sec // 2, bat)
        slot = jnp.where(half, lax.rem(sec, 2) * 2 + core, sec)
        return item, part, to_bat, slot, jnp.logical_and(step == sec, to_bat == bat)

    def return_y(step, pos, begin):
        item, part, to_bat, slot, mine = home(step, pos)
        for u in range(2):
            deliver(emb_in.at[step, pos, u], y_home.at[item, lax.rem(2 * part + 1 + u, 4)], y_ss.at[step, pos, u],
                    y_rs.at[pos, slot, u], step, to_bat, mine, begin)

    def return_grads(step, pos, begin):
        item, part, to_bat, slot, mine = home(step, pos)
        deliver(cot_in.at[step, pos], fg_home.at[item, part], fg_ss.at[step, pos], fg_rs.at[pos, slot],
                step, to_bat, mine, begin)
        deliver(lg_st.at[step, pos], lg_home.at[item, :, pl.ds(pl.multiple_of(256 * part, 256), 256)],
                lg_ss.at[step, pos], lg_rs.at[pos, slot], step, to_bat, mine, begin)

    def exchange(buf, par, off, ssem, rsem, n):
        return pltpu.make_async_remote_copy(
            src_ref=buf.at[par, 0, :, pl.ds(off, 32), :],
            dst_ref=buf.at[par, 3, :, pl.ds(off, 32), :],
            send_sem=ssem.at[n], recv_sem=rsem.at[n],
            device_id={"section": sec, "batch": partner}, device_id_type=MESH)

    xy = (SECTIONS, sec, lambda i: {"section": i, "batch": bat})
    zs = (size // 2, bat // 2, lambda i: {"section": sec, "batch": 2 * i + core})
    bases = (0, rows_a, rows_a + 2 * halves[1])
    jobs = []
    for k, half in enumerate(halves):
        if half:
            g1, g2 = (zs, xy) if k == 2 else (xy, zs)
            jobs.append(Reduction(bases[k], half, g1, g2, core, {"section": sec, "batch": partner}, grads, gathered,
                                  reduction[19 * k:19 * k + 7], reduction[19 * k + 7:19 * k + 19]))
    early = jobs[0]

    spread_tiles(True)
    loads = [local_copy(far, near, w_ls.at[i]) for i, (far, near) in enumerate(
        ((pick_far, pick), (wq_far, wq), (wo_far, wo), (wu_far, wu), (wd_far, wd)))]
    for load in loads:
        load.start()
    local_copy(cot, cot_mk, cot_ls).start()
    xs[1] = jnp.zeros((4, 4, 64, 256), F32)
    dxs[1] = jnp.zeros((4, 4, 64, 256), F32)
    loads[0].wait()
    for i, ref in enumerate((ga, sa, gm, sm)):
        for blk in range(2):
            gn[blk, i:i + 1, :] = ref[blk:blk + 1, :].astype(F32)
    fill_bias(rel, pick, line, bt)
    for ref in (gb, gv, gl):
        ref[...] = jnp.zeros(ref.shape, F32)

    def clear(t):
        grads[pl.ds(pl.multiple_of(64 * t, 64), 64), :] = jnp.zeros((64, 256), F32)

    ring((rows_a + rows_b) // 64, clear)
    for load in loads[1:]:
        load.wait()

    def act_out(ph, pos):
        return local_copy(act.at[lax.rem(ph, 2), pos], act_far.at[ph, pos], act_os.at[ph, pos])

    def act_in(ph, pos):
        return local_copy(act_far.at[ph, pos], act.at[lax.rem(ph, 2), pos], act_is.at[ph, pos])

    def keep(ref, pos):
        def run(value):
            ref[pos] = value
        return run

    def forward_phase(ph):
        step = ph // 2
        blk = lax.rem(ph, 2)
        par = lax.rem(ph, 2)
        old = 1 - par

        def build(pos):
            @pl.when(blk == 0)
            def _():
                local_copy(emb.at[0, 0], emb_in.at[step, pos], emb_rs.at[step, pos]).wait()
                local_copy(hid.at[0, :, pl.ds(0, 256)], hid_in.at[step, pos], hid_rs.at[step, pos]).wait()
                lifted = emb_in[step, pos].reshape(256, 256).astype(F32) + dot_tn(hid_in[step, pos], wl[...])
                carried = toward_plain(xs, old, pos).astype(BF).astype(F32)
                xin[pos] = to_windows(lifted).reshape(256, 256) + carried

            @pl.when(blk == 1)
            def _():
                xin[pos] = toward_shifted(xs, old, pos)

        def parts(pos):
            bottom = core if pos == 0 else pos - 1

            def bias(g, wp):
                return bt[jnp.where(blk == 0, 0, 1 + 2 * bottom + wp), :, g * 512:(g + 1) * 512]

            return f_parts(lambda: xin[pos], wq.at[blk], wo.at[blk], wu.at[blk], wd.at[blk], gn.at[blk], bias,
                           act.at[lax.rem(ph, 2), pos], rst.at[ph, pos], keep(xin, pos))

        def finish(pos):
            xs[par, pos] = xin[pos].reshape(4, 64, 256)

            @pl.when(blk == 1)
            def _():
                rows = to_rows(shift_back(xs[par, pos].reshape(4, 8, 8, 256))).astype(BF)
                emb_in[step, pos] = rows.reshape(2, 128, 256)
                return_y(step, pos, True)

            @pl.when(ph < 6)
            def _():
                act_out(ph, pos).start()

        p0, p1, p2 = parts(0), parts(1), parts(2)

        @pl.when(ph >= 2)
        def _():
            for pos in range(3):
                act_out(ph - 2, pos).wait()

        build(1)
        build(2)
        ordered(F_FIRST, p0, p1, p2)

        @pl.when(ph >= 1)
        def _():
            exchange(xs, old, pl.multiple_of(32 * old, 32), xf_ss, xf_rs, ph - 1).wait_recv()

        build(0)
        ordered(F_MAIN, p0, p1, p2)

        @pl.when(ph >= 2)
        def _():
            exchange(xs, par, pl.multiple_of(32 * par, 32), xf_ss, xf_rs, ph - 2).wait_send()

        finish(0)

        @pl.when(ph < 7)
        def _():
            exchange(xs, par, pl.multiple_of(32 * par, 32), xf_ss, xf_rs, ph).start()

        @pl.when(ph == 4 - sec)
        def _():
            local_copy(cot, cot_mk, cot_ls).wait()
            for i in range(6):
                on = jnp.where(sec < lengths[i], 1.0, 0.0)
                for u in range(4):
                    cot_mk[i, u] = (cot_mk[i, u].astype(F32) * on).astype(BF)
            spread_cotangents(True)

        ordered(F_LAST, p0, p1, p2)
        finish(1)
        finish(2)

    ring(8, forward_phase)
    exchange(xs, 0, 0, xf_ss, xf_rs, 6).wait_send()

    def backward_phase(bph):
        ph = 7 - bph
        step = ph // 2
        blk = lax.rem(ph, 2)
        par = lax.rem(bph, 2)
        old = 1 - par

        def build(pos):
            @pl.when(blk == 1)
            def _():
                for u in range(2):
                    local_copy(cot_mk.at[0, 0], cot_in.at[step, pos, u], cot_rs.at[step, pos, u]).wait()
                rows = cot_in[step, pos].reshape(256, 256).astype(F32)
                xin[pos] = shift_out(to_windows(rows)).reshape(256, 256) + toward_shifted(dxs, old, pos)

            @pl.when(blk == 0)
            def _():
                xin[pos] = toward_plain(dxs, old, pos)

            @pl.when(ph < 6)
            def _():
                act_in(ph, pos).wait()

        def gw(t):
            return grads.at[pl.ds(pl.multiple_of(rows_a * (1 - blk) + 256 * t, 256), 256)]

        def parts(pos):
            return b_parts(lambda: xin[pos], wq.at[blk], wo.at[blk], wu.at[blk], wd.at[blk], gn.at[blk],
                           act.at[lax.rem(ph, 2), pos], rst.at[ph, pos], gv.at[blk], gb.at[blk], gw, keep(xin, pos))

        def finish(pos):
            @pl.when(ph >= 2)
            def _():
                act_in(ph - 2, pos).start()

            @pl.when(blk == 1)
            def _():
                dxs[par, pos] = xin[pos].reshape(4, 64, 256)

            @pl.when(blk == 0)
            def _():
                db = xin[pos].astype(BF).astype(F32)
                dxs[par, pos] = db.reshape(4, 64, 256)
                rows = to_rows(db.reshape(4, 8, 8, 256)).astype(BF)
                cot_in[step, pos] = rows.reshape(2, 128, 256)
                lg_st[step, pos] = dot_nt(wl[...], rows).astype(BF)
                gl[...] += dot(hid_in[step, pos], rows)
                return_grads(step, pos, True)

        p0, p1, p2 = parts(0), parts(1), parts(2)

        @pl.when(bph == 7)
        def _():
            early.swap()

        build(1)
        build(2)
        ordered(B_FIRST, p0, p1, p2)

        @pl.when(bph >= 1)
        def _():
            exchange(dxs, old, pl.multiple_of(32 * par, 32), xb_ss, xb_rs, bph - 1).wait_recv()

        build(0)

        @pl.when(bph == 7)
        def _():
            early.stage1()

        ordered(B_MLP + B_MAIN, p0, p1, p2)

        @pl.when(bph >= 2)
        def _():
            exchange(dxs, par, pl.multiple_of(32 * old, 32), xb_ss, xb_rs, bph - 2).wait_send()

        finish(0)

        @pl.when(bph < 7)
        def _():
            exchange(dxs, par, pl.multiple_of(32 * old, 32), xb_ss, xb_rs, bph).start()

        ordered(B_LAST, p0, p1, p2)
        finish(1)
        finish(2)

    ring(8, backward_phase)
    exchange(dxs, 0, 32, xb_ss, xb_rs, 6).wait_send()

    small = rows_a + 3072
    grads[small:small + 8, :] = jnp.concatenate(
        [jnp.sum(gv[blk, i], axis=0, keepdims=True) for blk in range(2) for i in range(4)], axis=0)
    grads[small + 8:small + 40, :] = gl[...]
    for blk in range(2):
        grads[small + 40 + 8 * blk:small + 48 + 8 * blk, 0:225] = table_grad(gb.at[blk], pick, line)

    ends = jobs[2:]
    middle = jobs[1]

    def publish(lo, hi):
        copy = local_copy(gathered.at[pl.ds(lo, hi - lo)], sums.at[pl.ds(lo, hi - lo)], out_ss.at[len(copies)])
        copy.start()
        copies.append(copy)

    copies = []
    late = ends + [middle]
    for job in late:
        job.swap()
    early.stage2()
    for job in late:
        job.stage1()
    early.stage3()
    for job in late:
        job.stage2()
    early.stage4()
    for job in late:
        job.stage3()
    early.stage5()
    for job in late:
        job.stage4()
    early.stage6()
    publish(0, rows_a)
    for job in late:
        job.stage5()
    for job in late:
        job.stage6()
    publish(rows_a, rows_a + rows_b)

    spread_tiles(False)
    spread_cotangents(False)

    def leave(i):
        return_y(i // 3, lax.rem(i, 3), False)
        return_grads(i // 3, lax.rem(i, 3), False)

    ring(3 * SECTIONS, leave)
    for pos in range(3):
        for t in range(4):
            item, part = (4 + t // 2, t % 2) if pos == 0 else (t, pos - 1)
            for u in range(2):
                local_copy(emb_in.at[0, 0, 0], y_home.at[item, (2 * part + 1 + u) % 4], y_rs.at[pos, t, u]).wait()
            local_copy(cot_in.at[0, 0], fg_home.at[item, part], fg_rs.at[pos, t]).wait()
            local_copy(lg_st.at[0, 0], lg_home.at[item, :, pl.ds(256 * part, 256)], lg_rs.at[pos, t]).wait()
    for job in jobs:
        job.drain()
    for copy in copies:
        copy.wait()


def rollout(size, *operands):
    vm = pl.BlockSpec(memory_space=pltpu.VMEM)
    far = pl.BlockSpec(memory_space=pl.ANY)
    S = jax.ShapeDtypeStruct
    dma = pltpu.SemaphoreType.DMA
    rows_a, rows_b, halves = sizes(size)
    reduction = []
    for k, half in enumerate(halves):
        n1, n2 = (size // 2, SECTIONS) if k == 2 else (SECTIONS, size // 2)
        p1 = max(half // n1, 16)
        p2 = max(p1 // n2, 16)
        reduction += [pltpu.VMEM((n1, p1, 256), BF)] * 4 + [pltpu.VMEM((n2, p2, 256), BF)] * 2
        reduction += [pltpu.VMEM((p1, 256), F32)]
        reduction += [dma((n1,))] * 4 + [dma((n2,))] * 4 + [dma((n1, n2))] * 4
    return pl.pallas_call(
        functools.partial(rollout_kernel, size),
        name="rollout",
        in_specs=[pl.BlockSpec(memory_space=pltpu.SMEM)] + [far] * 7 + [vm] * 6 + [far],
        out_specs=(far,) * 5,
        out_shape=(
            S((6, 4, 128, 256), BF), S((6, 2, 2, 128, 256), BF), S((6, 32, 512), BF),
            S((rows_a + rows_b, 256), BF),
            S((6, 3, 18, 256, 256), BF),
        ),
        scratch_shapes=[
            pltpu.VMEM((4, 3, 2, 128, 256), BF), pltpu.VMEM((4, 3, 2, 128, 256), BF), pltpu.VMEM((4, 3, 32, 256), BF),
            pltpu.VMEM((4, 3, 32, 256), BF),
            pltpu.VMEM((6, 4, 128, 256), BF),
            pltpu.VMEM((2, 4, 4, 64, 256), F32), pltpu.VMEM((2, 4, 4, 64, 256), F32),
            pltpu.VMEM((3, 256, 256), F32),
            pltpu.VMEM((2, 3, 18, 256, 256), BF), pltpu.VMEM((8, 3, 256, 128), F32),
            pltpu.VMEM((2, 64, 1024), F32), pltpu.VMEM((2, 4, 8, 256), F32), pltpu.VMEM((32, 256), F32),
            pltpu.VMEM((2, 4, 256), F32), pltpu.VMEM((5, 64, 1024), F32), pltpu.VMEM((512, 128), F32),
            pltpu.VMEM((rows_a + rows_b, 256), F32), pltpu.VMEM((rows_a + rows_b, 256), BF),
            pltpu.VMEM((2, 256, 768), BF), pltpu.VMEM((2, 256, 256), BF), pltpu.VMEM((2, 256, 1024), BF),
            pltpu.VMEM((2, 1024, 256), BF), pltpu.VMEM((225, 4096), BF),
            dma((3, 4)), dma((4, 3)), dma((3, 4)), dma((4, 3)), dma((3, 4, 2)), dma((4, 3, 2)),
            dma((4, 3, 2)), dma((3, 4, 2)), dma((4, 3)), dma((3, 4)), dma((4, 3)), dma((3, 4)),
            dma((7,)), dma((7,)), dma((7,)), dma((7,)), dma((6, 3)), dma((6, 3)), dma, dma((2,)), dma((5,)),
        ] + reduction,
        compiler_params=pltpu.CompilerParams(collective_id=0, has_side_effects=True, vmem_limit_bytes=61 * 2**20),
        cost_estimate=pl.CostEstimate(flops=60 * 10**9, bytes_accessed=100 * 10**6, transcendentals=0),
    )(*operands)


def finish_kernel(rows_a, lengths, y, fg, lg, sums, y_out, fg_out, lg_out, gq, go, gu, gd, g_ga, g_sa, g_gm, g_sm, g_rel, g_lat,
                  y_in, fg_in, lg_in, near, wide, y_is, y_os, n_is, w_os, f_is, f_os):
    sec = lax.axis_index("section")
    small = rows_a + 3072
    groups = [(0, 1024), (1024, 2048), (2048, 3072), (rows_a, rows_a + 1024), (rows_a + 1024, rows_a + 2048), (rows_a + 2048, rows_a + 3072),
              (small, small + 64)]
    reads = [local_copy(sums.at[pl.ds(lo, hi - lo)], near.at[pl.ds(lo, hi - lo)], n_is.at[i]) for i, (lo, hi) in enumerate(groups)]
    items = [local_copy(y.at[i], y_in.at[i], y_is.at[i]) for i in range(6)]
    passed = [local_copy(fg.at[i], fg_in.at[i], f_is.at[i]) for i in range(6)] + [local_copy(lg, lg_in, f_is.at[6])]
    for copy in reads + items + passed:
        copy.start()
    writes = []

    def write(src, dst, sem):
        copy = local_copy(src, dst, sem)
        copy.start()
        writes.append(copy)

    for i, read in enumerate(reads[:6]):
        read.wait()
        blk, kind = 1 - i // 3, i % 3
        for j in range(4):
            t = 4 * i + j
            lo = groups[i][0] + 256 * j
            value = near[lo:lo + 256, :].astype(F32)
            wide[t] = value.T if kind == 1 else value
            cols = pl.ds(256 * j, 256)
            dst = (gu.at[blk, :, cols], gd.at[blk, cols, :], gq.at[blk, :, cols] if j < 3 else go.at[blk])[kind]
            write(wide.at[t], dst, w_os.at[t])
    for i in range(6):
        items[i].wait()
        on = jnp.where(sec < lengths[i], 1.0, 0.0)
        y_in[i] = (y_in[i].astype(F32) * on).astype(BF)
        write(y_in.at[i], y_out.at[i], y_os.at[i])
    for i in range(6):
        passed[i].wait()
        write(fg_in.at[i], fg_out.at[i], f_os.at[i])
    passed[6].wait()
    write(lg_in, lg_out, f_os.at[6])
    reads[6].wait()
    tail = near[small:small + 64, :].astype(F32)
    for i, ref in enumerate((g_ga, g_sa, g_gm, g_sm)):
        for blk in range(2):
            ref[blk:blk + 1, :] = tail[4 * blk + i:4 * blk + i + 1]
    g_lat[...] = tail[8:40]
    for blk in range(2):
        g_rel[blk] = tail[40 + 8 * blk:48 + 8 * blk, 0:225]
    for copy in writes:
        copy.wait()


def finish(size, lengths, y, fg, lg, sums):
    vm = pl.BlockSpec(memory_space=pltpu.VMEM)
    far = pl.BlockSpec(memory_space=pl.ANY)
    S = jax.ShapeDtypeStruct
    dma = pltpu.SemaphoreType.DMA
    rows_a, rows_b, _ = sizes(size)
    return pl.pallas_call(
        functools.partial(finish_kernel, rows_a),
        name="finish",
        in_specs=[pl.BlockSpec(memory_space=pltpu.SMEM)] + [far] * 4,
        out_specs=(far,) * 7 + (vm,) * 6,
        out_shape=(
            S((6, 512, 256), BF), S((6, 512, 256), BF), S((6, 32, 512), BF),
            S((2, 256, 768), F32), S((2, 256, 256), F32), S((2, 256, 1024), F32), S((2, 1024, 256), F32),
            S((2, 256), F32), S((2, 256), F32), S((2, 256), F32), S((2, 256), F32),
            S((2, 8, 225), F32), S((32, 256), F32),
        ),
        scratch_shapes=[
            pltpu.VMEM((6, 512, 256), BF), pltpu.VMEM((6, 512, 256), BF), pltpu.VMEM((6, 32, 512), BF),
            pltpu.VMEM((rows_a + rows_b, 256), BF), pltpu.VMEM((24, 256, 256), F32),
            dma((6,)), dma((6,)), dma((7,)), dma((24,)), dma((7,)), dma((7,)),
        ],
        compiler_params=pltpu.CompilerParams(vmem_limit_bytes=61 * 2**20),
        cost_estimate=pl.CostEstimate(flops=0, bytes_accessed=16 * 10**6, transcendentals=0),
    )(lengths, y.reshape(6, 512, 256), fg.reshape(6, 512, 256), lg, sums)


def picker():
    row = np.repeat(np.arange(8), 8)
    col = np.tile(np.arange(8), 8)
    index = (row[None, :] - row[:, None] + 7) * 15 + col[None, :] - col[:, None] + 7
    return (np.arange(225)[:, None] == index.reshape(1, -1)).astype(np.float32)


def on_device(
    embedded_tiles, hidden_sample, cotangent, lengths, gain_attn, shift_attn, w_qkv, rel_table, w_out,
    gain_mlp, shift_mlp, w_up, w_down, w_latent,
):
    size = lax.axis_size("batch")
    y, fg, lg, sums, _ = rollout(
        size, lengths, embedded_tiles.reshape(6, 2, 2, 128, 256),
        hidden_sample[0].transpose(0, 2, 1), cotangent.reshape(6, 4, 128, 256),
        w_qkv, w_out, w_up, w_down, w_latent, gain_attn, shift_attn, gain_mlp, shift_mlp,
        rel_table.transpose(0, 2, 1), jnp.asarray(picker(), BF))
    y, fg, lg, gq, go, gu, gd, g_ga, g_sa, g_gm, g_sm, g_rel, g_lat = finish(size, lengths, y, fg, lg, sums)
    return (
        y[None], fg[None], lg.transpose(0, 2, 1)[None],
        g_ga, g_sa, gq, g_rel.transpose(0, 2, 1), go, g_gm, g_sm, gu, gd, g_lat,
    )


def solution(mesh):
    data = P("section", "batch", None, None)
    return jax.shard_map(
        on_device,
        mesh=mesh,
        in_specs=(data, data, data, P("batch")) + (P(),) * 10,
        out_specs=(data, data, data) + (P(),) * 10,
        check_vma=False,
    )
```

```python
import functools

import jax
import jax.numpy as jnp
import numpy as np
from jax import lax
from jax.experimental import pallas as pl
from jax.experimental.pallas import tpu as pltpu
from jax.sharding import PartitionSpec as P

BF = jnp.bfloat16
F32 = jnp.float32
LOG2E = 1.4426950408889634
SCALE = 32**-0.5


def dot(a, b):
    return lax.dot_general(a, b, (((1,), (0,)), ((), ())), preferred_element_type=F32)


def dot_nt(a, b):
    return lax.dot_general(a, b, (((1,), (1,)), ((), ())), preferred_element_type=F32)


def dot_tn(a, b):
    return lax.dot_general(a, b, (((0,), (0,)), ((), ())), preferred_element_type=F32)


PHI = (0.7978695563668204, 0.0363928095591428, -8.82196615782389e-05, -3.6600001215273455e-05, 1.418529678284452e-06)


def gelu_pair(z):
    square = z * z
    poly = PHI[4]
    for c in PHI[3::-1]:
        poly = poly * square + c
    phi = 0.5 + 0.5 * jnp.tanh(z * poly)
    density = jnp.exp2(square * (-0.5 * LOG2E)) * 0.3989422804014327
    return z * phi, phi + z * density


def norm(x):
    centered = x - jnp.mean(x, axis=-1, keepdims=True)
    r = lax.rsqrt(jnp.mean(centered * centered, axis=-1, keepdims=True) + 1e-5)
    return centered * r, r


def norm_back(dn, n, r):
    m1 = jnp.mean(dn, axis=-1, keepdims=True)
    m2 = jnp.mean(dn * n, axis=-1, keepdims=True)
    return r * (dn - m1 - n * m2)


def low_lanes(rows):
    return lax.broadcasted_iota(jnp.int32, (rows, 128), 1) < 64


def head_rows(t):
    lane = lax.broadcasted_iota(jnp.int32, (1, 128), 1)
    return jnp.concatenate([t * jnp.where(lane // 32 == h, 1.0, 0.0).astype(BF) for h in range(4)], axis=0)


def own_rows(both):
    lo = low_lanes(64)
    return jnp.concatenate(
        [jnp.where(lo, both[128 * h:128 * h + 64], both[128 * h + 64:128 * h + 128]) for h in range(4)], axis=1)


def own_heads(rows):
    lane = lax.broadcasted_iota(jnp.int32, (128, 128), 1)
    return jnp.where(lane < 64, jnp.where(lane < 32, rows[0:128], rows[128:256]), jnp.where(lane < 96, rows[256:384], rows[384:512]))


def stacked(p):
    return jnp.concatenate([p[:, 128 * h:128 * h + 128] for h in range(4)], axis=0)


def by_window(p):
    lane = lax.broadcasted_iota(jnp.int32, (1, 512), 1)
    lo = jnp.where(lane % 128 < 64, 1.0, 0.0).astype(BF)
    hi = jnp.where(lane % 128 < 64, 0.0, 1.0).astype(BF)
    return jnp.concatenate([p * lo, p * hi], axis=0)


def f_parts(x, wq, wo, wu, wd, gn, bias, act, rst, done):
    s = {}

    def start():
        xv = x()
        n1, r1 = norm(xv)
        s['r1'] = r1
        act[0] = n1.astype(BF)
        normed = (n1 * gn[0:1] + gn[1:2]).astype(BF)
        act[1] = normed
        qkv = dot(normed, wq[...]).astype(BF)
        s['q'], s['k'], s['v'] = qkv[:, 0:256], qkv[:, 256:512], qkv[:, 512:768]
        act[3] = s['k']
        act[4] = s['v']
        s['qt'] = s['q'].T
        act[2] = s['qt']
        s['vt'] = s['v'].T

    def attention(g, wp):
        def run():
            ch = slice(g * 128, (g + 1) * 128)
            tok = slice(wp * 128, (wp + 1) * 128)
            both = dot(head_rows(s['k'][tok, ch]), s['qt'][ch, tok])
            sc = own_rows(both) * (SCALE * LOG2E) + bias(g, wp)
            e = jnp.exp2(sc - jnp.max(sc, axis=0, keepdims=True))
            p = (e * (1.0 / jnp.sum(e, axis=0, keepdims=True))).astype(BF)
            act[5 + g, wp * 128:wp * 128 + 64, :] = p[:, 0:256]
            act[5 + g, wp * 128 + 64:wp * 128 + 128, :] = p[:, 256:512]
            pb = by_window(p)
            for h in range(4):
                rows = slice(g * 128 + 32 * h, g * 128 + 32 * h + 32)
                act[7, rows, tok] = dot(s['vt'][rows, tok], pb[:, 128 * h:128 * h + 128]).astype(BF)
        return run

    def middle():
        h = x() + dot_tn(act[7], wo[...])
        n2, r2 = norm(h)
        rst[...] = jnp.where(low_lanes(256), s['r1'], r2)
        act[8] = n2.astype(BF)
        second = (n2 * gn[2:3] + gn[3:4]).astype(BF)
        act[9] = second
        s['second'] = second
        s['y'] = h

    def mlp(j):
        def run():
            a, slope = gelu_pair(dot(s['second'], wu[:, j * 256:(j + 1) * 256]))
            a = a.astype(BF)
            act[10 + j] = a
            act[14 + j] = slope.astype(BF)
            s['y'] = s['y'] + dot(a, wd[j * 256:(j + 1) * 256, :])
            if j == 3:
                done(s['y'])
        return run

    return [start] + [attention(g, wp) for g in range(2) for wp in range(2)] + [middle] + [mlp(j) for j in range(4)]


def colsum(a):
    return jnp.sum(a.reshape(32, 8, 256), axis=0)


def b_parts(dout, wq, wo, wu, wd, gn, act, rst, gv, gb, gw, done):
    s = {}

    def start():
        s['dout'] = dout()
        s['db'] = s['dout'].astype(BF)
        s['dbt'] = s['db'].T
        s['st'] = act[9].T
        s['ds'] = None

    def mlp(j):
        def run():
            c = slice(j * 256, (j + 1) * 256)
            da = dot_nt(s['db'], wd[c, :])
            dpre = (da * act[14 + j].astype(F32)).astype(BF)
            ds = dot_nt(dpre, wu[:, c])
            s['ds'] = ds if s['ds'] is None else s['ds'] + ds
            gw(4 + j)[...] += dot(s['dbt'], act[10 + j])
            gw(j)[...] += dot(s['st'], dpre)
        return run

    def middle():
        ds = s['ds']
        n2 = act[8].astype(F32)
        gv[2] += colsum(ds * n2)
        gv[3] += colsum(ds)
        s['dh'] = s['dout'] + norm_back(ds * gn[2:3], n2, rst[...][:, 64:65])
        db2 = s['dh'].astype(BF)
        s['dat'] = dot_nt(wo[...], db2).astype(BF)
        s['da'] = s['dat'].T
        s['q'] = act[2].T
        gw(11)[...] += dot(act[7], db2)
        s['kt'] = act[3].T
        s['gb'] = [None, None]
        s['dq'], s['dk'], s['dv'] = {}, {}, {}

    def attention(g, wp):
        def run():
            ch = slice(g * 128, (g + 1) * 128)
            tok = slice(wp * 128, (wp + 1) * 128)
            dp = own_rows(dot(head_rows(act[4, tok, ch]), s['dat'][ch, tok]))
            p = jnp.concatenate(
                [act[5 + g, wp * 128:wp * 128 + 64, :], act[5 + g, wp * 128 + 64:wp * 128 + 128, :]], axis=1)
            pf = p.astype(F32)
            t = dp * pf
            dsc = t - pf * jnp.sum(t, axis=0, keepdims=True)
            s['gb'][g] = dsc if s['gb'][g] is None else s['gb'][g] + dsc
            sb = by_window((dsc * SCALE).astype(BF))
            s['dv'][g, wp] = own_heads(dot(stacked(by_window(p)), s['da'][tok, ch])).astype(BF)
            s['dk'][g, wp] = own_heads(dot(stacked(sb), s['q'][tok, ch])).astype(BF)
            for h in range(4):
                rows = slice(g * 128 + 32 * h, g * 128 + 32 * h + 32)
                s['dq'][g, h, wp] = dot(s['kt'][rows, tok], sb[:, 128 * h:128 * h + 128]).astype(BF)
        return run

    def finish():
        for g in range(2):
            gb[:, g * 512:(g + 1) * 512] += s['gb'][g]
        cat = jnp.concatenate
        dqt = cat([cat([s['dq'][g, h, wp] for wp in range(2)], axis=1) for g in range(2) for h in range(4)], axis=0)
        dq = dqt.T
        dk = cat([cat([s['dk'][g, wp] for g in range(2)], axis=1) for wp in range(2)], axis=0)
        dv = cat([cat([s['dv'][g, wp] for g in range(2)], axis=1) for wp in range(2)], axis=0)
        dn = dot_nt(dq, wq[:, 0:256]) + dot_nt(dk, wq[:, 256:512]) + dot_nt(dv, wq[:, 512:768])
        nt = act[1].T
        gw(8)[...] += dot(nt, dq)
        gw(9)[...] += dot(nt, dk)
        gw(10)[...] += dot(nt, dv)
        n1 = act[0].astype(F32)
        gv[0] += colsum(dn * n1)
        gv[1] += colsum(dn)
        done(s['dh'] + norm_back(dn * gn[0:1], n1, rst[...][:, 0:1]))

    return ([start] + [mlp(j) for j in range(4)] + [middle]
            + [attention(g, wp) for g in range(2) for wp in range(2)] + [finish])


MESH = pl.DeviceIdType.MESH
SECTIONS = 4


def local_copy(src, dst, sem):
    return pltpu.make_async_copy(src, dst, sem)


def to_windows(rows):
    return rows.reshape(8, 4, 8, rows.shape[-1]).transpose(1, 0, 2, 3)


def to_rows(tiles):
    return tiles.transpose(1, 0, 2, 3).reshape(256, tiles.shape[-1])


def turn(tiles):
    flat = tiles.reshape(32, 8, 256)
    return jnp.concatenate([flat[:, 4:8], flat[:, 0:4]], axis=1).reshape(4, 8, 8, 256)


def shift_out(tiles):
    turned = turn(tiles)
    nxt = jnp.concatenate([turned[1:], turned[:1]], axis=0)
    low_half = lax.broadcasted_iota(jnp.int32, (1, 1, 8, 256), 2) < 4
    return jnp.where(low_half, turned, nxt)


def shift_back(tiles):
    turned = turn(tiles)
    prev = jnp.concatenate([turned[3:], turned[:3]], axis=0)
    low_half = lax.broadcasted_iota(jnp.int32, (1, 1, 8, 256), 2) < 4
    return jnp.where(low_half, prev, turned)


def toward_shifted(buf, par, pos):
    own = buf[par, pos, :, 32:64, :].reshape(4, 4, 8, 256)
    other = buf[par, 3 - pos, :, 0:32, :].reshape(4, 4, 8, 256)
    return shift_out(jnp.concatenate([own, other], axis=1)).reshape(256, 256)


def toward_plain(buf, par, pos):
    other = buf[par, 3 - pos, :, 32:64, :].reshape(4, 4, 8, 256)
    own = buf[par, pos, :, 0:32, :].reshape(4, 4, 8, 256)
    return shift_back(jnp.concatenate([other, own], axis=1)).reshape(256, 256)


F_FIRST = []
F_MAIN = [((0,), 0), ((1,), 1), ((2,), 2), ((3,), 3), ((4,), 4), ((5,), 5), ((6,), 6), ((7, 8), 7), ((9,), 8)]
F_LAST = [((), 9)]
B_FIRST = []
B_MLP = []
B_MAIN = [((0,), 0), ((1,), 1), ((2,), 2), ((3,), 3), ((4,), 4), ((5,), 5), ((6,), 6), ((7,), 7), ((8, 9), 8), ((10,), 9)]
B_LAST = [((), 10)]


def ordered(plan, p0, p1, p2):
    for mine, both in plan:
        p1[both]()
        p2[both]()
        for i in mine:
            p0[i]()


def ring(n, fn, start=0):
    def body(k, c):
        fn(k)
        return c
    lax.fori_loop(start, n, body, 0)


def fill_bias(rel, pick, line, bt):
    lo = low_lanes(8)
    key = lax.broadcasted_iota(jnp.int32, (64, 128), 0)
    lane = lax.broadcasted_iota(jnp.int32, (64, 128), 1)
    apart_rows = key // 32 != (lane % 64) // 32
    apart_cols = jnp.logical_and((key % 8) // 4 != (lane % 8) // 4, lane >= 64)
    for blk in range(2):
        raw = dot(rel[blk], pick[...]) * LOG2E
        for n in range(32):
            tile = raw[:, 128 * n:128 * n + 128]
            other = pltpu.roll(tile, 64, 1)
            line[16 * n:16 * n + 8, :] = jnp.where(lo, tile, other)
            line[16 * n + 8:16 * n + 16, :] = jnp.where(lo, other, tile)
        for h in range(8):
            cols = slice(128 * h, 128 * h + 128)
            plain = line[pl.ds(h, 64, stride=8), :]
            if blk == 0:
                bt[0, :, cols] = plain
            else:
                cut = plain - 100.0 * LOG2E
                bt[1, :, cols] = plain
                bt[2, :, cols] = jnp.where(apart_cols, cut, plain)
                bt[3, :, cols] = jnp.where(apart_rows, cut, plain)
                bt[4, :, cols] = jnp.where(jnp.logical_or(apart_rows, apart_cols), cut, plain)


def table_grad(gb, pick, line):
    for h in range(8):
        a = gb[:, 128 * h:128 * h + 128]
        line[pl.ds(h, 64, stride=8), :] = a + pltpu.roll(a, 64, 1)
    lo = low_lanes(8)
    row = jnp.concatenate(
        [jnp.where(lo, line[16 * n:16 * n + 8, :], line[16 * n + 8:16 * n + 16, :]) for n in range(32)], axis=1)
    high = row.astype(BF)
    rest = (row - high.astype(F32)).astype(BF)
    return dot_nt(high, pick[...]) + dot_nt(rest, pick[...])


def sizes(batch):
    unit = 16 * SECTIONS * (batch // 2)
    ra = -(-3072 // (2 * unit)) * 2 * unit
    rb = -(-(3072 + 64) // (2 * unit)) * 2 * unit
    units = rb // 2 // unit
    c = units * 3 // 7
    return ra, rb, (ra // 2, (units - c) * unit, c * unit)


class Reduction:
    def __init__(self, base, half, g1, g2, square, core, partner, grads, gathered, bufs, sems):
        self.square = square
        self.n1, self.me1, self.dev1 = g1
        self.n2, self.me2, self.dev2 = g2
        self.p1 = half // self.n1
        self.p2 = self.p1 // self.n2
        self.mine = base + core * half
        self.theirs = base + (1 - core) * half
        self.partner, self.grads, self.gathered = partner, grads, gathered
        self.o1, self.i1, self.o2, self.i2, self.o3, self.i3, self.t = bufs
        (self.s1, self.r1, self.s2, self.r2, self.s3, self.r3, self.sg2, self.rg2, self.sg1, self.rg1, self.sc, self.rc) = sems

    def rows1(self, start, i1):
        return pl.ds(pl.multiple_of(start + i1 * self.p1, 16), self.p1)

    def piece(self, start, i1, i2):
        return self.gathered.at[pl.ds(pl.multiple_of(start + i1 * self.p1 + i2 * self.p2, 16), self.p2)]

    def send(self, src, dst, ssem, rsem, device):
        return pltpu.make_async_remote_copy(
            src_ref=src, dst_ref=dst, send_sem=ssem, recv_sem=rsem, device_id=device, device_id_type=MESH)

    def landed(self, ref, sem):
        pltpu.make_async_copy(ref, ref, sem).wait()

    def others1(self, fn):
        ring(self.n1, lambda k: fn(lax.rem(self.me1 + k, self.n1)), 1)

    def others2(self, fn):
        ring(self.n2, lambda k: fn(lax.rem(self.me2 + k, self.n2)), 1)

    def to_partner(self, i):
        return self.send(self.o1.at[i], self.i1.at[i], self.s1.at[i], self.r1.at[i], self.partner)

    def scatter1(self, i):
        return self.send(self.o2.at[i], self.i2.at[self.me1], self.s2.at[i], self.r2.at[self.me1], self.dev1(i))

    def scatter2(self, i):
        return self.send(self.o3.at[i], self.i3.at[self.me2], self.s3.at[i], self.r3.at[self.me2], self.dev2(i))

    def gather2(self, i):
        here = self.piece(self.mine, self.me1, self.me2)
        return self.send(here, here, self.sg2.at[i], self.rg2.at[self.me2], self.dev2(i))

    def gather1(self, i, j2):
        here = self.piece(self.mine, self.me1, j2)
        return self.send(here, here, self.sg1.at[i, j2], self.rg1.at[self.me1, j2], self.dev1(i))

    def share(self, i1, i2):
        here = self.piece(self.mine, i1, i2)
        return self.send(here, here, self.sc.at[i1, i2], self.rc.at[i1, i2], self.partner)

    def swap(self):
        def one(k):
            i = lax.rem(self.me1 + k, self.n1)
            self.o1[i] = self.grads[self.rows1(self.theirs, i), :].astype(BF)
            self.to_partner(i).start()
        ring(self.n1 + 1, one, 1)

    def summed(self, i):
        self.landed(self.i1.at[i], self.r1.at[i])
        return self.grads[self.rows1(self.mine, i), :] + self.i1[i].astype(F32)

    def stage1(self):
        def one(i):
            self.o2[i] = self.summed(i).astype(BF)
            self.scatter1(i).start()
        self.others1(one)
        self.t[...] = self.summed(self.me1)

    def stage2(self):
        def add(j):
            self.landed(self.i2.at[j], self.r2.at[j])
            self.t[...] += self.i2[j].astype(F32)
        self.others1(add)

        def one(i):
            self.o3[i] = self.t[self.slice2(i), :].astype(BF)
            self.scatter2(i).start()
        self.others2(one)

    def slice2(self, i):
        return pl.ds(pl.multiple_of(i * self.p2, 16), self.p2)

    def beside(self):
        x, y = lax.rem(self.me1, 2), self.me1 // 2
        return self.me1 + 1 - 2 * x, self.me1 + 2 - 4 * y

    def forward(self, j2):
        nx, ny = self.beside()
        odd = lax.rem(j2, 2)
        origin, target = jnp.where(odd == 1, ny, nx), jnp.where(odd == 1, nx, ny)
        here = self.piece(self.mine, origin, j2)
        return self.send(here, here, self.sg1.at[3 - self.me1, j2], self.rg1.at[origin, j2], self.dev1(target))

    def pass_on(self, j2):
        if self.square:
            for i in self.beside():
                self.gather1(i, j2).start()
        else:
            self.others1(lambda i: self.gather1(i, j2).start())
        self.share(self.me1, j2).start()

    def stage3(self):
        here = self.slice2(self.me2)

        def add(j):
            self.landed(self.i3.at[j], self.r3.at[j])
            self.t[here, :] += self.i3[j].astype(F32)
        self.others2(add)
        self.piece(self.mine, self.me1, self.me2)[...] = self.t[here, :].astype(BF)
        self.others2(lambda i: self.gather2(i).start())
        self.pass_on(self.me2)

    def stage4(self):
        def one(j):
            self.landed(self.piece(self.mine, self.me1, j), self.rg2.at[j])
            self.pass_on(j)
        self.others2(one)

    def stage5(self):
        def arrive(j1, j2):
            self.landed(self.piece(self.mine, j1, j2), self.rg1.at[j1, j2])
            self.share(j1, j2).start()

        if not self.square:
            self.others1(lambda j1: ring(self.n2, lambda j2: arrive(j1, j2)))
            return
        nx, ny = self.beside()

        def sides(j2):
            arrive(nx, j2)
            arrive(ny, j2)
            self.forward(j2).start()

        ring(self.n2, sides)
        ring(self.n2, lambda j2: arrive(3 - self.me1, j2))

    def stage6(self):
        ring(self.n1, lambda i: ring(self.n2, lambda j: self.landed(self.piece(self.theirs, i, j), self.rc.at[i, j])))

    def drain(self):
        ring(self.n1, lambda i: self.to_partner(i).wait_send())
        self.others1(lambda i: self.scatter1(i).wait_send())
        self.others2(lambda i: self.scatter2(i).wait_send())
        self.others2(lambda i: self.gather2(i).wait_send())
        if self.square:
            for i in self.beside():
                ring(self.n2, lambda j: self.gather1(i, j).wait_send())
            ring(self.n2, lambda j: self.forward(j).wait_send())
        else:
            self.others1(lambda i: ring(self.n2, lambda j: self.gather1(i, j).wait_send()))
        ring(self.n1, lambda i: ring(self.n2, lambda j: self.share(i, j).wait_send()))


LATE = "C0 B0 A2 C1 B1 A3 C2 B2 A4 C3 B3 A5 C4 B4 A6 C5 B5 C6 B6".split()


def rollout_kernel(
    size, lengths, emb, hid, cot, wq_far, wo_far, wu_far, wd_far, wl, ga, sa, gm, sm, rel, pick_far,
    y_home, fg_home, lg_home, sums, act_far,
    emb_in, cot_in, hid_in, lg_st, cot_mk, xs, dxs, xin, act, rst, gb, gv, gl, gn, bt, line,
    grads, gathered, wq, wo, wu, wd, pick,
    emb_ss, emb_rs, hid_ss, hid_rs, cot_ss, cot_rs,
    y_ss, y_rs, fg_ss, fg_rs, lg_ss, lg_rs, xf_ss, xf_rs, xb_ss, xb_rs, act_os, act_is, cot_ls, out_ss, w_ls, *reduction,
):
    sec = lax.axis_index("section")
    bat = lax.axis_index("batch")
    core = lax.rem(bat, 2)
    first = bat - core
    partner = first + 1 - core
    rows_a, rows_b, halves = sizes(size)

    barrier = pltpu.get_barrier_semaphore()
    for ds in range(SECTIONS):
        for dc in range(2):
            if ds == 0 and dc == 0:
                continue
            pl.semaphore_signal(
                barrier, inc=1,
                device_id={"section": lax.rem(sec + ds, SECTIONS), "batch": first + lax.rem(core + dc, 2)},
                device_id_type=MESH)

    def greet(k):
        pl.semaphore_signal(
            barrier, inc=1, device_id={"section": sec, "batch": lax.rem(bat + 2 * k, size)}, device_id_type=MESH)

    ring(size // 2, greet, 1)
    pl.semaphore_wait(barrier, 2 * SECTIONS - 1 + size // 2 - 1)

    def route(pos, t):
        if pos == 0:
            to_sec, to_bat = 2 * core + t // 2, first + t % 2
            return to_sec, to_bat, 4 + t // 2, t % 2, jnp.logical_and(to_sec == sec, core == t % 2)
        return jnp.int32(t), bat, t, pos - 1, sec == t

    def deliver(src, dst, ssem, rsem, to_sec, to_bat, mine, begin):
        @pl.when(mine)
        def _():
            if begin:
                local_copy(src, dst, rsem).start()

        @pl.when(jnp.logical_not(mine))
        def _():
            rc = pltpu.make_async_remote_copy(
                src_ref=src, dst_ref=dst, send_sem=ssem, recv_sem=rsem,
                device_id={"section": to_sec, "batch": to_bat}, device_id_type=MESH)
            if begin:
                rc.start()
            else:
                rc.wait_send()

    def spread_tiles(begin):
        for pos in (1, 2, 0):
            for t in range(4):
                to_sec, to_bat, item, part, mine = route(pos, t)
                deliver(emb.at[item, part], emb_in.at[sec, pos], emb_ss.at[pos, t], emb_rs.at[sec, pos],
                        to_sec, to_bat, mine, begin)
                deliver(hid.at[item, :, pl.ds(256 * part, 256)], hid_in.at[sec, pos], hid_ss.at[pos, t],
                        hid_rs.at[sec, pos], to_sec, to_bat, mine, begin)

    def spread_cotangents(begin):
        for pos in (1, 2, 0):
            for t in range(4):
                to_sec, to_bat, item, part, mine = route(pos, t)
                for u in range(2):
                    deliver(cot_mk.at[item, (2 * part + 1 + u) % 4], cot_in.at[sec, pos, u], cot_ss.at[pos, t, u],
                            cot_rs.at[sec, pos, u], to_sec, to_bat, mine, begin)

    def home(step, pos):
        half = pos == 0
        item = jnp.where(half, 4 + lax.rem(sec, 2), sec)
        part = jnp.where(half, core, pos - 1)
        to_bat = jnp.where(half, first + sec // 2, bat)
        slot = jnp.where(half, lax.rem(sec, 2) * 2 + core, sec)
        return item, part, to_bat, slot, jnp.logical_and(step == sec, to_bat == bat)

    def return_y(step, pos, begin):
        item, part, to_bat, slot, mine = home(step, pos)
        for u in range(2):
            deliver(emb_in.at[step, pos, u], y_home.at[item, lax.rem(2 * part + 1 + u, 4)], y_ss.at[step, pos, u],
                    y_rs.at[pos, slot, u], step, to_bat, mine, begin)

    def return_grads(step, pos, begin):
        item, part, to_bat, slot, mine = home(step, pos)
        deliver(cot_in.at[step, pos], fg_home.at[item, part], fg_ss.at[step, pos], fg_rs.at[pos, slot],
                step, to_bat, mine, begin)
        deliver(lg_st.at[step, pos], lg_home.at[item, :, pl.ds(pl.multiple_of(256 * part, 256), 256)],
                lg_ss.at[step, pos], lg_rs.at[pos, slot], step, to_bat, mine, begin)

    def exchange(buf, par, off, ssem, rsem, n):
        return pltpu.make_async_remote_copy(
            src_ref=buf.at[par, 0, :, pl.ds(off, 32), :],
            dst_ref=buf.at[par, 3, :, pl.ds(off, 32), :],
            send_sem=ssem.at[n], recv_sem=rsem.at[n],
            device_id={"section": sec, "batch": partner}, device_id_type=MESH)

    xy = (SECTIONS, sec, lambda i: {"section": i, "batch": bat})
    zs = (size // 2, bat // 2, lambda i: {"section": sec, "batch": 2 * i + core})
    bases = (0, rows_a, rows_a + 2 * halves[1])
    jobs = []
    for k, half in enumerate(halves):
        if half:
            g1, g2 = (zs, xy) if k == 2 else (xy, zs)
            jobs.append(Reduction(bases[k], half, g1, g2, k < 2, core, {"section": sec, "batch": partner}, grads, gathered,
                                  reduction[19 * k:19 * k + 7], reduction[19 * k + 7:19 * k + 19]))
    early = jobs[0]

    spread_tiles(True)
    loads = [local_copy(far, near, w_ls.at[i]) for i, (far, near) in enumerate(
        ((pick_far, pick), (wq_far, wq), (wo_far, wo), (wu_far, wu), (wd_far, wd)))]
    for load in loads:
        load.start()
    local_copy(cot, cot_mk, cot_ls).start()
    xs[1] = jnp.zeros((4, 4, 64, 256), F32)
    dxs[1] = jnp.zeros((4, 4, 64, 256), F32)
    loads[0].wait()
    for i, ref in enumerate((ga, sa, gm, sm)):
        for blk in range(2):
            gn[blk, i:i + 1, :] = ref[blk:blk + 1, :].astype(F32)
    fill_bias(rel, pick, line, bt)
    for ref in (gb, gv, gl):
        ref[...] = jnp.zeros(ref.shape, F32)

    def clear(t):
        grads[pl.ds(pl.multiple_of(64 * t, 64), 64), :] = jnp.zeros((64, 256), F32)

    ring((rows_a + rows_b) // 64, clear)
    for load in loads[1:]:
        load.wait()

    def act_out(ph, pos):
        return local_copy(act.at[lax.rem(ph, 2), pos], act_far.at[ph, pos], act_os.at[ph, pos])

    def act_in(ph, pos):
        return local_copy(act_far.at[ph, pos], act.at[lax.rem(ph, 2), pos], act_is.at[ph, pos])

    def forward_phase(ph):
        step = ph // 2
        blk = lax.rem(ph, 2)
        par = lax.rem(ph, 2)
        old = 1 - par

        def build(pos):
            @pl.when(blk == 0)
            def _():
                local_copy(emb.at[0, 0], emb_in.at[step, pos], emb_rs.at[step, pos]).wait()
                local_copy(hid.at[0, :, pl.ds(0, 256)], hid_in.at[step, pos], hid_rs.at[step, pos]).wait()
                lifted = emb_in[step, pos].reshape(256, 256).astype(F32) + dot_tn(hid_in[step, pos], wl[...])
                carried = toward_plain(xs, old, pos).astype(BF).astype(F32)
                xin[pos] = to_windows(lifted).reshape(256, 256) + carried

            @pl.when(blk == 1)
            def _():
                xin[pos] = toward_shifted(xs, old, pos)

        def parts(pos):
            bottom = core if pos == 0 else pos - 1

            def done(value):
                xs[par, pos] = value.reshape(4, 64, 256)

            def bias(g, wp):
                return bt[jnp.where(blk == 0, 0, 1 + 2 * bottom + wp), :, g * 512:(g + 1) * 512]

            return f_parts(lambda: xin[pos], wq.at[blk], wo.at[blk], wu.at[blk], wd.at[blk], gn.at[blk], bias,
                           act.at[lax.rem(ph, 2), pos], rst.at[ph, pos], done)

        def finish(pos):
            @pl.when(blk == 1)
            def _():
                rows = to_rows(shift_back(xs[par, pos].reshape(4, 8, 8, 256))).astype(BF)
                emb_in[step, pos] = rows.reshape(2, 128, 256)
                return_y(step, pos, True)

            @pl.when(ph < 6)
            def _():
                act_out(ph, pos).start()

        p0, p1, p2 = parts(0), parts(1), parts(2)

        @pl.when(ph >= 2)
        def _():
            for pos in range(3):
                act_out(ph - 2, pos).wait()

        build(1)
        build(2)
        @pl.when(ph >= 2)
        def _():
            exchange(xs, par, pl.multiple_of(32 * par, 32), xf_ss, xf_rs, ph - 2).wait_send()

        ordered(F_FIRST, p0, p1, p2)

        @pl.when(ph >= 1)
        def _():
            exchange(xs, old, pl.multiple_of(32 * old, 32), xf_ss, xf_rs, ph - 1).wait_recv()

        build(0)
        ordered(F_MAIN, p0, p1, p2)

        finish(0)

        @pl.when(ph < 7)
        def _():
            exchange(xs, par, pl.multiple_of(32 * par, 32), xf_ss, xf_rs, ph).start()

        @pl.when(ph == 4 - sec)
        def _():
            local_copy(cot, cot_mk, cot_ls).wait()
            for i in range(6):
                on = jnp.where(sec < lengths[i], 1.0, 0.0)
                for u in range(4):
                    cot_mk[i, u] = (cot_mk[i, u].astype(F32) * on).astype(BF)
            spread_cotangents(True)

        ordered(F_LAST, p0, p1, p2)
        finish(1)
        finish(2)

    ring(8, forward_phase)
    exchange(xs, 0, 0, xf_ss, xf_rs, 6).wait_send()

    def backward_phase(bph):
        ph = 7 - bph
        step = ph // 2
        blk = lax.rem(ph, 2)
        par = lax.rem(bph, 2)
        old = 1 - par

        def build(pos):
            @pl.when(blk == 1)
            def _():
                for u in range(2):
                    local_copy(cot_mk.at[0, 0], cot_in.at[step, pos, u], cot_rs.at[step, pos, u]).wait()
                rows = cot_in[step, pos].reshape(256, 256).astype(F32)
                xin[pos] = shift_out(to_windows(rows)).reshape(256, 256) + toward_shifted(dxs, old, pos)

            @pl.when(blk == 0)
            def _():
                xin[pos] = toward_plain(dxs, old, pos)

            @pl.when(ph < 6)
            def _():
                act_in(ph, pos).wait()

        def gw(t):
            return grads.at[pl.ds(pl.multiple_of(rows_a * (1 - blk) + 256 * t, 256), 256)]

        def parts(pos):
            def done(value):
                dxs[par, pos] = jnp.where(blk == 0, value.astype(BF).astype(F32), value).reshape(4, 64, 256)

            return b_parts(lambda: xin[pos], wq.at[blk], wo.at[blk], wu.at[blk], wd.at[blk], gn.at[blk],
                           act.at[lax.rem(ph, 2), pos], rst.at[ph, pos], gv.at[blk], gb.at[blk], gw, done)

        def finish(pos):
            @pl.when(ph >= 2)
            def _():
                act_in(ph - 2, pos).start()

            @pl.when(blk == 0)
            def _():
                rows = to_rows(dxs[par, pos].reshape(4, 8, 8, 256)).astype(BF)
                cot_in[step, pos] = rows.reshape(2, 128, 256)
                lg_st[step, pos] = dot_nt(wl[...], rows).astype(BF)
                gl[...] += dot(hid_in[step, pos], rows)
                return_grads(step, pos, True)

        p0, p1, p2 = parts(0), parts(1), parts(2)

        @pl.when(bph == 7)
        def _():
            early.swap()

        build(1)
        build(2)
        @pl.when(bph >= 2)
        def _():
            exchange(dxs, par, pl.multiple_of(32 * old, 32), xb_ss, xb_rs, bph - 2).wait_send()

        ordered(B_FIRST, p0, p1, p2)

        @pl.when(bph >= 1)
        def _():
            exchange(dxs, old, pl.multiple_of(32 * par, 32), xb_ss, xb_rs, bph - 1).wait_recv()

        build(0)

        @pl.when(bph == 7)
        def _():
            early.stage1()

        ordered(B_MLP + B_MAIN, p0, p1, p2)

        finish(0)

        @pl.when(bph < 7)
        def _():
            exchange(dxs, par, pl.multiple_of(32 * old, 32), xb_ss, xb_rs, bph).start()

        ordered(B_LAST, p0, p1, p2)
        finish(1)
        finish(2)

    ring(8, backward_phase)
    exchange(dxs, 0, 32, xb_ss, xb_rs, 6).wait_send()

    small = rows_a + 3072
    grads[small:small + 8, :] = jnp.concatenate(
        [jnp.sum(gv[blk, i], axis=0, keepdims=True) for blk in range(2) for i in range(4)], axis=0)
    grads[small + 8:small + 40, :] = gl[...]
    for blk in range(2):
        grads[small + 40 + 8 * blk:small + 48 + 8 * blk, 0:225] = table_grad(gb.at[blk], pick, line)


    def publish(lo, hi):
        copy = local_copy(gathered.at[pl.ds(lo, hi - lo)], sums.at[pl.ds(lo, hi - lo)], out_ss.at[len(copies)])
        copy.start()
        copies.append(copy)

    copies = []
    by_name = dict(zip("ABC", jobs))
    for entry in LATE:
        if entry[0] not in by_name:
            continue
        job = by_name[entry[0]]
        (job.swap, job.stage1, job.stage2, job.stage3, job.stage4, job.stage5, job.stage6)[int(entry[1])]()
        if entry == "A6":
            publish(0, rows_a)
    publish(rows_a, rows_a + rows_b)

    spread_tiles(False)
    spread_cotangents(False)

    def leave(i):
        return_y(i // 3, lax.rem(i, 3), False)
        return_grads(i // 3, lax.rem(i, 3), False)

    ring(3 * SECTIONS, leave)
    for pos in range(3):
        for t in range(4):
            item, part = (4 + t // 2, t % 2) if pos == 0 else (t, pos - 1)
            for u in range(2):
                local_copy(emb_in.at[0, 0, 0], y_home.at[item, (2 * part + 1 + u) % 4], y_rs.at[pos, t, u]).wait()
            local_copy(cot_in.at[0, 0], fg_home.at[item, part], fg_rs.at[pos, t]).wait()
            local_copy(lg_st.at[0, 0], lg_home.at[item, :, pl.ds(256 * part, 256)], lg_rs.at[pos, t]).wait()
    for job in jobs:
        job.drain()
    for copy in copies:
        copy.wait()


def rollout(size, *operands):
    vm = pl.BlockSpec(memory_space=pltpu.VMEM)
    far = pl.BlockSpec(memory_space=pl.ANY)
    S = jax.ShapeDtypeStruct
    dma = pltpu.SemaphoreType.DMA
    rows_a, rows_b, halves = sizes(size)
    reduction = []
    for k, half in enumerate(halves):
        n1, n2 = (size // 2, SECTIONS) if k == 2 else (SECTIONS, size // 2)
        p1 = max(half // n1, 16)
        p2 = max(p1 // n2, 16)
        reduction += [pltpu.VMEM((n1, p1, 256), BF)] * 4 + [pltpu.VMEM((n2, p2, 256), BF)] * 2
        reduction += [pltpu.VMEM((p1, 256), F32)]
        reduction += [dma((n1,))] * 4 + [dma((n2,))] * 4 + [dma((n1, n2))] * 4
    return pl.pallas_call(
        functools.partial(rollout_kernel, size),
        name="rollout",
        in_specs=[pl.BlockSpec(memory_space=pltpu.SMEM)] + [far] * 7 + [vm] * 6 + [far],
        out_specs=(far,) * 5,
        out_shape=(
            S((6, 4, 128, 256), BF), S((6, 2, 2, 128, 256), BF), S((6, 32, 512), BF),
            S((rows_a + rows_b, 256), BF),
            S((6, 3, 18, 256, 256), BF),
        ),
        scratch_shapes=[
            pltpu.VMEM((4, 3, 2, 128, 256), BF), pltpu.VMEM((4, 3, 2, 128, 256), BF), pltpu.VMEM((4, 3, 32, 256), BF),
            pltpu.VMEM((4, 3, 32, 256), BF),
            pltpu.VMEM((6, 4, 128, 256), BF),
            pltpu.VMEM((2, 4, 4, 64, 256), F32), pltpu.VMEM((2, 4, 4, 64, 256), F32),
            pltpu.VMEM((3, 256, 256), F32),
            pltpu.VMEM((2, 3, 18, 256, 256), BF), pltpu.VMEM((8, 3, 256, 128), F32),
            pltpu.VMEM((2, 64, 1024), F32), pltpu.VMEM((2, 4, 8, 256), F32), pltpu.VMEM((32, 256), F32),
            pltpu.VMEM((2, 4, 256), F32), pltpu.VMEM((5, 64, 1024), F32), pltpu.VMEM((512, 128), F32),
            pltpu.VMEM((rows_a + rows_b, 256), F32), pltpu.VMEM((rows_a + rows_b, 256), BF),
            pltpu.VMEM((2, 256, 768), BF), pltpu.VMEM((2, 256, 256), BF), pltpu.VMEM((2, 256, 1024), BF),
            pltpu.VMEM((2, 1024, 256), BF), pltpu.VMEM((225, 4096), BF),
            dma((3, 4)), dma((4, 3)), dma((3, 4)), dma((4, 3)), dma((3, 4, 2)), dma((4, 3, 2)),
            dma((4, 3, 2)), dma((3, 4, 2)), dma((4, 3)), dma((3, 4)), dma((4, 3)), dma((3, 4)),
            dma((7,)), dma((7,)), dma((7,)), dma((7,)), dma((6, 3)), dma((6, 3)), dma, dma((2,)), dma((5,)),
        ] + reduction,
        compiler_params=pltpu.CompilerParams(collective_id=0, has_side_effects=True, vmem_limit_bytes=61 * 2**20),
        cost_estimate=pl.CostEstimate(flops=60 * 10**9, bytes_accessed=100 * 10**6, transcendentals=0),
    )(*operands)


def finish_kernel(rows_a, lengths, y, fg, lg, sums, y_out, fg_out, lg_out, gq, go, gu, gd, g_ga, g_sa, g_gm, g_sm, g_rel, g_lat,
                  y_in, fg_in, lg_in, near, wide, y_is, y_os, n_is, w_os, f_is, f_os):
    sec = lax.axis_index("section")
    small = rows_a + 3072
    groups = [(0, 1024), (1024, 2048), (2048, 3072), (rows_a, rows_a + 1024), (rows_a + 1024, rows_a + 2048), (rows_a + 2048, rows_a + 3072),
              (small, small + 64)]
    reads = [local_copy(sums.at[pl.ds(lo, hi - lo)], near.at[pl.ds(lo, hi - lo)], n_is.at[i]) for i, (lo, hi) in enumerate(groups)]
    items = [local_copy(y.at[i], y_in.at[i], y_is.at[i]) for i in range(6)]
    passed = [local_copy(fg.at[i], fg_in.at[i], f_is.at[i]) for i in range(6)] + [local_copy(lg, lg_in, f_is.at[6])]
    for i in range(6):
        for copy in (reads[i], passed[i], items[i]):
            copy.start()
    reads[6].start()
    passed[6].start()
    writes = []

    def write(src, dst, sem):
        copy = local_copy(src, dst, sem)
        copy.start()
        writes.append(copy)

    for i, read in enumerate(reads[:6]):
        read.wait()
        blk, kind = 1 - i // 3, i % 3
        for j in range(4):
            t = 4 * i + j
            lo = groups[i][0] + 256 * j
            value = near[lo:lo + 256, :].astype(F32)
            wide[t] = value.T if kind == 1 else value
            cols = pl.ds(256 * j, 256)
            dst = (gu.at[blk, :, cols], gd.at[blk, cols, :], gq.at[blk, :, cols] if j < 3 else go.at[blk])[kind]
            write(wide.at[t], dst, w_os.at[t])
        passed[i].wait()
        write(fg_in.at[i], fg_out.at[i], f_os.at[i])
        items[i].wait()
        on = jnp.where(sec < lengths[i], 1.0, 0.0)
        y_in[i] = (y_in[i].astype(F32) * on).astype(BF)
        write(y_in.at[i], y_out.at[i], y_os.at[i])
    passed[6].wait()
    write(lg_in, lg_out, f_os.at[6])
    reads[6].wait()
    tail = near[small:small + 64, :].astype(F32)
    for i, ref in enumerate((g_ga, g_sa, g_gm, g_sm)):
        for blk in range(2):
            ref[blk:blk + 1, :] = tail[4 * blk + i:4 * blk + i + 1]
    g_lat[...] = tail[8:40]
    for blk in range(2):
        g_rel[blk] = tail[40 + 8 * blk:48 + 8 * blk, 0:225]
    for copy in writes:
        copy.wait()


def finish(size, lengths, y, fg, lg, sums):
    vm = pl.BlockSpec(memory_space=pltpu.VMEM)
    far = pl.BlockSpec(memory_space=pl.ANY)
    S = jax.ShapeDtypeStruct
    dma = pltpu.SemaphoreType.DMA
    rows_a, rows_b, _ = sizes(size)
    return pl.pallas_call(
        functools.partial(finish_kernel, rows_a),
        name="finish",
        in_specs=[pl.BlockSpec(memory_space=pltpu.SMEM)] + [far] * 4,
        out_specs=(far,) * 7 + (vm,) * 6,
        out_shape=(
            S((6, 512, 256), BF), S((6, 512, 256), BF), S((6, 32, 512), BF),
            S((2, 256, 768), F32), S((2, 256, 256), F32), S((2, 256, 1024), F32), S((2, 1024, 256), F32),
            S((2, 256), F32), S((2, 256), F32), S((2, 256), F32), S((2, 256), F32),
            S((2, 8, 225), F32), S((32, 256), F32),
        ),
        scratch_shapes=[
            pltpu.VMEM((6, 512, 256), BF), pltpu.VMEM((6, 512, 256), BF), pltpu.VMEM((6, 32, 512), BF),
            pltpu.VMEM((rows_a + rows_b, 256), BF), pltpu.VMEM((24, 256, 256), F32),
            dma((6,)), dma((6,)), dma((7,)), dma((24,)), dma((7,)), dma((7,)),
        ],
        compiler_params=pltpu.CompilerParams(vmem_limit_bytes=61 * 2**20),
        cost_estimate=pl.CostEstimate(flops=0, bytes_accessed=16 * 10**6, transcendentals=0),
    )(lengths, y.reshape(6, 512, 256), fg.reshape(6, 512, 256), lg, sums)


def picker():
    row = np.repeat(np.arange(8), 8)
    col = np.tile(np.arange(8), 8)
    index = (row[None, :] - row[:, None] + 7) * 15 + col[None, :] - col[:, None] + 7
    return (np.arange(225)[:, None] == index.reshape(1, -1)).astype(np.float32)


def on_device(
    embedded_tiles, hidden_sample, cotangent, lengths, gain_attn, shift_attn, w_qkv, rel_table, w_out,
    gain_mlp, shift_mlp, w_up, w_down, w_latent,
):
    size = lax.axis_size("batch")
    y, fg, lg, sums, _ = rollout(
        size, lengths, embedded_tiles.reshape(6, 2, 2, 128, 256),
        hidden_sample[0].transpose(0, 2, 1), cotangent.reshape(6, 4, 128, 256),
        w_qkv, w_out, w_up, w_down, w_latent, gain_attn, shift_attn, gain_mlp, shift_mlp,
        rel_table.transpose(0, 2, 1), jnp.asarray(picker(), BF))
    y, fg, lg, gq, go, gu, gd, g_ga, g_sa, g_gm, g_sm, g_rel, g_lat = finish(size, lengths, y, fg, lg, sums)
    return (
        y[None], fg[None], lg.transpose(0, 2, 1)[None],
        g_ga, g_sa, gq, g_rel.transpose(0, 2, 1), go, g_gm, g_sm, gu, gd, g_lat,
    )


def solution(mesh):
    data = P("section", "batch", None, None)
    return jax.shard_map(
        on_device,
        mesh=mesh,
        in_specs=(data, data, data, P("batch")) + (P(),) * 10,
        out_specs=(data, data, data) + (P(),) * 10,
        check_vma=False,
    )
```

```python
import functools

import jax
import jax.numpy as jnp
import numpy as np
from jax import lax
from jax.experimental import pallas as pl
from jax.experimental.pallas import tpu as pltpu
from jax.sharding import PartitionSpec as P

BF = jnp.bfloat16
F32 = jnp.float32
LOG2E = 1.4426950408889634
SCALE = 32**-0.5


def dot(a, b):
    return lax.dot_general(a, b, (((1,), (0,)), ((), ())), preferred_element_type=F32)


def dot_nt(a, b):
    return lax.dot_general(a, b, (((1,), (1,)), ((), ())), preferred_element_type=F32)


def dot_tn(a, b):
    return lax.dot_general(a, b, (((0,), (0,)), ((), ())), preferred_element_type=F32)


PHI = (0.7978695563668204, 0.0363928095591428, -8.82196615782389e-05, -3.6600001215273455e-05, 1.418529678284452e-06)


def gelu_pair(z):
    square = z * z
    poly = PHI[4]
    for c in PHI[3::-1]:
        poly = poly * square + c
    phi = 0.5 + 0.5 * jnp.tanh(z * poly)
    density = jnp.exp2(square * (-0.5 * LOG2E)) * 0.3989422804014327
    return z * phi, phi + z * density


def norm(x):
    centered = x - jnp.mean(x, axis=-1, keepdims=True)
    r = lax.rsqrt(jnp.mean(centered * centered, axis=-1, keepdims=True) + 1e-5)
    return centered * r, r


def norm_back(dn, n, r):
    m1 = jnp.mean(dn, axis=-1, keepdims=True)
    m2 = jnp.mean(dn * n, axis=-1, keepdims=True)
    return r * (dn - m1 - n * m2)


def low_lanes(rows):
    return lax.broadcasted_iota(jnp.int32, (rows, 128), 1) < 64


def head_rows(t):
    lane = lax.broadcasted_iota(jnp.int32, (1, 128), 1)
    return jnp.concatenate([t * jnp.where(lane // 32 == h, 1.0, 0.0).astype(BF) for h in range(4)], axis=0)


def own_rows(both):
    lo = low_lanes(64)
    return jnp.concatenate(
        [jnp.where(lo, both[128 * h:128 * h + 64], both[128 * h + 64:128 * h + 128]) for h in range(4)], axis=1)


def own_heads(rows):
    lane = lax.broadcasted_iota(jnp.int32, (128, 128), 1)
    return jnp.where(lane < 64, jnp.where(lane < 32, rows[0:128], rows[128:256]), jnp.where(lane < 96, rows[256:384], rows[384:512]))


def stacked(p):
    return jnp.concatenate([p[:, 128 * h:128 * h + 128] for h in range(4)], axis=0)


def by_window(p):
    lane = lax.broadcasted_iota(jnp.int32, (1, 512), 1)
    lo = jnp.where(lane % 128 < 64, 1.0, 0.0).astype(BF)
    hi = jnp.where(lane % 128 < 64, 0.0, 1.0).astype(BF)
    return jnp.concatenate([p * lo, p * hi], axis=0)


def f_parts(x, wq, wo, wu, wd, gn, bias, act, rst, done):
    s = {}

    def start():
        xv = x()
        n1, r1 = norm(xv)
        s['r1'] = r1
        act[0] = n1.astype(BF)
        normed = (n1 * gn[0:1] + gn[1:2]).astype(BF)
        act[1] = normed
        qkv = dot(normed, wq[...]).astype(BF)
        s['q'], s['k'], s['v'] = qkv[:, 0:256], qkv[:, 256:512], qkv[:, 512:768]
        act[3] = s['k']
        act[4] = s['v']
        s['qt'] = s['q'].T
        act[2] = s['qt']
        s['vt'] = s['v'].T

    def attention(g, wp):
        def run():
            ch = slice(g * 128, (g + 1) * 128)
            tok = slice(wp * 128, (wp + 1) * 128)
            both = dot(head_rows(s['k'][tok, ch]), s['qt'][ch, tok])
            sc = own_rows(both) * (SCALE * LOG2E) + bias(g, wp)
            e = jnp.exp2(sc - jnp.max(sc, axis=0, keepdims=True))
            p = (e * (1.0 / jnp.sum(e, axis=0, keepdims=True))).astype(BF)
            act[5 + g, wp * 128:wp * 128 + 64, :] = p[:, 0:256]
            act[5 + g, wp * 128 + 64:wp * 128 + 128, :] = p[:, 256:512]
            pb = by_window(p)
            for h in range(4):
                rows = slice(g * 128 + 32 * h, g * 128 + 32 * h + 32)
                act[7, rows, tok] = dot(s['vt'][rows, tok], pb[:, 128 * h:128 * h + 128]).astype(BF)
        return run

    def middle():
        h = x() + dot_tn(act[7], wo[...])
        n2, r2 = norm(h)
        rst[...] = jnp.where(low_lanes(256), s['r1'], r2)
        act[8] = n2.astype(BF)
        second = (n2 * gn[2:3] + gn[3:4]).astype(BF)
        act[9] = second
        s['second'] = second
        s['y'] = h

    def mlp(j):
        def run():
            a, slope = gelu_pair(dot(s['second'], wu[:, j * 256:(j + 1) * 256]))
            a = a.astype(BF)
            act[10 + j] = a
            act[14 + j] = slope.astype(BF)
            s['y'] = s['y'] + dot(a, wd[j * 256:(j + 1) * 256, :])
            if j == 3:
                done(s['y'])
        return run

    return [start] + [attention(g, wp) for g in range(2) for wp in range(2)] + [middle] + [mlp(j) for j in range(4)]


def colsum(a):
    return jnp.sum(a.reshape(32, 8, 256), axis=0)


def b_parts(dout, wq, wo, wu, wd, gn, act, rst, gv, gb, gw, done):
    s = {}

    def start():
        s['dout'] = dout()
        s['db'] = s['dout'].astype(BF)
        s['dbt'] = s['db'].T
        s['st'] = act[9].T
        s['ds'] = None

    def mlp(j):
        def run():
            c = slice(j * 256, (j + 1) * 256)
            da = dot_nt(s['db'], wd[c, :])
            dpre = (da * act[14 + j].astype(F32)).astype(BF)
            ds = dot_nt(dpre, wu[:, c])
            s['ds'] = ds if s['ds'] is None else s['ds'] + ds
            gw(4 + j)[...] += dot(s['dbt'], act[10 + j])
            gw(j)[...] += dot(s['st'], dpre)
        return run

    def middle():
        ds = s['ds']
        n2 = act[8].astype(F32)
        gv[2] += colsum(ds * n2)
        gv[3] += colsum(ds)
        s['dh'] = s['dout'] + norm_back(ds * gn[2:3], n2, rst[...][:, 64:65])
        db2 = s['dh'].astype(BF)
        s['dat'] = dot_nt(wo[...], db2).astype(BF)
        s['da'] = s['dat'].T
        s['q'] = act[2].T
        gw(11)[...] += dot(act[7], db2)
        s['kt'] = act[3].T
        s['gb'] = [None, None]
        s['dq'], s['dk'], s['dv'] = {}, {}, {}

    def attention(g, wp):
        def run():
            ch = slice(g * 128, (g + 1) * 128)
            tok = slice(wp * 128, (wp + 1) * 128)
            dp = own_rows(dot(head_rows(act[4, tok, ch]), s['dat'][ch, tok]))
            p = jnp.concatenate(
                [act[5 + g, wp * 128:wp * 128 + 64, :], act[5 + g, wp * 128 + 64:wp * 128 + 128, :]], axis=1)
            pf = p.astype(F32)
            t = dp * pf
            dsc = t - pf * jnp.sum(t, axis=0, keepdims=True)
            s['gb'][g] = dsc if s['gb'][g] is None else s['gb'][g] + dsc
            sb = by_window((dsc * SCALE).astype(BF))
            s['dv'][g, wp] = own_heads(dot(stacked(by_window(p)), s['da'][tok, ch])).astype(BF)
            s['dk'][g, wp] = own_heads(dot(stacked(sb), s['q'][tok, ch])).astype(BF)
            for h in range(4):
                rows = slice(g * 128 + 32 * h, g * 128 + 32 * h + 32)
                s['dq'][g, h, wp] = dot(s['kt'][rows, tok], sb[:, 128 * h:128 * h + 128]).astype(BF)
        return run

    def finish():
        for g in range(2):
            gb[:, g * 512:(g + 1) * 512] += s['gb'][g]
        cat = jnp.concatenate
        dqt = cat([cat([s['dq'][g, h, wp] for wp in range(2)], axis=1) for g in range(2) for h in range(4)], axis=0)
        dq = dqt.T
        dk = cat([cat([s['dk'][g, wp] for g in range(2)], axis=1) for wp in range(2)], axis=0)
        dv = cat([cat([s['dv'][g, wp] for g in range(2)], axis=1) for wp in range(2)], axis=0)
        dn = dot_nt(dq, wq[:, 0:256]) + dot_nt(dk, wq[:, 256:512]) + dot_nt(dv, wq[:, 512:768])
        nt = act[1].T
        gw(8)[...] += dot(nt, dq)
        gw(9)[...] += dot(nt, dk)
        gw(10)[...] += dot(nt, dv)
        n1 = act[0].astype(F32)
        gv[0] += colsum(dn * n1)
        gv[1] += colsum(dn)
        done(s['dh'] + norm_back(dn * gn[0:1], n1, rst[...][:, 0:1]))

    return ([start] + [mlp(j) for j in range(4)] + [middle]
            + [attention(g, wp) for g in range(2) for wp in range(2)] + [finish])


MESH = pl.DeviceIdType.MESH
SECTIONS = 4


def local_copy(src, dst, sem):
    return pltpu.make_async_copy(src, dst, sem)


def to_windows(rows):
    return rows.reshape(8, 4, 8, rows.shape[-1]).transpose(1, 0, 2, 3)


def to_rows(tiles):
    return tiles.transpose(1, 0, 2, 3).reshape(256, tiles.shape[-1])


def turn(tiles):
    flat = tiles.reshape(32, 8, 256)
    return jnp.concatenate([flat[:, 4:8], flat[:, 0:4]], axis=1).reshape(4, 8, 8, 256)


def shift_out(tiles):
    turned = turn(tiles)
    nxt = jnp.concatenate([turned[1:], turned[:1]], axis=0)
    low_half = lax.broadcasted_iota(jnp.int32, (1, 1, 8, 256), 2) < 4
    return jnp.where(low_half, turned, nxt)


def shift_back(tiles):
    turned = turn(tiles)
    prev = jnp.concatenate([turned[3:], turned[:3]], axis=0)
    low_half = lax.broadcasted_iota(jnp.int32, (1, 1, 8, 256), 2) < 4
    return jnp.where(low_half, prev, turned)


def toward_shifted(buf, par, pos):
    own = buf[par, pos, :, 32:64, :].reshape(4, 4, 8, 256)
    other = buf[par, 3 - pos, :, 0:32, :].reshape(4, 4, 8, 256)
    return shift_out(jnp.concatenate([own, other], axis=1)).reshape(256, 256)


def toward_plain(buf, par, pos):
    other = buf[par, 3 - pos, :, 32:64, :].reshape(4, 4, 8, 256)
    own = buf[par, pos, :, 0:32, :].reshape(4, 4, 8, 256)
    return shift_back(jnp.concatenate([other, own], axis=1)).reshape(256, 256)


F_FIRST = []
F_MAIN = [((0,), 0), ((1,), 1), ((2,), 2), ((3,), 3), ((4,), 4), ((5,), 5), ((6,), 6), ((7, 8), 7), ((9,), 8)]
F_LAST = [((), 9)]
B_FIRST = []
B_MLP = []
B_MAIN = [((0,), 0), ((1,), 1), ((2,), 2), ((3,), 3), ((4,), 4), ((5,), 5), ((6,), 6), ((7,), 7), ((8, 9), 8), ((10,), 9)]
B_LAST = [((), 10)]


def ordered(plan, p0, p1, p2):
    for mine, both in plan:
        p1[both]()
        p2[both]()
        for i in mine:
            p0[i]()


def ring(n, fn, start=0):
    def body(k, c):
        fn(k)
        return c
    lax.fori_loop(start, n, body, 0)


def fill_bias(rel, pick, line, bt):
    lo = low_lanes(8)
    key = lax.broadcasted_iota(jnp.int32, (64, 128), 0)
    lane = lax.broadcasted_iota(jnp.int32, (64, 128), 1)
    apart_rows = key // 32 != (lane % 64) // 32
    apart_cols = jnp.logical_and((key % 8) // 4 != (lane % 8) // 4, lane >= 64)
    for blk in range(2):
        raw = dot(rel[blk], pick[...]) * LOG2E
        for n in range(32):
            tile = raw[:, 128 * n:128 * n + 128]
            other = pltpu.roll(tile, 64, 1)
            line[16 * n:16 * n + 8, :] = jnp.where(lo, tile, other)
            line[16 * n + 8:16 * n + 16, :] = jnp.where(lo, other, tile)
        for h in range(8):
            cols = slice(128 * h, 128 * h + 128)
            plain = line[pl.ds(h, 64, stride=8), :]
            if blk == 0:
                bt[0, :, cols] = plain
            else:
                cut = plain - 100.0 * LOG2E
                bt[1, :, cols] = plain
                bt[2, :, cols] = jnp.where(apart_cols, cut, plain)
                bt[3, :, cols] = jnp.where(apart_rows, cut, plain)
                bt[4, :, cols] = jnp.where(jnp.logical_or(apart_rows, apart_cols), cut, plain)


def table_grad(gb, pick, line):
    for h in range(8):
        a = gb[:, 128 * h:128 * h + 128]
        line[pl.ds(h, 64, stride=8), :] = a + pltpu.roll(a, 64, 1)
    lo = low_lanes(8)
    row = jnp.concatenate(
        [jnp.where(lo, line[16 * n:16 * n + 8, :], line[16 * n + 8:16 * n + 16, :]) for n in range(32)], axis=1)
    high = row.astype(BF)
    rest = (row - high.astype(F32)).astype(BF)
    return dot_nt(high, pick[...]) + dot_nt(rest, pick[...])


def sizes(batch):
    unit = 16 * SECTIONS * (batch // 2)
    ra = -(-3072 // (2 * unit)) * 2 * unit
    rb = -(-(3072 + 64) // (2 * unit)) * 2 * unit
    units = rb // 2 // unit
    c = units * 3 // 7
    return ra, rb, (ra // 2, (units - c) * unit, c * unit)


class Reduction:
    def __init__(self, base, half, g1, g2, square, core, partner, grads, gathered, bufs, sems):
        self.square = square
        self.n1, self.me1, self.dev1 = g1
        self.n2, self.me2, self.dev2 = g2
        self.p1 = half // self.n1
        self.p2 = self.p1 // self.n2
        self.mine = base + core * half
        self.theirs = base + (1 - core) * half
        self.partner, self.grads, self.gathered = partner, grads, gathered
        self.o1, self.i1, self.o2, self.i2, self.o3, self.i3, self.t = bufs
        (self.s1, self.r1, self.s2, self.r2, self.s3, self.r3, self.sg2, self.rg2, self.sg1, self.rg1, self.sc, self.rc) = sems

    def rows1(self, start, i1):
        return pl.ds(pl.multiple_of(start + i1 * self.p1, 16), self.p1)

    def piece(self, start, i1, i2):
        return self.gathered.at[pl.ds(pl.multiple_of(start + i1 * self.p1 + i2 * self.p2, 16), self.p2)]

    def send(self, src, dst, ssem, rsem, device):
        return pltpu.make_async_remote_copy(
            src_ref=src, dst_ref=dst, send_sem=ssem, recv_sem=rsem, device_id=device, device_id_type=MESH)

    def landed(self, ref, sem):
        pltpu.make_async_copy(ref, ref, sem).wait()

    def others1(self, fn):
        ring(self.n1, lambda k: fn(lax.rem(self.me1 + k, self.n1)), 1)

    def others2(self, fn):
        ring(self.n2, lambda k: fn(lax.rem(self.me2 + k, self.n2)), 1)

    def to_partner(self, i):
        return self.send(self.o1.at[i], self.i1.at[i], self.s1.at[i], self.r1.at[i], self.partner)

    def scatter1(self, i):
        return self.send(self.o2.at[i], self.i2.at[self.me1], self.s2.at[i], self.r2.at[self.me1], self.dev1(i))

    def scatter2(self, i):
        return self.send(self.o3.at[i], self.i3.at[self.me2], self.s3.at[i], self.r3.at[self.me2], self.dev2(i))

    def gather2(self, i):
        here = self.piece(self.mine, self.me1, self.me2)
        return self.send(here, here, self.sg2.at[i], self.rg2.at[self.me2], self.dev2(i))

    def gather1(self, i, j2):
        here = self.piece(self.mine, self.me1, j2)
        return self.send(here, here, self.sg1.at[i, j2], self.rg1.at[self.me1, j2], self.dev1(i))

    def share(self, i1, i2):
        here = self.piece(self.mine, i1, i2)
        return self.send(here, here, self.sc.at[i1, i2], self.rc.at[i1, i2], self.partner)

    def swap(self):
        def one(k):
            i = lax.rem(self.me1 + k, self.n1)
            self.o1[i] = self.grads[self.rows1(self.theirs, i), :].astype(BF)
            self.to_partner(i).start()
        ring(self.n1 + 1, one, 1)

    def summed(self, i):
        self.landed(self.i1.at[i], self.r1.at[i])
        return self.grads[self.rows1(self.mine, i), :] + self.i1[i].astype(F32)

    def stage1(self):
        def one(i):
            self.o2[i] = self.summed(i).astype(BF)
            self.scatter1(i).start()
        self.others1(one)
        self.t[...] = self.summed(self.me1)

    def stage2(self):
        def add(j):
            self.landed(self.i2.at[j], self.r2.at[j])
            self.t[...] += self.i2[j].astype(F32)
        self.others1(add)

        def one(i):
            self.o3[i] = self.t[self.slice2(i), :].astype(BF)
            self.scatter2(i).start()
        self.others2(one)

    def slice2(self, i):
        return pl.ds(pl.multiple_of(i * self.p2, 16), self.p2)

    def beside(self):
        x, y = lax.rem(self.me1, 2), self.me1 // 2
        return self.me1 + 1 - 2 * x, self.me1 + 2 - 4 * y

    def forward(self, j2):
        nx, ny = self.beside()
        odd = lax.rem(j2, 2)
        origin, target = jnp.where(odd == 1, ny, nx), jnp.where(odd == 1, nx, ny)
        here = self.piece(self.mine, origin, j2)
        return self.send(here, here, self.sg1.at[3 - self.me1, j2], self.rg1.at[origin, j2], self.dev1(target))

    def pass_on(self, j2):
        if self.square:
            for i in self.beside():
                self.gather1(i, j2).start()
        else:
            self.others1(lambda i: self.gather1(i, j2).start())
        self.share(self.me1, j2).start()

    def stage3(self):
        here = self.slice2(self.me2)

        def add(j):
            self.landed(self.i3.at[j], self.r3.at[j])
            self.t[here, :] += self.i3[j].astype(F32)
        self.others2(add)
        self.piece(self.mine, self.me1, self.me2)[...] = self.t[here, :].astype(BF)
        self.others2(lambda i: self.gather2(i).start())
        self.pass_on(self.me2)

    def stage4(self):
        def one(j):
            self.landed(self.piece(self.mine, self.me1, j), self.rg2.at[j])
            self.pass_on(j)
        self.others2(one)

    def stage5(self):
        def arrive(j1, j2):
            self.landed(self.piece(self.mine, j1, j2), self.rg1.at[j1, j2])
            self.share(j1, j2).start()

        if not self.square:
            self.others1(lambda j1: ring(self.n2, lambda j2: arrive(j1, j2)))
            return
        nx, ny = self.beside()

        def sides(j2):
            arrive(nx, j2)
            arrive(ny, j2)
            self.forward(j2).start()

        ring(self.n2, sides)
        ring(self.n2, lambda j2: arrive(3 - self.me1, j2))

    def stage6(self):
        ring(self.n1, lambda i: ring(self.n2, lambda j: self.landed(self.piece(self.theirs, i, j), self.rc.at[i, j])))

    def drain(self):
        ring(self.n1, lambda i: self.to_partner(i).wait_send())
        self.others1(lambda i: self.scatter1(i).wait_send())
        self.others2(lambda i: self.scatter2(i).wait_send())
        self.others2(lambda i: self.gather2(i).wait_send())
        if self.square:
            for i in self.beside():
                ring(self.n2, lambda j: self.gather1(i, j).wait_send())
            ring(self.n2, lambda j: self.forward(j).wait_send())
        else:
            self.others1(lambda i: ring(self.n2, lambda j: self.gather1(i, j).wait_send()))
        ring(self.n1, lambda i: ring(self.n2, lambda j: self.share(i, j).wait_send()))


LATE = (
    "C0", "B0", "A2", "C1", "B1", "A3", "C2", "B2", "A4", "C3",
    "B3", "A5", "C4", "B4", "A6", "C5", "B5", "C6", "B6",
)


def rollout_kernel(
    size, lengths, emb, hid, cot, wq_far, wo_far, wu_far, wd_far, wl, ga, sa, gm, sm, rel, pick_far,
    y_home, fg_home, lg_home, sums, act_far,
    emb_in, cot_in, hid_in, lg_st, cot_mk, xs, dxs, xin, act, rst, gb, gv, gl, gn, bt, line,
    grads, gathered, wq, wo, wu, wd, pick,
    emb_ss, emb_rs, hid_ss, hid_rs, cot_ss, cot_rs,
    y_ss, y_rs, fg_ss, fg_rs, lg_ss, lg_rs, xf_ss, xf_rs, xb_ss, xb_rs, act_os, act_is, cot_ls, out_ss, w_ls, *reduction,
):
    sec = lax.axis_index("section")
    bat = lax.axis_index("batch")
    core = lax.rem(bat, 2)
    first = bat - core
    partner = first + 1 - core
    rows_a, rows_b, halves = sizes(size)

    barrier = pltpu.get_barrier_semaphore()
    for ds in range(SECTIONS):
        for dc in range(2):
            if ds == 0 and dc == 0:
                continue
            pl.semaphore_signal(
                barrier, inc=1,
                device_id={"section": lax.rem(sec + ds, SECTIONS), "batch": first + lax.rem(core + dc, 2)},
                device_id_type=MESH)

    def greet(k):
        pl.semaphore_signal(
            barrier, inc=1, device_id={"section": sec, "batch": lax.rem(bat + 2 * k, size)}, device_id_type=MESH)

    ring(size // 2, greet, 1)
    pl.semaphore_wait(barrier, 2 * SECTIONS - 1 + size // 2 - 1)

    def route(pos, t):
        if pos == 0:
            to_sec, to_bat = 2 * core + t // 2, first + t % 2
            return to_sec, to_bat, 4 + t // 2, t % 2, jnp.logical_and(to_sec == sec, core == t % 2)
        return jnp.int32(t), bat, t, pos - 1, sec == t

    def deliver(src, dst, ssem, rsem, to_sec, to_bat, mine, begin):
        @pl.when(mine)
        def _():
            if begin:
                local_copy(src, dst, rsem).start()

        @pl.when(jnp.logical_not(mine))
        def _():
            rc = pltpu.make_async_remote_copy(
                src_ref=src, dst_ref=dst, send_sem=ssem, recv_sem=rsem,
                device_id={"section": to_sec, "batch": to_bat}, device_id_type=MESH)
            if begin:
                rc.start()
            else:
                rc.wait_send()

    def spread_tiles(begin):
        for pos in (1, 2, 0):
            for t in range(4):
                to_sec, to_bat, item, part, mine = route(pos, t)
                deliver(emb.at[item, part], emb_in.at[sec, pos], emb_ss.at[pos, t], emb_rs.at[sec, pos],
                        to_sec, to_bat, mine, begin)
                deliver(hid.at[item, :, pl.ds(256 * part, 256)], hid_in.at[sec, pos], hid_ss.at[pos, t],
                        hid_rs.at[sec, pos], to_sec, to_bat, mine, begin)

    def spread_cotangents(begin):
        for pos in (1, 2, 0):
            for t in range(4):
                to_sec, to_bat, item, part, mine = route(pos, t)
                for u in range(2):
                    deliver(cot_mk.at[item, (2 * part + 1 + u) % 4], cot_in.at[sec, pos, u], cot_ss.at[pos, t, u],
                            cot_rs.at[sec, pos, u], to_sec, to_bat, mine, begin)

    def home(step, pos):
        half = pos == 0
        item = jnp.where(half, 4 + lax.rem(sec, 2), sec)
        part = jnp.where(half, core, pos - 1)
        to_bat = jnp.where(half, first + sec // 2, bat)
        slot = jnp.where(half, lax.rem(sec, 2) * 2 + core, sec)
        return item, part, to_bat, slot, jnp.logical_and(step == sec, to_bat == bat)

    def return_y(step, pos, begin):
        item, part, to_bat, slot, mine = home(step, pos)
        for u in range(2):
            deliver(emb_in.at[step, pos, u], y_home.at[item, lax.rem(2 * part + 1 + u, 4)], y_ss.at[step, pos, u],
                    y_rs.at[pos, slot, u], step, to_bat, mine, begin)

    def return_grads(step, pos, begin):
        item, part, to_bat, slot, mine = home(step, pos)
        deliver(cot_in.at[step, pos], fg_home.at[item, part], fg_ss.at[step, pos], fg_rs.at[pos, slot],
                step, to_bat, mine, begin)
        deliver(lg_st.at[step, pos], lg_home.at[item, :, pl.ds(pl.multiple_of(256 * part, 256), 256)],
                lg_ss.at[step, pos], lg_rs.at[pos, slot], step, to_bat, mine, begin)

    def exchange(buf, par, off, ssem, rsem, n):
        return pltpu.make_async_remote_copy(
            src_ref=buf.at[par, 0, :, pl.ds(off, 32), :],
            dst_ref=buf.at[par, 3, :, pl.ds(off, 32), :],
            send_sem=ssem.at[n], recv_sem=rsem.at[n],
            device_id={"section": sec, "batch": partner}, device_id_type=MESH)

    xy = (SECTIONS, sec, lambda i: {"section": i, "batch": bat})
    zs = (size // 2, bat // 2, lambda i: {"section": sec, "batch": 2 * i + core})
    bases = (0, rows_a, rows_a + 2 * halves[1])
    jobs = []
    for k, half in enumerate(halves):
        if half:
            g1, g2 = (zs, xy) if k == 2 else (xy, zs)
            jobs.append(Reduction(bases[k], half, g1, g2, k < 2, core, {"section": sec, "batch": partner}, grads, gathered,
                                  reduction[19 * k:19 * k + 7], reduction[19 * k + 7:19 * k + 19]))
    early = jobs[0]

    spread_tiles(True)
    loads = [local_copy(far, near, w_ls.at[i]) for i, (far, near) in enumerate(
        ((pick_far, pick), (wq_far, wq), (wo_far, wo), (wu_far, wu), (wd_far, wd)))]
    for load in loads:
        load.start()
    local_copy(cot, cot_mk, cot_ls).start()
    xs[1] = jnp.zeros((4, 4, 64, 256), F32)
    dxs[1] = jnp.zeros((4, 4, 64, 256), F32)
    loads[0].wait()
    for i, ref in enumerate((ga, sa, gm, sm)):
        for blk in range(2):
            gn[blk, i:i + 1, :] = ref[blk:blk + 1, :].astype(F32)
    fill_bias(rel, pick, line, bt)
    for ref in (gb, gv, gl):
        ref[...] = jnp.zeros(ref.shape, F32)

    def clear(t):
        grads[pl.ds(pl.multiple_of(64 * t, 64), 64), :] = jnp.zeros((64, 256), F32)

    ring((rows_a + rows_b) // 64, clear)
    for load in loads[1:]:
        load.wait()

    def act_out(ph, pos):
        return local_copy(act.at[lax.rem(ph, 2), pos], act_far.at[ph, pos], act_os.at[ph, pos])

    def act_in(ph, pos):
        return local_copy(act_far.at[ph, pos], act.at[lax.rem(ph, 2), pos], act_is.at[ph, pos])

    def forward_phase(ph):
        step = ph // 2
        blk = lax.rem(ph, 2)
        par = lax.rem(ph, 2)
        old = 1 - par

        def build(pos):
            @pl.when(blk == 0)
            def _():
                local_copy(emb.at[0, 0], emb_in.at[step, pos], emb_rs.at[step, pos]).wait()
                local_copy(hid.at[0, :, pl.ds(0, 256)], hid_in.at[step, pos], hid_rs.at[step, pos]).wait()
                lifted = emb_in[step, pos].reshape(256, 256).astype(F32) + dot_tn(hid_in[step, pos], wl[...])
                carried = toward_plain(xs, old, pos).astype(BF).astype(F32)
                xin[pos] = to_windows(lifted).reshape(256, 256) + carried

            @pl.when(blk == 1)
            def _():
                xin[pos] = toward_shifted(xs, old, pos)

        def parts(pos):
            bottom = core if pos == 0 else pos - 1

            def done(value):
                xs[par, pos] = value.reshape(4, 64, 256)

            def bias(g, wp):
                return bt[jnp.where(blk == 0, 0, 1 + 2 * bottom + wp), :, g * 512:(g + 1) * 512]

            return f_parts(lambda: xin[pos], wq.at[blk], wo.at[blk], wu.at[blk], wd.at[blk], gn.at[blk], bias,
                           act.at[lax.rem(ph, 2), pos], rst.at[ph, pos], done)

        def finish(pos):
            @pl.when(blk == 1)
            def _():
                rows = to_rows(shift_back(xs[par, pos].reshape(4, 8, 8, 256))).astype(BF)
                emb_in[step, pos] = rows.reshape(2, 128, 256)
                return_y(step, pos, True)

            @pl.when(ph < 6)
            def _():
                act_out(ph, pos).start()

        p0, p1, p2 = parts(0), parts(1), parts(2)

        @pl.when(ph >= 2)
        def _():
            for pos in range(3):
                act_out(ph - 2, pos).wait()

        build(1)
        build(2)
        @pl.when(ph >= 2)
        def _():
            exchange(xs, par, pl.multiple_of(32 * par, 32), xf_ss, xf_rs, ph - 2).wait_send()

        ordered(F_FIRST, p0, p1, p2)

        @pl.when(ph >= 1)
        def _():
            exchange(xs, old, pl.multiple_of(32 * old, 32), xf_ss, xf_rs, ph - 1).wait_recv()

        build(0)
        ordered(F_MAIN, p0, p1, p2)

        finish(0)

        @pl.when(ph < 7)
        def _():
            exchange(xs, par, pl.multiple_of(32 * par, 32), xf_ss, xf_rs, ph).start()

        @pl.when(ph == 4 - sec)
        def _():
            local_copy(cot, cot_mk, cot_ls).wait()
            for i in range(6):
                on = jnp.where(sec < lengths[i], 1.0, 0.0)
                for u in range(4):
                    cot_mk[i, u] = (cot_mk[i, u].astype(F32) * on).astype(BF)
            spread_cotangents(True)

        ordered(F_LAST, p0, p1, p2)
        finish(1)
        finish(2)

    ring(8, forward_phase)
    exchange(xs, 0, 0, xf_ss, xf_rs, 6).wait_send()

    def backward_phase(bph):
        ph = 7 - bph
        step = ph // 2
        blk = lax.rem(ph, 2)
        par = lax.rem(bph, 2)
        old = 1 - par

        def build(pos):
            @pl.when(blk == 1)
            def _():
                for u in range(2):
                    local_copy(cot_mk.at[0, 0], cot_in.at[step, pos, u], cot_rs.at[step, pos, u]).wait()
                rows = cot_in[step, pos].reshape(256, 256).astype(F32)
                xin[pos] = shift_out(to_windows(rows)).reshape(256, 256) + toward_shifted(dxs, old, pos)

            @pl.when(blk == 0)
            def _():
                xin[pos] = toward_plain(dxs, old, pos)

            @pl.when(ph < 6)
            def _():
                act_in(ph, pos).wait()

        def gw(t):
            return grads.at[pl.ds(pl.multiple_of(rows_a * (1 - blk) + 256 * t, 256), 256)]

        def parts(pos):
            def done(value):
                dxs[par, pos] = jnp.where(blk == 0, value.astype(BF).astype(F32), value).reshape(4, 64, 256)

            return b_parts(lambda: xin[pos], wq.at[blk], wo.at[blk], wu.at[blk], wd.at[blk], gn.at[blk],
                           act.at[lax.rem(ph, 2), pos], rst.at[ph, pos], gv.at[blk], gb.at[blk], gw, done)

        def finish(pos):
            @pl.when(ph >= 2)
            def _():
                act_in(ph - 2, pos).start()

            @pl.when(blk == 0)
            def _():
                rows = to_rows(dxs[par, pos].reshape(4, 8, 8, 256)).astype(BF)
                cot_in[step, pos] = rows.reshape(2, 128, 256)
                lg_st[step, pos] = dot_nt(wl[...], rows).astype(BF)
                gl[...] += dot(hid_in[step, pos], rows)
                return_grads(step, pos, True)

        p0, p1, p2 = parts(0), parts(1), parts(2)

        @pl.when(bph == 7)
        def _():
            early.swap()

        build(1)
        build(2)
        @pl.when(bph >= 2)
        def _():
            exchange(dxs, par, pl.multiple_of(32 * old, 32), xb_ss, xb_rs, bph - 2).wait_send()

        ordered(B_FIRST, p0, p1, p2)

        @pl.when(bph >= 1)
        def _():
            exchange(dxs, old, pl.multiple_of(32 * par, 32), xb_ss, xb_rs, bph - 1).wait_recv()

        build(0)

        @pl.when(bph == 7)
        def _():
            early.stage1()

        ordered(B_MLP + B_MAIN, p0, p1, p2)

        finish(0)

        @pl.when(bph < 7)
        def _():
            exchange(dxs, par, pl.multiple_of(32 * old, 32), xb_ss, xb_rs, bph).start()

        ordered(B_LAST, p0, p1, p2)
        finish(1)
        finish(2)

    ring(8, backward_phase)
    exchange(dxs, 0, 32, xb_ss, xb_rs, 6).wait_send()

    small = rows_a + 3072
    grads[small:small + 8, :] = jnp.concatenate(
        [jnp.sum(gv[blk, i], axis=0, keepdims=True) for blk in range(2) for i in range(4)], axis=0)
    grads[small + 8:small + 40, :] = gl[...]
    for blk in range(2):
        grads[small + 40 + 8 * blk:small + 48 + 8 * blk, 0:225] = table_grad(gb.at[blk], pick, line)


    def publish(lo, hi):
        copy = local_copy(gathered.at[pl.ds(lo, hi - lo)], sums.at[pl.ds(lo, hi - lo)], out_ss.at[len(copies)])
        copy.start()
        copies.append(copy)

    copies = []
    by_name = dict(zip("ABC", jobs))
    for entry in LATE:
        if entry[0] not in by_name:
            continue
        job = by_name[entry[0]]
        (job.swap, job.stage1, job.stage2, job.stage3, job.stage4, job.stage5, job.stage6)[int(entry[1])]()
        if entry == "A6":
            publish(0, rows_a)
    publish(rows_a, rows_a + rows_b)

    spread_tiles(False)
    spread_cotangents(False)

    def leave(i):
        return_y(i // 3, lax.rem(i, 3), False)
        return_grads(i // 3, lax.rem(i, 3), False)

    ring(3 * SECTIONS, leave)
    for pos in range(3):
        for t in range(4):
            item, part = (4 + t // 2, t % 2) if pos == 0 else (t, pos - 1)
            for u in range(2):
                local_copy(emb_in.at[0, 0, 0], y_home.at[item, (2 * part + 1 + u) % 4], y_rs.at[pos, t, u]).wait()
            local_copy(cot_in.at[0, 0], fg_home.at[item, part], fg_rs.at[pos, t]).wait()
            local_copy(lg_st.at[0, 0], lg_home.at[item, :, pl.ds(256 * part, 256)], lg_rs.at[pos, t]).wait()
    for job in jobs:
        job.drain()
    for copy in copies:
        copy.wait()


def rollout(size, *operands):
    vm = pl.BlockSpec(memory_space=pltpu.VMEM)
    far = pl.BlockSpec(memory_space=pl.ANY)
    S = jax.ShapeDtypeStruct
    dma = pltpu.SemaphoreType.DMA
    rows_a, rows_b, halves = sizes(size)
    reduction = []
    for k, half in enumerate(halves):
        n1, n2 = (size // 2, SECTIONS) if k == 2 else (SECTIONS, size // 2)
        p1 = max(half // n1, 16)
        p2 = max(p1 // n2, 16)
        reduction += [pltpu.VMEM((n1, p1, 256), BF)] * 4 + [pltpu.VMEM((n2, p2, 256), BF)] * 2
        reduction += [pltpu.VMEM((p1, 256), F32)]
        reduction += [dma((n1,))] * 4 + [dma((n2,))] * 4 + [dma((n1, n2))] * 4
    return pl.pallas_call(
        functools.partial(rollout_kernel, size),
        name="rollout",
        in_specs=[pl.BlockSpec(memory_space=pltpu.SMEM)] + [far] * 7 + [vm] * 6 + [far],
        out_specs=(far,) * 5,
        out_shape=(
            S((6, 4, 128, 256), BF), S((6, 2, 2, 128, 256), BF), S((6, 32, 512), BF),
            S((rows_a + rows_b, 256), BF),
            S((6, 3, 18, 256, 256), BF),
        ),
        scratch_shapes=[
            pltpu.VMEM((4, 3, 2, 128, 256), BF), pltpu.VMEM((4, 3, 2, 128, 256), BF), pltpu.VMEM((4, 3, 32, 256), BF),
            pltpu.VMEM((4, 3, 32, 256), BF),
            pltpu.VMEM((6, 4, 128, 256), BF),
            pltpu.VMEM((2, 4, 4, 64, 256), F32), pltpu.VMEM((2, 4, 4, 64, 256), F32),
            pltpu.VMEM((3, 256, 256), F32),
            pltpu.VMEM((2, 3, 18, 256, 256), BF), pltpu.VMEM((8, 3, 256, 128), F32),
            pltpu.VMEM((2, 64, 1024), F32), pltpu.VMEM((2, 4, 8, 256), F32), pltpu.VMEM((32, 256), F32),
            pltpu.VMEM((2, 4, 256), F32), pltpu.VMEM((5, 64, 1024), F32), pltpu.VMEM((512, 128), F32),
            pltpu.VMEM((rows_a + rows_b, 256), F32), pltpu.VMEM((rows_a + rows_b, 256), BF),
            pltpu.VMEM((2, 256, 768), BF), pltpu.VMEM((2, 256, 256), BF), pltpu.VMEM((2, 256, 1024), BF),
            pltpu.VMEM((2, 1024, 256), BF), pltpu.VMEM((225, 4096), BF),
            dma((3, 4)), dma((4, 3)), dma((3, 4)), dma((4, 3)), dma((3, 4, 2)), dma((4, 3, 2)),
            dma((4, 3, 2)), dma((3, 4, 2)), dma((4, 3)), dma((3, 4)), dma((4, 3)), dma((3, 4)),
            dma((7,)), dma((7,)), dma((7,)), dma((7,)), dma((6, 3)), dma((6, 3)), dma, dma((2,)), dma((5,)),
        ] + reduction,
        compiler_params=pltpu.CompilerParams(collective_id=0, has_side_effects=True, vmem_limit_bytes=61 * 2**20),
        cost_estimate=pl.CostEstimate(flops=60 * 10**9, bytes_accessed=100 * 10**6, transcendentals=0),
    )(*operands)


def finish_kernel(rows_a, lengths, y, fg, lg, sums, y_out, fg_out, lg_out, gq, go, gu, gd, g_ga, g_sa, g_gm, g_sm, g_rel, g_lat,
                  y_in, fg_in, lg_in, near, wide, y_is, y_os, n_is, w_os, f_is, f_os):
    sec = lax.axis_index("section")
    small = rows_a + 3072
    groups = [(0, 1024), (1024, 2048), (2048, 3072), (rows_a, rows_a + 1024), (rows_a + 1024, rows_a + 2048), (rows_a + 2048, rows_a + 3072),
              (small, small + 64)]
    reads = [local_copy(sums.at[pl.ds(lo, hi - lo)], near.at[pl.ds(lo, hi - lo)], n_is.at[i]) for i, (lo, hi) in enumerate(groups)]
    items = [local_copy(y.at[i], y_in.at[i], y_is.at[i]) for i in range(6)]
    passed = [local_copy(fg.at[i], fg_in.at[i], f_is.at[i]) for i in range(6)] + [local_copy(lg, lg_in, f_is.at[6])]
    for i in range(6):
        for copy in (reads[i], passed[i], items[i]):
            copy.start()
    reads[6].start()
    passed[6].start()
    writes = []

    def write(src, dst, sem):
        copy = local_copy(src, dst, sem)
        copy.start()
        writes.append(copy)

    for i, read in enumerate(reads[:6]):
        read.wait()
        blk, kind = 1 - i // 3, i % 3
        for j in range(4):
            t = 4 * i + j
            lo = groups[i][0] + 256 * j
            value = near[lo:lo + 256, :].astype(F32)
            wide[t] = value.T if kind == 1 else value
            cols = pl.ds(256 * j, 256)
            dst = (gu.at[blk, :, cols], gd.at[blk, cols, :], gq.at[blk, :, cols] if j < 3 else go.at[blk])[kind]
            write(wide.at[t], dst, w_os.at[t])
        passed[i].wait()
        write(fg_in.at[i], fg_out.at[i], f_os.at[i])
        items[i].wait()
        on = jnp.where(sec < lengths[i], 1.0, 0.0)
        y_in[i] = (y_in[i].astype(F32) * on).astype(BF)
        write(y_in.at[i], y_out.at[i], y_os.at[i])
    passed[6].wait()
    write(lg_in, lg_out, f_os.at[6])
    reads[6].wait()
    tail = near[small:small + 64, :].astype(F32)
    for i, ref in enumerate((g_ga, g_sa, g_gm, g_sm)):
        for blk in range(2):
            ref[blk:blk + 1, :] = tail[4 * blk + i:4 * blk + i + 1]
    g_lat[...] = tail[8:40]
    for blk in range(2):
        g_rel[blk] = tail[40 + 8 * blk:48 + 8 * blk, 0:225]
    for copy in writes:
        copy.wait()


def finish(size, lengths, y, fg, lg, sums):
    vm = pl.BlockSpec(memory_space=pltpu.VMEM)
    far = pl.BlockSpec(memory_space=pl.ANY)
    S = jax.ShapeDtypeStruct
    dma = pltpu.SemaphoreType.DMA
    rows_a, rows_b, _ = sizes(size)
    return pl.pallas_call(
        functools.partial(finish_kernel, rows_a),
        name="finish",
        in_specs=[pl.BlockSpec(memory_space=pltpu.SMEM)] + [far] * 4,
        out_specs=(far,) * 7 + (vm,) * 6,
        out_shape=(
            S((6, 512, 256), BF), S((6, 512, 256), BF), S((6, 32, 512), BF),
            S((2, 256, 768), F32), S((2, 256, 256), F32), S((2, 256, 1024), F32), S((2, 1024, 256), F32),
            S((2, 256), F32), S((2, 256), F32), S((2, 256), F32), S((2, 256), F32),
            S((2, 8, 225), F32), S((32, 256), F32),
        ),
        scratch_shapes=[
            pltpu.VMEM((6, 512, 256), BF), pltpu.VMEM((6, 512, 256), BF), pltpu.VMEM((6, 32, 512), BF),
            pltpu.VMEM((rows_a + rows_b, 256), BF), pltpu.VMEM((24, 256, 256), F32),
            dma((6,)), dma((6,)), dma((7,)), dma((24,)), dma((7,)), dma((7,)),
        ],
        compiler_params=pltpu.CompilerParams(vmem_limit_bytes=61 * 2**20),
        cost_estimate=pl.CostEstimate(flops=0, bytes_accessed=16 * 10**6, transcendentals=0),
    )(lengths, y.reshape(6, 512, 256), fg.reshape(6, 512, 256), lg, sums)


def picker():
    row = np.repeat(np.arange(8), 8)
    col = np.tile(np.arange(8), 8)
    index = (row[None, :] - row[:, None] + 7) * 15 + col[None, :] - col[:, None] + 7
    return (np.arange(225)[:, None] == index.reshape(1, -1)).astype(np.float32)


def on_device(
    embedded_tiles, hidden_sample, cotangent, lengths, gain_attn, shift_attn, w_qkv, rel_table, w_out,
    gain_mlp, shift_mlp, w_up, w_down, w_latent,
):
    size = lax.axis_size("batch")
    y, fg, lg, sums, _ = rollout(
        size, lengths, embedded_tiles.reshape(6, 2, 2, 128, 256),
        hidden_sample[0].transpose(0, 2, 1), cotangent.reshape(6, 4, 128, 256),
        w_qkv, w_out, w_up, w_down, w_latent, gain_attn, shift_attn, gain_mlp, shift_mlp,
        rel_table.transpose(0, 2, 1), jnp.asarray(picker(), BF))
    y, fg, lg, gq, go, gu, gd, g_ga, g_sa, g_gm, g_sm, g_rel, g_lat = finish(size, lengths, y, fg, lg, sums)
    return (
        y[None], fg[None], lg.transpose(0, 2, 1)[None],
        g_ga, g_sa, gq, g_rel.transpose(0, 2, 1), go, g_gm, g_sm, gu, gd, g_lat,
    )


def solution(mesh):
    data = P("section", "batch", None, None)
    return jax.shard_map(
        on_device,
        mesh=mesh,
        in_specs=(data, data, data, P("batch")) + (P(),) * 10,
        out_specs=(data, data, data) + (P(),) * 10,
        check_vma=False,
    )
```
